128 devices in a mesh: dp: 8 (over z_lo, x), frame: 16 (over y, z_hi, core).
Axes of the slice: x: 4, y: 4, z: 4 (z_hi: 2, z_lo: 2; z = z_hi * 2 + z_lo), core: 2. Of those that a mesh axis runs over, the one named last changes fastest.
Arguments:
- frames_in: bfloat16 [8, 16, 128, 1024], P('dp', 'frame'), may hold values from -6 to 6
- bottleneck: bfloat16 [8, 4, 1024], P('dp'), may hold values from -6 to 6
- spatial_entry: bfloat16 [1024, 1536], replicated, may hold values from -2 to 2
- spatial_exit: bfloat16 [1024, 512], replicated, may hold values from -0.25 to 0.25
- temporal_entry: bfloat16 [1024, 1536], replicated, may hold values from -2 to 2
- temporal_exit: bfloat16 [1024, 512], replicated, may hold values from -0.25 to 0.25
- output_grad: bfloat16 [8, 16, 128, 1024], P('dp', 'frame'), may hold values from -6 to 6
- joined_grad: bfloat16 [8, 4, 1024], P('dp'), may hold values from -6 to 6
Outputs:
- frames_delta: bfloat16 [8, 16, 128, 1024], P('dp', 'frame')
- bottleneck_delta: bfloat16 [8, 4, 1024], P('dp')
- spatialin_grad: bfloat16 [1024, 1536], P(('dp', 'frame'))
- spatialout_grad: bfloat16 [1024, 512], P(('dp', 'frame'))
- temporalin_grad: bfloat16 [1024, 1536], P(('dp', 'frame'))
- temporalout_grad: bfloat16 [1024, 512], P(('dp', 'frame'))
The draws below stay inside these ranges and needn't reach their ends.
All inputs are finite; a program needn't handle non-finite values.
Results may differ from the reference program's by a relative error of at most 0.024.
Values may be sent and summed in bfloat16 or wider, within the bound.
No kernel may reach another device: no remote copies, remote signals or barrier semaphores. Data moves between devices by JAX's collectives and lax.ppermute only.
A program may use at most 64 MiB of HBM per device.

```python
import math
import jax
import jax.numpy as jnp
from jax import lax

D = 1024
HEAD = 64
HEADS = 8
BOT = 4
CLIPS = 8
FRAMES = 16
PATCHES = 128


def entry_draw(key):
    base_key = jax.random.fold_in(key, 0)
    drawn = jax.random.normal(base_key, (D, 3 * HEADS * HEAD), jnp.float32) / math.sqrt(D)
    return jnp.clip(drawn, -2.0, 2.0)


def draw_spatial_entry(key, part):
    return entry_draw(jax.random.fold_in(key, 17)).astype(jnp.bfloat16)


def draw_temporal_entry(key, part):
    return entry_draw(jax.random.fold_in(key, 29)).astype(jnp.bfloat16)


def strengthened(values, key, source, target, blocks, factor):
    owner, partner = [(jnp.arange(values.shape[dim]) // (values.shape[dim] // blocks)).reshape([-1 if axis == dim else 1 for axis in range(values.ndim)]) for dim in (source, target)]
    chosen = jax.random.permutation(key, blocks)[partner]
    strong = (owner == chosen) | (owner == (partner + blocks // 2) % blocks)
    return jnp.where(strong, factor * values, values)


def block_levels(stream_key, extent, cuts, least, largest):
    level = 1.0
    for dim, parts in cuts:
        draws = jax.random.uniform(jax.random.fold_in(jax.random.fold_in(stream_key, 6), dim), (parts,), jnp.float32, least / len(cuts), largest / len(cuts))
        level = level * jnp.repeat(jnp.exp(draws), extent[dim] // parts).reshape((-1,) + (1,) * (len(extent) - 1 - dim))
    return level


def scatter_about(own_key, dims, spread, limit, cuts=(), dtype=jnp.bfloat16):
    loudness = block_levels(own_key, dims, cuts, -0.22, 0.18) if cuts else 1.0
    array = jax.random.normal(own_key, dims, jnp.float32) * spread * loudness
    return jnp.minimum(jnp.maximum(array, -limit), limit).astype(dtype)


def noise_with(stream_key, shape, deviation, limit, cuts, heavy, dtype=jnp.bfloat16):
    values = deviation * jax.random.normal(stream_key, shape, jnp.float32)
    if cuts:
        values = values * block_levels(stream_key, shape, cuts, -0.22, 0.18)
    return jnp.clip(strengthened(values, jax.random.fold_in(stream_key, 3), *heavy), -limit, limit).astype(dtype)


def setup_inputs(seed: int = 0) -> dict:
    arg_keys = jax.random.split(jax.random.key(seed), 9)
    return {
        "frames_in": scatter_about(arg_keys[0], (CLIPS, FRAMES, PATCHES, D), 1.0, 6.0, ((0, 8), (1, 16))),
        "bottleneck": scatter_about(arg_keys[1], (CLIPS, BOT, D), 1.0, 6.0, ((0, 8),)),
        "spatial_entry": draw_spatial_entry(jax.random.fold_in(arg_keys[8], 71), 0),
        "spatial_exit": scatter_about(arg_keys[3], (D, HEADS * HEAD), (HEADS * HEAD) ** -0.5, 0.25),
        "temporal_entry": draw_temporal_entry(jax.random.fold_in(arg_keys[8], 71), 0),
        "temporal_exit": scatter_about(arg_keys[5], (D, HEADS * HEAD), (HEADS * HEAD) ** -0.5, 0.25),
        "output_grad": noise_with(arg_keys[6], (CLIPS, FRAMES, PATCHES, D), 1.0, 6.0, ((0, 8), (1, 16)), (1, 3, 16, 2.0)),
        "joined_grad": scatter_about(arg_keys[7], (CLIPS, BOT, D), 1.0, 6.0, ((0, 8),)),
    }


EPSILON = 1e-05

def product_form(form, left, right):
    left, right = lax.optimization_barrier((left, right))
    return jnp.einsum(form, left.astype(jnp.float32), right.astype(jnp.float32), preferred_element_type=jnp.float32)

def product_general(left, right, numbers):
    left, right = lax.optimization_barrier((left, right))
    return lax.dot_general(left.astype(jnp.float32), right.astype(jnp.float32), numbers, preferred_element_type=jnp.float32)

def normalize(inputs):
    widened = lax.optimization_barrier(inputs).astype(jnp.float32)
    centred = widened - lax.optimization_barrier(jnp.mean(widened, axis=-1, keepdims=True))
    inverse = lax.rsqrt(lax.optimization_barrier(jnp.mean(centred * centred, axis=-1, keepdims=True)) + EPSILON)
    return (centred * inverse, inverse)

def attend(inputs, entry_weight, head_count):
    normed, inverse = normalize(inputs)
    normed_low = normed.astype(jnp.bfloat16)
    mixture = product_general(normed_low, entry_weight, (((3,), (0,)), ((), ()))).astype(jnp.bfloat16)
    lead_count, seq_length, side_count = (inputs.shape[0], inputs.shape[1], inputs.shape[2])
    head_width = entry_weight.shape[1] // 3
    head_size = head_width // head_count
    pieces = mixture.reshape(lead_count, seq_length, side_count, 3, head_count, head_size)
    queries = pieces[:, :, :, 0]
    key_heads = pieces[:, :, :, 1]
    values = pieces[:, :, :, 2]
    factor = 1.0 / math.sqrt(head_size)
    scores = product_form('albhe,ambhe->abhlm', queries, key_heads) * factor
    scores = scores - lax.optimization_barrier(jnp.max(scores, axis=-1, keepdims=True))
    expon = jnp.exp(scores)
    softmax_weights = expon / lax.optimization_barrier(jnp.sum(expon, axis=-1, keepdims=True))
    softmax_low = softmax_weights.astype(jnp.bfloat16)
    attended = product_form('abhlm,ambhe->albhe', softmax_low, values).astype(jnp.bfloat16)
    attended = attended.reshape(lead_count, seq_length, side_count, head_width)
    return (normed, inverse, normed_low, queries, key_heads, values, softmax_weights, softmax_low, attended)

def project_out(inputs, attended, exit_weight):
    return lax.optimization_barrier(inputs).astype(jnp.float32) + product_general(attended, exit_weight, (((3,), (1,)), ((), ())))

def backward(cotangent, saved, entry_weight, exit_weight, head_count):
    normed, inverse, normed_low, queries, key_heads, values, softmax_weights, softmax_low, attended = saved
    lead_count, seq_length, side_count = (cotangent.shape[0], cotangent.shape[1], cotangent.shape[2])
    head_width = exit_weight.shape[1]
    head_size = head_width // head_count
    factor = 1.0 / math.sqrt(head_size)
    rows_dims = (((0, 1, 2), (0, 1, 2)), ((), ()))
    exit_grad = product_general(cotangent, attended, rows_dims)
    attended_grad = product_general(cotangent, exit_weight, (((3,), (0,)), ((), ()))).astype(jnp.bfloat16)
    attended_grad = attended_grad.reshape(lead_count, seq_length, side_count, head_count, head_size)
    softmax_grad = product_form('albhe,ambhe->abhlm', attended_grad, values)
    values_grad = product_form('abhlm,albhe->ambhe', softmax_low, attended_grad)
    centre = lax.optimization_barrier(jnp.sum(softmax_weights * softmax_grad, axis=-1, keepdims=True))
    scores_grad = (softmax_weights * (softmax_grad - centre) * factor).astype(jnp.bfloat16)
    queries_grad = product_form('abhlm,ambhe->albhe', scores_grad, key_heads)
    keys_grad = product_form('abhlm,albhe->ambhe', scores_grad, queries)
    mixture_grad = jnp.stack([queries_grad, keys_grad, values_grad], axis=3).astype(jnp.bfloat16)
    mixture_grad = mixture_grad.reshape(lead_count, seq_length, side_count, 3 * head_width)
    entry_grad = product_general(normed_low, mixture_grad, rows_dims)
    normed_grad = product_general(mixture_grad, entry_weight, (((3,), (1,)), ((), ())))
    inner_term = normed_grad - lax.optimization_barrier(jnp.mean(normed_grad, axis=-1, keepdims=True)) - normed * lax.optimization_barrier(jnp.mean(normed_grad * normed, axis=-1, keepdims=True))
    inputs_grad = lax.optimization_barrier(cotangent).astype(jnp.float32) + inverse * inner_term
    return (inputs_grad, entry_grad, exit_grad)

def reference(frames_in, bottleneck, spatial_entry, spatial_exit, temporal_entry, temporal_exit, output_grad, joined_grad):

    def per_clip(carry, items):
        frames, bottle, output_cot, joined_cot = items
        tokens_in = jnp.concatenate([frames, jnp.broadcast_to(bottle[None], (FRAMES, BOT, D))], axis=1)
        sequences = tokens_in[:, :, None, :]
        spatial_saved = attend(sequences, spatial_entry, HEADS)
        block_out = project_out(sequences, spatial_saved[8], spatial_exit)
        states = block_out[:, :PATCHES, 0, :].astype(jnp.bfloat16)[None]
        temporal_saved = attend(states, temporal_entry, HEADS)
        states_grad, temporal_in, temporal_out = backward(output_cot[None], temporal_saved, temporal_entry, temporal_exit, HEADS)
        state_grads = states_grad[0].astype(jnp.bfloat16)
        joined_rows = (lax.optimization_barrier(joined_cot).astype(jnp.float32) / FRAMES).astype(jnp.bfloat16)
        cotangent = jnp.concatenate([state_grads, jnp.broadcast_to(joined_rows[None], (FRAMES, BOT, D))], axis=1)[:, :, None, :]
        tokens_grad, spatial_in, spatial_out = backward(cotangent, spatial_saved, spatial_entry, spatial_exit, HEADS)
        frames_delta = tokens_grad[:, :PATCHES, 0, :].astype(jnp.bfloat16)
        bottleneck_delta = lax.optimization_barrier(jnp.sum(tokens_grad[:, PATCHES:, 0, :], axis=0)).astype(jnp.bfloat16)
        updated = (carry[0] + spatial_in, carry[1] + spatial_out, carry[2] + temporal_in, carry[3] + temporal_out)
        return (updated, (frames_delta, bottleneck_delta))
    start = (jnp.zeros((D, 3 * HEADS * HEAD), jnp.float32), jnp.zeros((D, HEADS * HEAD), jnp.float32), jnp.zeros((D, 3 * HEADS * HEAD), jnp.float32), jnp.zeros((D, HEADS * HEAD), jnp.float32))
    totals, stacked = lax.scan(per_clip, start, (frames_in, bottleneck, output_grad, joined_grad))
    grad_factor = 1.0 / math.sqrt(CLIPS * FRAMES * PATCHES)
    spatialin_grad = (totals[0] * grad_factor).astype(jnp.bfloat16)
    spatialout_grad = (totals[1] * grad_factor).astype(jnp.bfloat16)
    temporalin_grad = (totals[2] * grad_factor).astype(jnp.bfloat16)
    temporalout_grad = (totals[3] * grad_factor).astype(jnp.bfloat16)
    return (stacked[0], stacked[1], spatialin_grad, spatialout_grad, temporalin_grad, temporalout_grad)
```

```python
import functools
import math

import jax
import jax.numpy as jnp
from jax import lax
from jax.experimental import pallas as pl
from jax.experimental.pallas import tpu as pltpu
from jax.sharding import Mesh
from jax.sharding import PartitionSpec as P

HEADS = 8
EPSILON = 1e-05
FRAME = ("y", "zh", "c")
CHIPS = ("zl", "x", "y", "zh")
ALL = ("zl", "x", "y", "zh", "c")
BF = jnp.bfloat16
F32 = jnp.float32

NN = (((1,), (0,)), ((), ()))
NT = (((1,), (1,)), ((), ()))
TN = (((0,), (0,)), ((), ()))


def mm(a, b, dims):
    return lax.dot_general(a, b, dims, preferred_element_type=F32)


def normalize(u):
    centred = u - jnp.mean(u, axis=-1, keepdims=True)
    inverse = lax.rsqrt(jnp.mean(centred * centred, axis=-1, keepdims=True) + EPSILON)
    return centred * inverse, inverse


def half_masks(size):
    lane = lax.broadcasted_iota(jnp.int32, (1, 2 * size), 1)
    low = (lane < size).astype(F32)
    return low.astype(BF), (1.0 - low).astype(BF)


def attention_forward(mix_ref, keep, masks, save, put):
    width = 2 * (mix_ref.shape[1] // 3 // HEADS)
    side = mix_ref.shape[1] // 3
    factor = 1.0 / math.sqrt(width // 2)
    for p in range(HEADS // 2):
        q2 = mix_ref[:, p * width : (p + 1) * width]
        k2 = mix_ref[:, side + p * width : side + (p + 1) * width]
        v2 = mix_ref[:, 2 * side + p * width : 2 * side + (p + 1) * width]
        total = None
        for h in range(2):
            scores = mm(q2 * masks[h], k2, NT) * factor
            scores = jnp.where(keep, scores, -jnp.inf)
            scores = scores - jnp.max(scores, axis=-1, keepdims=True)
            expon = jnp.exp(scores)
            weights = expon / jnp.sum(expon, axis=-1, keepdims=True)
            save(2 * p + h, weights)
            part = mm(weights.astype(BF), v2 * masks[h], NN)
            total = part if total is None else total + part
        put(p, width, total.astype(BF))


def attention_backward(mix_ref, load, d_att, masks, put):
    width = 2 * (mix_ref.shape[1] // 3 // HEADS)
    side = mix_ref.shape[1] // 3
    factor = 1.0 / math.sqrt(width // 2)
    for p in range(HEADS // 2):
        q2 = mix_ref[:, p * width : (p + 1) * width]
        k2 = mix_ref[:, side + p * width : side + (p + 1) * width]
        v2 = mix_ref[:, 2 * side + p * width : 2 * side + (p + 1) * width]
        d2 = d_att[:, p * width : (p + 1) * width]
        dq = dk = dv = None
        for h in range(2):
            dh = d2 * masks[h]
            weights = load(2 * p + h)
            grad = mm(dh, v2, NT)
            centre = jnp.sum(weights * grad, axis=-1, keepdims=True)
            ds = (weights * (grad - centre) * factor).astype(BF)
            a = mm(ds, k2 * masks[h], NN)
            b = mm(ds, q2 * masks[h], TN)
            c = mm(weights.astype(BF), dh, TN)
            dq = a if dq is None else dq + a
            dk = b if dk is None else dk + b
            dv = c if dv is None else dv + c
        put(p * width, width, dq.astype(BF))
        put(side + p * width, width, dk.astype(BF))
        put(2 * side + p * width, width, dv.astype(BF))


def inputs_gradient(c, normed, inverse, d_normed):
    inner = (
        d_normed
        - jnp.mean(d_normed, axis=-1, keepdims=True)
        - normed * jnp.mean(d_normed * normed, axis=-1, keepdims=True)
    )
    return c.astype(F32) + inverse * inner


def picker(half):
    row = lax.broadcasted_iota(jnp.int32, (256, 128), 0)
    col = lax.broadcasted_iota(jnp.int32, (256, 128), 1)
    source = (col // 8) * 16 + half * 8 + col % 8
    return (row == source).astype(F32).astype(BF)


def pick(values, chosen, out_ref, at):
    for b in range(values.shape[1] // 256):
        part = mm(values[:, 256 * b : 256 * (b + 1)], chosen, NN)
        out_ref[:, at + 128 * b : at + 128 * (b + 1)] = part.astype(BF)


def spatial_forward_kernel(
    frames_ref, bottle_ref, entry_ref, exit_ref, grad_ref,
    packed_ref, normed_ref, inverse_ref, mix_ref, weights_ref, att_ref, tokens,
):
    patches, bots = frames_ref.shape[0], bottle_ref.shape[0]
    rows, width = tokens.shape
    tokens[0:patches, :] = frames_ref[...].astype(F32)
    tokens[patches:rows, :] = jnp.zeros((rows - patches, width), F32)
    tokens[patches : patches + bots, :] = bottle_ref[...].astype(F32)
    normed, inverse = normalize(tokens[...])
    normed_ref[...] = normed
    inverse_ref[...] = inverse
    low = normed.astype(BF)
    mix_ref[...] = mm(low, entry_ref[...], NN).astype(BF)
    masks = half_masks(exit_ref.shape[1] // HEADS)
    keep = lax.broadcasted_iota(jnp.int32, (rows, rows), 1) < patches + bots

    def save(h, weights):
        weights_ref[h] = weights

    def put(p, w, value):
        att_ref[:, p * w : (p + 1) * w] = value

    attention_forward(mix_ref, keep, masks, save, put)
    out = tokens[0:patches, :] + mm(att_ref[0:patches, :], exit_ref[...], NT)
    packed_ref[:, 0:width] = out.astype(BF)
    packed_ref[:, width : 2 * width] = grad_ref[...]


def temporal_kernel(
    frames, core_ref, moved_ref, entry_ref, exit_ref,
    back_ref, send_ref, kept_ref, mix_ref, weights_ref, att_ref, d_mix_ref,
):
    rows, width = back_ref.shape
    side = exit_ref.shape[1]
    seqs = rows // frames
    normed, inverse = normalize(moved_ref[:, 0:width].astype(F32))
    low = normed.astype(BF)
    mix_ref[...] = mm(low, entry_ref[...], NN).astype(BF)
    masks = half_masks(side // HEADS)
    keep = (
        lax.broadcasted_iota(jnp.int32, (rows, rows), 0) % seqs
        == lax.broadcasted_iota(jnp.int32, (rows, rows), 1) % seqs
    )

    def save(h, weights):
        weights_ref[h] = weights

    def put(p, w, value):
        att_ref[:, p * w : (p + 1) * w] = value

    attention_forward(mix_ref, keep, masks, save, put)
    c = moved_ref[:, width : 2 * width]
    d_att = mm(c, exit_ref[...], NN).astype(BF)

    def put_grad(at, w, value):
        d_mix_ref[:, at : at + w] = value

    attention_backward(mix_ref, lambda h: weights_ref[h], d_att, masks, put_grad)
    d_normed = mm(d_mix_ref[...], entry_ref[...], NT)
    back_ref[...] = inputs_gradient(c, normed, inverse, d_normed).astype(BF)
    core = core_ref[0]
    other, own = picker(1 - core), picker(core)
    pick(low, other, send_ref, 0)
    pick(c, other, send_ref, width // 2)
    send_ref[:, width : width + 3 * side] = d_mix_ref[...]
    send_ref[:, width + 3 * side : width + 4 * side] = att_ref[...]
    pick(low, own, kept_ref, 0)
    pick(c, own, kept_ref, width // 2)


def spatial_backward_kernel(
    core_ref, back_ref, joined_ref, normed_ref, inverse_ref, mix_ref, weights_ref, att_ref,
    entry_ref, exit_ref, delta_ref, bottle_ref, send_ref, kept_ref, cot, d_mix_ref,
):
    patches, width = back_ref.shape
    rows, bots, side = normed_ref.shape[0], joined_ref.shape[0], exit_ref.shape[1]
    cot[0:patches, :] = back_ref[...].astype(F32)
    cot[patches:rows, :] = jnp.zeros((rows - patches, width), F32)
    cot[patches : patches + bots, :] = joined_ref[...].astype(F32)
    c = cot[...].astype(BF)
    masks = half_masks(side // HEADS)
    d_att = mm(c, exit_ref[...], NN).astype(BF)

    def put_grad(at, w, value):
        d_mix_ref[:, at : at + w] = value

    attention_backward(mix_ref, lambda h: weights_ref[h], d_att, masks, put_grad)
    d_normed = mm(d_mix_ref[...], entry_ref[...], NT)
    normed = normed_ref[...]
    grads = inputs_gradient(c, normed, inverse_ref[...], d_normed)
    delta_ref[...] = grads[0:patches, :].astype(BF)
    bottle_ref[...] = grads[patches : patches + 8, :]
    low = normed.astype(BF)
    core = core_ref[0]
    other, own = picker(1 - core), picker(core)
    pick(low, other, send_ref, 0)
    pick(c, other, send_ref, width // 2)
    send_ref[:, width : width + 3 * side] = d_mix_ref[...]
    send_ref[:, width + 3 * side : width + 4 * side] = att_ref[...]
    pick(low, own, kept_ref, 0)
    pick(c, own, kept_ref, width // 2)


def weight_gradient_kernel(kept_ref, sent_ref, got_ref, out_ref):
    half = kept_ref.shape[1] // 2
    rows, width = kept_ref.shape
    side = (sent_ref.shape[1] - width) // 4
    left = [
        jnp.concatenate([kept_ref[:, at : at + half], got_ref[:, at : at + half]], axis=0)
        for at in (0, half)
    ]
    for j in range(4):
        cols = slice(width + j * side, width + (j + 1) * side)
        right = jnp.concatenate([sent_ref[:, cols], got_ref[:, cols]], axis=0)
        out_ref[:, j * side : (j + 1) * side] = mm(left[j // 3], right, TN).astype(BF)


def sum_kernel(scale, parts_ref, entry_ref, exit_ref):
    total = jnp.sum(parts_ref[...].astype(F32), axis=0) * scale
    entry_ref[...] = total[:, : entry_ref.shape[1]].astype(BF)
    exit_ref[...] = total[:, entry_ref.shape[1] :].astype(BF)


VMEM = pl.BlockSpec(memory_space=pltpu.VMEM)
SMEM = pl.BlockSpec(memory_space=pltpu.SMEM)


def call(kernel, out_shape, in_specs, scratch=(), flops=0, limit=40):
    return pl.pallas_call(
        kernel,
        out_shape=tuple(jax.ShapeDtypeStruct(s, d) for s, d in out_shape),
        in_specs=in_specs,
        out_specs=tuple(VMEM for _ in out_shape),
        scratch_shapes=list(scratch),
        compiler_params=pltpu.CompilerParams(vmem_limit_bytes=limit * 1024 * 1024),
        cost_estimate=pl.CostEstimate(flops=flops, bytes_accessed=4_000_000, transcendentals=0),
    )


def per_device(
    frames_in, bottleneck, spatial_entry, spatial_exit, temporal_entry, temporal_exit,
    output_grad, joined_grad,
):
    patches, width = frames_in.shape[2], frames_in.shape[3]
    bots, side = bottleneck.shape[1], spatial_exit.shape[1]
    frames = lax.axis_size(FRAME)
    chips = lax.axis_size(CHIPS)
    rows = -(-(patches + bots) // 16) * 16
    core = lax.axis_index("c").astype(jnp.int32).reshape(1)
    clips = lax.axis_size(("zl", "x"))
    scale = 1.0 / math.sqrt(clips * frames * patches)

    packed, normed, inverse, mix, weights, att = call(
        spatial_forward_kernel,
        [
            ((patches, 2 * width), BF), ((rows, width), F32), ((rows, 1), F32),
            ((rows, 3 * side), BF), ((HEADS, rows, rows), F32), ((rows, side), BF),
        ],
        [VMEM] * 5,
        [pltpu.VMEM((rows, width), F32)],
        flops=1_000_000_000,
    )(frames_in[0, 0], bottleneck[0], spatial_entry, spatial_exit, output_grad[0, 0])

    moved = lax.all_to_all(
        packed.reshape(frames, patches // frames, 2 * width), FRAME, 0, 0, tiled=True
    ).reshape(patches, 2 * width)

    back, send_t, kept_t = call(
        functools.partial(temporal_kernel, frames),
        [((patches, width), BF), ((patches, width + 4 * side), BF), ((patches, width), BF)],
        [SMEM] + [VMEM] * 3,
        [
            pltpu.VMEM((patches, 3 * side), BF), pltpu.VMEM((HEADS, patches, patches), F32),
            pltpu.VMEM((patches, side), BF), pltpu.VMEM((patches, 3 * side), BF),
        ],
        flops=2_000_000_000,
    )(core, moved, temporal_entry, temporal_exit)

    back = lax.all_to_all(
        back.reshape(frames, patches // frames, width), FRAME, 0, 0, tiled=True
    ).reshape(patches, width)

    def chip_sums(kept, sent):
        got = lax.ppermute(sent, "c", [(0, 1), (1, 0)])
        (partial,) = call(
            weight_gradient_kernel, [((width // 2, 4 * side), BF)], [VMEM] * 3,
            flops=1_000_000_000,
        )(kept, sent, got)
        return partial.reshape(chips, -1, 4 * side)

    joined = (joined_grad[0].astype(F32) / frames).astype(BF)
    delta, local_bottle, send_s, kept_s = call(
        spatial_backward_kernel,
        [
            ((patches, width), BF), ((8, width), F32),
            ((rows, width + 4 * side), BF), ((rows, width), BF),
        ],
        [SMEM] + [VMEM] * 9,
        [pltpu.VMEM((rows, width), F32), pltpu.VMEM((rows, 3 * side), BF)],
        flops=2_000_000_000,
    )(core, back, joined, normed, inverse, mix, weights, att, spatial_entry, spatial_exit)

    bottleneck_delta = lax.psum(local_bottle[:bots], FRAME).astype(BF)[None]

    def finish(partial):
        parts = lax.all_to_all(partial, CHIPS, 0, 0, tiled=True)
        own = parts.shape[1]
        return call(
            functools.partial(sum_kernel, scale),
            [((own, 3 * side), BF), ((own, side), BF)], [VMEM],
            flops=1_000_000,
        )(parts)

    t_entry, t_exit = finish(chip_sums(kept_t, send_t))
    s_entry, s_exit = finish(chip_sums(kept_s, send_s))
    return (delta[None, None], bottleneck_delta, s_entry, s_exit, t_entry, t_exit)


def solution(mesh):
    finer = Mesh(mesh.devices.reshape(2, mesh.shape["dp"] // 2, 4, 2, 2), ALL)
    dp = ("zl", "x")
    row = P(ALL, None)
    clip = P(dp, None, None)
    patch = P(dp, FRAME, None, None)
    return jax.shard_map(
        per_device,
        mesh=finer,
        in_specs=(patch, clip, P(), P(), P(), P(), patch, clip),
        out_specs=(patch, clip, row, row, row, row),
        check_vma=False,
    )
```

```python
import functools
import math

import jax
import jax.numpy as jnp
from jax import lax
from jax.experimental import pallas as pl
from jax.experimental.pallas import tpu as pltpu
from jax.sharding import Mesh
from jax.sharding import PartitionSpec as P

HEADS = 8
EPSILON = 1e-05
FRAME = ("y", "zh", "c")
CHIPS = ("zl", "x", "y", "zh")
ALL = ("zl", "x", "y", "zh", "c")
BF = jnp.bfloat16
F32 = jnp.float32

NN = (((1,), (0,)), ((), ()))
NT = (((1,), (1,)), ((), ()))
TN = (((0,), (0,)), ((), ()))


def mm(a, b, dims):
    return lax.dot_general(a, b, dims, preferred_element_type=F32)


def normalize(u):
    centred = u - jnp.mean(u, axis=-1, keepdims=True)
    inverse = lax.rsqrt(jnp.mean(centred * centred, axis=-1, keepdims=True) + EPSILON)
    return centred * inverse, inverse


def half_masks(size):
    lane = lax.broadcasted_iota(jnp.int32, (1, 2 * size), 1)
    low = (lane < size).astype(F32)
    return low.astype(BF), (1.0 - low).astype(BF)


def attention_forward(mix_ref, keep, masks, save, put):
    width = 2 * (mix_ref.shape[1] // 3 // HEADS)
    side = mix_ref.shape[1] // 3
    factor = 1.0 / math.sqrt(width // 2)
    for p in range(HEADS // 2):
        q2 = mix_ref[:, p * width : (p + 1) * width]
        k2 = mix_ref[:, side + p * width : side + (p + 1) * width]
        v2 = mix_ref[:, 2 * side + p * width : 2 * side + (p + 1) * width]
        total = None
        for h in range(2):
            scores = mm(q2 * masks[h], k2, NT) * factor
            scores = jnp.where(keep, scores, -jnp.inf)
            scores = scores - jnp.max(scores, axis=-1, keepdims=True)
            expon = jnp.exp(scores)
            weights = expon / jnp.sum(expon, axis=-1, keepdims=True)
            save(2 * p + h, weights)
            part = mm(weights.astype(BF), v2 * masks[h], NN)
            total = part if total is None else total + part
        put(p, width, total.astype(BF))


def attention_backward(mix_ref, load, d_att, masks, put):
    width = 2 * (mix_ref.shape[1] // 3 // HEADS)
    side = mix_ref.shape[1] // 3
    factor = 1.0 / math.sqrt(width // 2)
    for p in range(HEADS // 2):
        q2 = mix_ref[:, p * width : (p + 1) * width]
        k2 = mix_ref[:, side + p * width : side + (p + 1) * width]
        v2 = mix_ref[:, 2 * side + p * width : 2 * side + (p + 1) * width]
        d2 = d_att[:, p * width : (p + 1) * width]
        dq = dk = dv = None
        for h in range(2):
            dh = d2 * masks[h]
            weights = load(2 * p + h)
            grad = mm(dh, v2, NT)
            centre = jnp.sum(weights * grad, axis=-1, keepdims=True)
            ds = (weights * (grad - centre) * factor).astype(BF)
            a = mm(ds, k2 * masks[h], NN)
            b = mm(ds, q2 * masks[h], TN)
            c = mm(weights.astype(BF), dh, TN)
            dq = a if dq is None else dq + a
            dk = b if dk is None else dk + b
            dv = c if dv is None else dv + c
        put(p * width, width, dq.astype(BF))
        put(side + p * width, width, dk.astype(BF))
        put(2 * side + p * width, width, dv.astype(BF))


def inputs_gradient(c, normed, inverse, d_normed):
    inner = (
        d_normed
        - jnp.mean(d_normed, axis=-1, keepdims=True)
        - normed * jnp.mean(d_normed * normed, axis=-1, keepdims=True)
    )
    return c.astype(F32) + inverse * inner


def picker(half):
    row = lax.broadcasted_iota(jnp.int32, (256, 128), 0)
    col = lax.broadcasted_iota(jnp.int32, (256, 128), 1)
    source = (col // 8) * 16 + half * 8 + col % 8
    return (row == source).astype(F32).astype(BF)


def pick(values, chosen, out_ref, at):
    for b in range(values.shape[1] // 256):
        part = mm(values[:, 256 * b : 256 * (b + 1)], chosen, NN)
        out_ref[:, at + 128 * b : at + 128 * (b + 1)] = part.astype(BF)


class Mover:
    def __init__(self, sems):
        self.sems, self.count = sems, 0

    def start(self, source, target):
        copy = pltpu.make_async_copy(source, target, self.sems.at[self.count])
        self.count += 1
        copy.start()
        return copy


def finish(copies):
    for copy in copies:
        copy.wait()


def fill_tokens(tokens, frames, bottle):
    patches, bots = frames.shape[0], bottle.shape[0]
    rows, width = tokens.shape
    tokens[0:patches, :] = frames[...].astype(F32)
    tokens[patches:rows, :] = jnp.zeros((rows - patches, width), F32)
    tokens[patches : patches + bots, :] = bottle[...].astype(F32)


def spatial_forward_kernel(
    frames_hbm, bottle_hbm, entry_hbm, exit_hbm, grad_hbm,
    packed_hbm, mix_hbm, weights_hbm, att_hbm,
    frames, bottle, entry, exit_, tokens, packed, mix, weights_buf, att, sems,
):
    move = Mover(sems)
    patches, bots = frames.shape[0], bottle.shape[0]
    rows, width = tokens.shape
    side = exit_.shape[1]
    first = [move.start(frames_hbm, frames), move.start(bottle_hbm, bottle)]
    columns = [slice(j * side, (j + 1) * side) for j in range(3)]
    entries = [move.start(entry_hbm.at[:, c], entry.at[:, c]) for c in columns]
    later = move.start(exit_hbm, exit_)
    grads = move.start(grad_hbm, packed.at[:, width : 2 * width])
    outs = []
    finish(first)
    fill_tokens(tokens, frames, bottle)
    low = normalize(tokens[...])[0].astype(BF)
    for c, copy in zip(columns, entries):
        copy.wait()
        mix[:, c] = mm(low, entry[:, c], NN).astype(BF)
    outs.append(move.start(mix, mix_hbm))
    masks = half_masks(side // HEADS)
    keep = lax.broadcasted_iota(jnp.int32, (rows, rows), 1) < patches + bots

    def save(h, weights):
        weights_buf[h] = weights
        outs.append(move.start(weights_buf.at[h], weights_hbm.at[h]))

    def put(p, w, value):
        att[:, p * w : (p + 1) * w] = value

    attention_forward(mix, keep, masks, save, put)
    outs.append(move.start(att, att_hbm))
    later.wait()
    out = tokens[0:patches, :] + mm(att[0:patches, :], exit_[...], NT)
    packed[:, 0:width] = out.astype(BF)
    grads.wait()
    outs.append(move.start(packed, packed_hbm))
    finish(outs)


def spatial_factors_kernel(
    core_ref, frames_hbm, bottle_hbm, att_hbm, send_hbm, kept_hbm,
    frames, bottle, tokens, send, kept, sems,
):
    move = Mover(sems)
    half = kept.shape[1]
    first = [move.start(frames_hbm, frames), move.start(bottle_hbm, bottle)]
    copied = move.start(att_hbm, send.at[:, half:])
    finish(first)
    fill_tokens(tokens, frames, bottle)
    low = normalize(tokens[...])[0].astype(BF)
    core = core_ref[0]
    pick(low, picker(1 - core), send, 0)
    copied.wait()
    outs = [move.start(send, send_hbm)]
    pick(low, picker(core), kept, 0)
    outs.append(move.start(kept, kept_hbm))
    finish(outs)


def temporal_kernel(
    frames, moved_hbm, entry_hbm, exit_hbm, back_hbm, d_mix_hbm, att_hbm,
    moved, entry, exit_, back, mix, weights_buf, att, d_mix, sems,
):
    move = Mover(sems)
    rows, width = back.shape
    side = exit_.shape[1]
    seqs = rows // frames
    first = move.start(moved_hbm, moved)
    columns = [slice(j * side, (j + 1) * side) for j in range(3)]
    entries = [move.start(entry_hbm.at[:, c], entry.at[:, c]) for c in columns]
    later = move.start(exit_hbm, exit_)
    first.wait()
    normed, inverse = normalize(moved[:, 0:width].astype(F32))
    low = normed.astype(BF)
    for c, copy in zip(columns, entries):
        copy.wait()
        mix[:, c] = mm(low, entry[:, c], NN).astype(BF)
    masks = half_masks(side // HEADS)
    keep = (
        lax.broadcasted_iota(jnp.int32, (rows, rows), 0) % seqs
        == lax.broadcasted_iota(jnp.int32, (rows, rows), 1) % seqs
    )

    def save(h, weights):
        weights_buf[h] = weights

    def put(p, w, value):
        att[:, p * w : (p + 1) * w] = value

    attention_forward(mix, keep, masks, save, put)
    outs = [move.start(att, att_hbm)]
    later.wait()
    cot = moved[:, width : 2 * width]
    d_att = mm(cot, exit_[...], NN).astype(BF)

    def put_grad(at, w, value):
        d_mix[:, at : at + w] = value

    attention_backward(mix, lambda h: weights_buf[h], d_att, masks, put_grad)
    outs.append(move.start(d_mix, d_mix_hbm))
    d_normed = mm(d_mix[...], entry[...], NT)
    back[...] = inputs_gradient(cot, normed, inverse, d_normed).astype(BF)
    outs.append(move.start(back, back_hbm))
    finish(outs)


def temporal_factors_kernel(
    core_ref, moved_hbm, att_hbm, d_mix_hbm, send_hbm, kept_hbm, moved, send, kept, sems
):
    move = Mover(sems)
    width = moved.shape[1] // 2
    half, side = width // 2, att_hbm.shape[1]
    first = move.start(moved_hbm, moved)
    copied = [
        move.start(att_hbm, send.at[:, half : half + side]),
        move.start(d_mix_hbm, send.at[:, width + side : width + 4 * side]),
    ]
    first.wait()
    low = normalize(moved[:, 0:width].astype(F32))[0].astype(BF)
    cot = moved[:, width : 2 * width]
    core = core_ref[0]
    other = picker(1 - core)
    pick(low, other, send, 0)
    pick(cot, other, send, half + side)
    finish(copied)
    outs = [move.start(send, send_hbm)]
    own = picker(core)
    pick(low, own, kept, 0)
    pick(cot, own, kept, half)
    outs.append(move.start(kept, kept_hbm))
    finish(outs)


def fill_cotangent(cot, joined, frames):
    patches = cot.shape[0] - 16
    rows = joined[...].astype(F32) / frames
    padded = jnp.concatenate([rows, jnp.zeros((16 - rows.shape[0], rows.shape[1]), F32)], axis=0)
    cot[patches:, :] = padded.astype(BF)


def spatial_backward_kernel(
    frames, core_ref, back_hbm, joined_hbm, mix_hbm, weights_hbm, exit_hbm, send_hbm, kept_hbm,
    cot, joined, mix, weights_buf, exit_, send, kept, sems,
):
    move = Mover(sems)
    side, half = exit_.shape[1], kept.shape[1]
    patches = back_hbm.shape[0]
    first = [move.start(joined_hbm, joined), move.start(back_hbm, cot.at[0:patches, :])]
    first.append(move.start(exit_hbm, exit_))
    second = move.start(mix_hbm, mix)
    heads = [move.start(weights_hbm.at[h], weights_buf.at[h]) for h in range(HEADS)]
    finish(first)
    fill_cotangent(cot, joined, frames)
    c = cot[...]
    d_att = mm(c, exit_[...], NN).astype(BF)
    core = core_ref[0]
    pick(c, picker(core), kept, 0)
    outs = [move.start(kept, kept_hbm)]
    pick(c, picker(1 - core), send, 0)
    masks = half_masks(side // HEADS)
    second.wait()

    def load(h):
        heads[h].wait()
        return weights_buf[h]

    def put_grad(at, w, value):
        send[:, half + at : half + at + w] = value

    attention_backward(mix, load, d_att, masks, put_grad)
    outs.append(move.start(send, send_hbm))
    finish(outs)


def spatial_inputs_kernel(
    frames_count, frames_hbm, bottle_hbm, back_hbm, joined_hbm, send_hbm, entry_hbm,
    delta_hbm, local_hbm, frames, bottle, cot, joined, d_mix, entry, tokens, delta, local, sems,
):
    move = Mover(sems)
    patches, width = delta.shape
    half = send_hbm.shape[1] - d_mix.shape[1]
    first = [move.start(frames_hbm, frames), move.start(bottle_hbm, bottle)]
    second = [
        move.start(send_hbm.at[:, half:], d_mix),
        move.start(entry_hbm, entry),
        move.start(joined_hbm, joined),
        move.start(back_hbm, cot.at[0:patches, :]),
    ]
    finish(first)
    fill_tokens(tokens, frames, bottle)
    normed, inverse = normalize(tokens[...])
    finish(second)
    fill_cotangent(cot, joined, frames_count)
    d_normed = mm(d_mix[...], entry[...], NT)
    grads = inputs_gradient(cot[...], normed, inverse, d_normed)
    delta[...] = grads[0:patches, :].astype(BF)
    outs = [move.start(delta, delta_hbm)]
    local[...] = grads[patches : patches + local.shape[0], :]
    outs.append(move.start(local, local_hbm))
    finish(outs)


def weight_gradient_kernel(places, in_turns, *refs):
    if in_turns:
        core_ref, refs = refs[0], refs[1:]
    arrays, refs = refs[: len(refs) - 7], refs[len(refs) - 7 :]
    out_hbm, left_n, left_c, right_m, right_a, out, sems = refs
    move = Mover(sems)
    rows = left_n.shape[0] // 2

    def both(target, pair):
        copies = []
        for k, (index, at) in enumerate(pair):
            source = arrays[index].at[:, at : at + target.shape[1]]
            copies.append(move.start(source, target.at[k * rows : (k + 1) * rows, :]))
        return copies

    ready = [both(t, places[k]) for k, t in enumerate((left_c, right_a, left_n, right_m))]
    side = right_a.shape[1]
    outs = []

    def put(at, value):
        if not in_turns:
            out[:, at : at + side] = value
        else:
            core = core_ref[0]
            for b in range(32):
                zl, x, y = b // 16, b // 4 % 4, b % 4
                turn = jnp.where(core == 0, x * 8 + y * 2 + zl, y * 8 + x * 2 + zl)
                where = pl.ds(pl.multiple_of(turn * 16, 16), 16)
                out[where, at : at + side] = value[b * 16 : (b + 1) * 16, :]
        columns = slice(at, at + side)
        outs.append(move.start(out.at[:, columns], out_hbm.at[:, columns]))

    finish(ready[0] + ready[1])
    put(3 * side, mm(left_c[...], right_a[...], TN).astype(BF))
    finish(ready[2] + ready[3])
    for j in range(3):
        put(j * side, mm(left_n[...], right_m[:, j * side : (j + 1) * side], TN).astype(BF))
    finish(outs)


def sum_kernel(
    scale, parts_hbm, summed_hbm, s_entry_hbm, s_exit_hbm, t_entry_hbm, t_exit_hbm,
    parts, summed, s_entry, s_exit, t_entry, t_exit, sems,
):
    move = Mover(sems)
    side = s_exit.shape[1]
    columns = [slice(j * side, (j + 1) * side) for j in range(4)]
    copies = [move.start(parts_hbm.at[:, :, c], parts.at[:, :, c]) for c in columns]
    temporal = move.start(summed_hbm, summed)
    for j, (c, copy) in enumerate(zip(columns, copies)):
        copy.wait()
        total = (jnp.sum(parts[:, :, c].astype(F32), axis=0) * scale).astype(BF)
        if j < 3:
            s_entry[:, c] = total
        else:
            s_exit[...] = total
    outs = [move.start(s_entry, s_entry_hbm), move.start(s_exit, s_exit_hbm)]
    temporal.wait()
    total = (summed[...].astype(F32) * scale).astype(BF)
    t_entry[...] = total[:, : 3 * side]
    t_exit[...] = total[:, 3 * side :]
    outs += [move.start(t_entry, t_entry_hbm), move.start(t_exit, t_exit_hbm)]
    finish(outs)


HBM = pl.BlockSpec(memory_space=pltpu.HBM)
SMEM = pl.BlockSpec(memory_space=pltpu.SMEM)


def call(kernel, outs, ins, scratch, copies, flops):
    moved = sum(math.prod(a.shape) * a.dtype.itemsize for a in ins)
    moved += sum(math.prod(s) * jnp.dtype(d).itemsize for s, d in outs)
    return pl.pallas_call(
        kernel,
        out_shape=tuple(jax.ShapeDtypeStruct(s, d) for s, d in outs),
        in_specs=[SMEM if a.ndim == 1 else HBM for a in ins],
        out_specs=tuple(HBM for _ in outs),
        scratch_shapes=[pltpu.VMEM(s, d) for s, d in scratch]
        + [pltpu.SemaphoreType.DMA((copies,))],
        compiler_params=pltpu.CompilerParams(vmem_limit_bytes=40 * 1024 * 1024),
        cost_estimate=pl.CostEstimate(flops=flops, bytes_accessed=moved, transcendentals=0),
    )(*ins)


def turns(shape):
    zls, xs, ys, zhs, cores = (range(n) for n in shape)

    def at(zl, x, y, zh, c):
        return (((zl * shape[1] + x) * shape[2] + y) * shape[3] + zh) * shape[4] + c

    along_x = [
        [[at(zl, x, y, zh, c) for x in xs] for zl in zls for y in ys for zh in zhs] for c in cores
    ]
    along_y = [
        [[at(zl, x, y, zh, c) for y in ys] for zl in zls for x in xs for zh in zhs] for c in cores
    ]
    along_z = [
        [at(zl, x, y, zh, c) for zl in zls for zh in zhs] for x in xs for y in ys for c in cores
    ]
    return along_x[0] + along_y[1], along_y[0] + along_x[1], along_z


def per_device(
    frames_in, bottleneck, spatial_entry, spatial_exit, temporal_entry, temporal_exit,
    output_grad, joined_grad,
):
    patches, width = frames_in.shape[2], frames_in.shape[3]
    bots, side = bottleneck.shape[1], spatial_exit.shape[1]
    half = width // 2
    frames = lax.axis_size(FRAME)
    chips = lax.axis_size(CHIPS)
    rows = patches + 16
    core = lax.axis_index("c").astype(jnp.int32).reshape(1)
    clips = lax.axis_size(("zl", "x"))
    scale = 1.0 / math.sqrt(clips * frames * patches)
    frame, bottle, joined = frames_in[0, 0], bottleneck[0], joined_grad[0]
    swap = [(0, 1), (1, 0)]

    def exchange(array):
        blocks = array.reshape(frames, patches // frames, array.shape[1])
        return lax.all_to_all(blocks, FRAME, 0, 0, tiled=True).reshape(array.shape)

    packed, mix, weights, att = call(
        spatial_forward_kernel,
        [
            ((patches, 2 * width), BF), ((rows, 3 * side), BF), ((HEADS, rows, rows), F32),
            ((rows, side), BF),
        ],
        [frame, bottle, spatial_entry, spatial_exit, output_grad[0, 0]],
        [
            ((patches, width), BF), ((bots, width), BF), ((width, 3 * side), BF),
            ((width, side), BF), ((rows, width), F32),
            ((patches, 2 * width), BF), ((rows, 3 * side), BF), ((HEADS, rows, rows), F32),
            ((rows, side), BF),
        ],
        10 + HEADS,
        1_000_000_000,
    )
    moved = exchange(packed)

    send_s1, kept_sn = call(
        spatial_factors_kernel,
        [((rows, half + side), BF), ((rows, half), BF)],
        [core, frame, bottle, att],
        [
            ((patches, width), BF), ((bots, width), BF), ((rows, width), F32),
            ((rows, half + side), BF), ((rows, half), BF),
        ],
        5,
        300_000_000,
    )
    got_s1 = lax.ppermute(send_s1, "c", swap)

    back, d_mix_t, att_t = call(
        functools.partial(temporal_kernel, frames),
        [((patches, width), BF), ((patches, 3 * side), BF), ((patches, side), BF)],
        [moved, temporal_entry, temporal_exit],
        [
            ((patches, 2 * width), BF), ((width, 3 * side), BF), ((width, side), BF),
            ((patches, width), BF), ((patches, 3 * side), BF), ((HEADS, patches, patches), F32),
            ((patches, side), BF), ((patches, 3 * side), BF),
        ],
        8,
        2_000_000_000,
    )
    back = exchange(back)

    send_t, kept_t = call(
        temporal_factors_kernel,
        [((patches, half + side + half + 3 * side), BF), ((patches, width), BF)],
        [core, moved, att_t, d_mix_t],
        [
            ((patches, 2 * width), BF), ((patches, half + side + half + 3 * side), BF),
            ((patches, width), BF),
        ],
        5,
        300_000_000,
    )
    got_t = lax.ppermute(send_t, "c", swap)

    def weight_gradient(count, places, arrays, in_turns):
        return call(
            functools.partial(weight_gradient_kernel, places, in_turns),
            [((half, 4 * side), BF)],
            ([core] if in_turns else []) + arrays,
            [
                ((2 * count, half), BF), ((2 * count, half), BF), ((2 * count, 3 * side), BF),
                ((2 * count, side), BF), ((half, 4 * side), BF),
            ],
            12,
            1_000_000_000,
        )[0]

    cot_at, mix_at = half + side, half + side + half
    partial_t = weight_gradient(
        patches,
        (
            ((0, half), (2, cot_at)), ((1, half), (2, half)),
            ((0, 0), (2, 0)), ((1, mix_at), (2, mix_at)),
        ),
        [kept_t, send_t, got_t],
        True,
    )
    summed_t = partial_t
    for groups in turns([lax.axis_size(a) for a in ALL]):
        summed_t = lax.psum_scatter(
            summed_t, ALL, scatter_dimension=0, axis_index_groups=groups, tiled=True
        )

    send_s2, kept_sc = call(
        functools.partial(spatial_backward_kernel, frames),
        [((rows, half + 3 * side), BF), ((rows, half), BF)],
        [core, back, joined, mix, weights, spatial_exit],
        [
            ((rows, width), BF), ((bots, width), BF), ((rows, 3 * side), BF),
            ((HEADS, rows, rows), F32), ((width, side), BF), ((rows, half + 3 * side), BF),
            ((rows, half), BF),
        ],
        6 + HEADS,
        1_500_000_000,
    )
    got_s2 = lax.ppermute(send_s2, "c", swap)
    delta, local = call(
        functools.partial(spatial_inputs_kernel, frames),
        [((patches, width), BF), ((8, width), F32)],
        [frame, bottle, back, joined, send_s2, spatial_entry],
        [
            ((patches, width), BF), ((bots, width), BF), ((rows, width), BF), ((bots, width), BF),
            ((rows, 3 * side), BF), ((width, 3 * side), BF), ((rows, width), F32),
            ((patches, width), BF), ((8, width), F32),
        ],
        8,
        1_000_000_000,
    )
    partial_s = weight_gradient(
        rows,
        (
            ((3, 0), (5, 0)), ((1, half), (2, half)),
            ((0, 0), (2, 0)), ((4, half), (5, half)),
        ),
        [kept_sn, send_s1, got_s1, kept_sc, send_s2, got_s2],
        False,
    )
    parts = lax.all_to_all(partial_s.reshape(chips, -1, 4 * side), CHIPS, 0, 0, tiled=True)

    local = local[:bots]
    for axis, bit in (("c", 1), ("zh", 1), ("y", 1), ("y", 2)):
        pairs = [(i, i ^ bit) for i in range(lax.axis_size(axis))]
        local = local + lax.ppermute(local, axis, pairs)

    own = parts.shape[1]
    s_entry, s_exit, t_entry, t_exit = call(
        functools.partial(sum_kernel, scale),
        [((own, 3 * side), BF), ((own, side), BF)] * 2,
        [parts, summed_t],
        [
            (parts.shape, BF), ((own, 4 * side), BF),
            ((own, 3 * side), BF), ((own, side), BF), ((own, 3 * side), BF), ((own, side), BF),
        ],
        9,
        1_000_000,
    )
    return (
        delta[None, None], local.astype(BF)[None], s_entry, s_exit, t_entry, t_exit
    )


def solution(mesh):
    finer = Mesh(mesh.devices.reshape(2, mesh.shape["dp"] // 2, 4, 2, 2), ALL)
    dp = ("zl", "x")
    row = P(ALL, None)
    clip = P(dp, None, None)
    patch = P(dp, FRAME, None, None)
    return jax.shard_map(
        per_device,
        mesh=finer,
        in_specs=(patch, clip, P(), P(), P(), P(), patch, clip),
        out_specs=(patch, clip, row, row, row, row),
        check_vma=False,
    )
```

```python
import functools
import itertools
import math

import jax
import jax.numpy as jnp
from jax import lax
from jax.experimental import pallas as pl
from jax.experimental.pallas import tpu as pltpu
from jax.sharding import Mesh
from jax.sharding import PartitionSpec as P

HEADS = 8
EPSILON = 1e-05
FRAME = ("y", "zh", "c")
ALL = ("zl", "x", "y", "zh", "c")
BF = jnp.bfloat16
F32 = jnp.float32

NN = (((1,), (0,)), ((), ()))
NT = (((1,), (1,)), ((), ()))
TN = (((0,), (0,)), ((), ()))


def mm(a, b, dims):
    return lax.dot_general(a, b, dims, preferred_element_type=F32)


def normalize(u):
    centred = u - jnp.mean(u, axis=-1, keepdims=True)
    inverse = lax.rsqrt(jnp.mean(centred * centred, axis=-1, keepdims=True) + EPSILON)
    return centred * inverse, inverse


def half_masks(size):
    lane = lax.broadcasted_iota(jnp.int32, (1, 2 * size), 1)
    low = (lane < size).astype(F32)
    return low.astype(BF), (1.0 - low).astype(BF)


def attention_forward(mix_ref, keep, masks, save, put):
    width = 2 * (mix_ref.shape[1] // 3 // HEADS)
    side = mix_ref.shape[1] // 3
    factor = 1.0 / math.sqrt(width // 2)
    for p in range(HEADS // 2):
        q2 = mix_ref[:, p * width : (p + 1) * width]
        k2 = mix_ref[:, side + p * width : side + (p + 1) * width]
        v2 = mix_ref[:, 2 * side + p * width : 2 * side + (p + 1) * width]
        total = None
        for h in range(2):
            scores = mm(q2 * masks[h], k2, NT) * factor
            scores = jnp.where(keep, scores, -jnp.inf)
            scores = scores - jnp.max(scores, axis=-1, keepdims=True)
            expon = jnp.exp(scores)
            weights = expon / jnp.sum(expon, axis=-1, keepdims=True)
            save(2 * p + h, weights)
            part = mm(weights.astype(BF), v2 * masks[h], NN)
            total = part if total is None else total + part
        put(p, width, total.astype(BF))


def attention_backward(mix_ref, load, d_att, masks, put):
    width = 2 * (mix_ref.shape[1] // 3 // HEADS)
    side = mix_ref.shape[1] // 3
    factor = 1.0 / math.sqrt(width // 2)
    for p in range(HEADS // 2):
        q2 = mix_ref[:, p * width : (p + 1) * width]
        k2 = mix_ref[:, side + p * width : side + (p + 1) * width]
        v2 = mix_ref[:, 2 * side + p * width : 2 * side + (p + 1) * width]
        d2 = d_att[:, p * width : (p + 1) * width]
        dq = dk = dv = None
        for h in range(2):
            dh = d2 * masks[h]
            weights = load(2 * p + h)
            grad = mm(dh, v2, NT)
            centre = jnp.sum(weights * grad, axis=-1, keepdims=True)
            ds = (weights * (grad - centre) * factor).astype(BF)
            a = mm(ds, k2 * masks[h], NN)
            b = mm(ds, q2 * masks[h], TN)
            c = mm(weights.astype(BF), dh, TN)
            dq = a if dq is None else dq + a
            dk = b if dk is None else dk + b
            dv = c if dv is None else dv + c
        put(p * width, width, dq.astype(BF))
        put(side + p * width, width, dk.astype(BF))
        put(2 * side + p * width, width, dv.astype(BF))


def inputs_gradient(c, normed, inverse, d_normed):
    inner = (
        d_normed
        - jnp.mean(d_normed, axis=-1, keepdims=True)
        - normed * jnp.mean(d_normed * normed, axis=-1, keepdims=True)
    )
    return c.astype(F32) + inverse * inner


def picker(half):
    row = lax.broadcasted_iota(jnp.int32, (256, 128), 0)
    col = lax.broadcasted_iota(jnp.int32, (256, 128), 1)
    source = (col // 8) * 16 + half * 8 + col % 8
    return (row == source).astype(F32).astype(BF)


def pick(values, chosen, out_ref, at):
    for b in range(values.shape[1] // 256):
        part = mm(values[:, 256 * b : 256 * (b + 1)], chosen, NN)
        out_ref[:, at + 128 * b : at + 128 * (b + 1)] = part.astype(BF)


class Mover:
    def __init__(self, sems):
        self.sems, self.count = sems, 0

    def start(self, source, target):
        copy = pltpu.make_async_copy(source, target, self.sems.at[self.count])
        self.count += 1
        copy.start()
        return copy


def finish(copies):
    for copy in copies:
        copy.wait()


def fill_tokens(tokens, frames, bottle):
    patches, bots = frames.shape[0], bottle.shape[0]
    rows, width = tokens.shape
    tokens[0:patches, :] = frames[...].astype(F32)
    tokens[patches:rows, :] = jnp.zeros((rows - patches, width), F32)
    tokens[patches : patches + bots, :] = bottle[...].astype(F32)


def spatial_forward_kernel(
    frames_hbm, bottle_hbm, entry_hbm, exit_hbm, grad_hbm,
    packed_hbm, mix_hbm, weights_hbm, att_hbm,
    frames, bottle, entry, exit_, tokens, packed, mix, weights_buf, att, sems,
):
    move = Mover(sems)
    patches, bots = frames.shape[0], bottle.shape[0]
    rows, width = tokens.shape
    side = exit_.shape[1]
    first = [move.start(frames_hbm, frames), move.start(bottle_hbm, bottle)]
    columns = [slice(j * side, (j + 1) * side) for j in range(3)]
    entries = [move.start(entry_hbm.at[:, c], entry.at[:, c]) for c in columns]
    later = move.start(exit_hbm, exit_)
    grads = move.start(grad_hbm, packed.at[:, width : 2 * width])
    outs = []
    finish(first)
    fill_tokens(tokens, frames, bottle)
    low = normalize(tokens[...])[0].astype(BF)
    for c, copy in zip(columns, entries):
        copy.wait()
        mix[:, c] = mm(low, entry[:, c], NN).astype(BF)
    outs.append(move.start(mix, mix_hbm))
    masks = half_masks(side // HEADS)
    keep = lax.broadcasted_iota(jnp.int32, (rows, rows), 1) < patches + bots

    def save(h, weights):
        weights_buf[h] = weights
        outs.append(move.start(weights_buf.at[h], weights_hbm.at[h]))

    def put(p, w, value):
        att[:, p * w : (p + 1) * w] = value

    attention_forward(mix, keep, masks, save, put)
    outs.append(move.start(att, att_hbm))
    later.wait()
    out = tokens[0:patches, :] + mm(att[0:patches, :], exit_[...], NT)
    packed[:, 0:width] = out.astype(BF)
    grads.wait()
    outs.append(move.start(packed, packed_hbm))
    finish(outs)


def spatial_factors_kernel(
    core_ref, frames_hbm, bottle_hbm, att_hbm, send_hbm, kept_hbm,
    frames, bottle, tokens, send, kept, sems,
):
    move = Mover(sems)
    half = kept.shape[1]
    first = [move.start(frames_hbm, frames), move.start(bottle_hbm, bottle)]
    copied = move.start(att_hbm, send.at[:, half:])
    finish(first)
    fill_tokens(tokens, frames, bottle)
    low = normalize(tokens[...])[0].astype(BF)
    core = core_ref[0]
    pick(low, picker(1 - core), send, 0)
    copied.wait()
    outs = [move.start(send, send_hbm)]
    pick(low, picker(core), kept, 0)
    outs.append(move.start(kept, kept_hbm))
    finish(outs)


def temporal_kernel(
    frames, moved_hbm, entry_hbm, exit_hbm, back_hbm, d_mix_hbm, att_hbm,
    moved, entry, exit_, back, mix, weights_buf, att, d_mix, sems,
):
    move = Mover(sems)
    rows, width = back.shape
    side = exit_.shape[1]
    seqs = rows // frames
    first = move.start(moved_hbm, moved)
    columns = [slice(j * side, (j + 1) * side) for j in range(3)]
    entries = [move.start(entry_hbm.at[:, c], entry.at[:, c]) for c in columns]
    later = move.start(exit_hbm, exit_)
    first.wait()
    normed, inverse = normalize(moved[:, 0:width].astype(F32))
    low = normed.astype(BF)
    for c, copy in zip(columns, entries):
        copy.wait()
        mix[:, c] = mm(low, entry[:, c], NN).astype(BF)
    masks = half_masks(side // HEADS)
    keep = (
        lax.broadcasted_iota(jnp.int32, (rows, rows), 0) % seqs
        == lax.broadcasted_iota(jnp.int32, (rows, rows), 1) % seqs
    )

    def save(h, weights):
        weights_buf[h] = weights

    def put(p, w, value):
        att[:, p * w : (p + 1) * w] = value

    attention_forward(mix, keep, masks, save, put)
    outs = [move.start(att, att_hbm)]
    later.wait()
    cot = moved[:, width : 2 * width]
    d_att = mm(cot, exit_[...], NN).astype(BF)

    def put_grad(at, w, value):
        d_mix[:, at : at + w] = value

    attention_backward(mix, lambda h: weights_buf[h], d_att, masks, put_grad)
    outs.append(move.start(d_mix, d_mix_hbm))
    d_normed = mm(d_mix[...], entry[...], NT)
    back[...] = inputs_gradient(cot, normed, inverse, d_normed).astype(BF)
    outs.append(move.start(back, back_hbm))
    finish(outs)


def temporal_factors_kernel(
    core_ref, moved_hbm, att_hbm, d_mix_hbm, send_hbm, kept_hbm, moved, send, kept, sems
):
    move = Mover(sems)
    width = moved.shape[1] // 2
    half, side = width // 2, att_hbm.shape[1]
    first = move.start(moved_hbm, moved)
    copied = [
        move.start(att_hbm, send.at[:, half : half + side]),
        move.start(d_mix_hbm, send.at[:, width + side : width + 4 * side]),
    ]
    first.wait()
    low = normalize(moved[:, 0:width].astype(F32))[0].astype(BF)
    cot = moved[:, width : 2 * width]
    core = core_ref[0]
    other = picker(1 - core)
    pick(low, other, send, 0)
    pick(cot, other, send, half + side)
    finish(copied)
    outs = [move.start(send, send_hbm)]
    own = picker(core)
    pick(low, own, kept, 0)
    pick(cot, own, kept, half)
    outs.append(move.start(kept, kept_hbm))
    finish(outs)


def fill_cotangent(cot, joined, frames):
    patches = cot.shape[0] - 16
    rows = joined[...].astype(F32) / frames
    padded = jnp.concatenate([rows, jnp.zeros((16 - rows.shape[0], rows.shape[1]), F32)], axis=0)
    cot[patches:, :] = padded.astype(BF)


def spatial_backward_kernel(
    frames, core_ref, back_hbm, joined_hbm, mix_hbm, weights_hbm, exit_hbm, send_hbm, kept_hbm,
    cot, joined, mix, weights_buf, exit_, send, kept, sems,
):
    move = Mover(sems)
    side, half = exit_.shape[1], kept.shape[1]
    patches = back_hbm.shape[0]
    first = [move.start(joined_hbm, joined), move.start(back_hbm, cot.at[0:patches, :])]
    first.append(move.start(exit_hbm, exit_))
    second = move.start(mix_hbm, mix)
    heads = [move.start(weights_hbm.at[h], weights_buf.at[h]) for h in range(HEADS)]
    finish(first)
    fill_cotangent(cot, joined, frames)
    c = cot[...]
    d_att = mm(c, exit_[...], NN).astype(BF)
    core = core_ref[0]
    pick(c, picker(core), kept, 0)
    outs = [move.start(kept, kept_hbm)]
    pick(c, picker(1 - core), send, 0)
    masks = half_masks(side // HEADS)
    second.wait()

    def load(h):
        heads[h].wait()
        return weights_buf[h]

    def put_grad(at, w, value):
        send[:, half + at : half + at + w] = value

    attention_backward(mix, load, d_att, masks, put_grad)
    outs.append(move.start(send, send_hbm))
    finish(outs)


def spatial_inputs_kernel(
    frames_count, frames_hbm, bottle_hbm, back_hbm, joined_hbm, send_hbm, entry_hbm,
    delta_hbm, local_hbm, frames, bottle, cot, joined, d_mix, entry, tokens, delta, local, sems,
):
    move = Mover(sems)
    patches, width = delta.shape
    half = send_hbm.shape[1] - d_mix.shape[1]
    first = [move.start(frames_hbm, frames), move.start(bottle_hbm, bottle)]
    second = [
        move.start(send_hbm.at[:, half:], d_mix),
        move.start(entry_hbm, entry),
        move.start(joined_hbm, joined),
        move.start(back_hbm, cot.at[0:patches, :]),
    ]
    finish(first)
    fill_tokens(tokens, frames, bottle)
    normed, inverse = normalize(tokens[...])
    finish(second)
    fill_cotangent(cot, joined, frames_count)
    d_normed = mm(d_mix[...], entry[...], NT)
    grads = inputs_gradient(cot[...], normed, inverse, d_normed)
    delta[...] = grads[0:patches, :].astype(BF)
    outs = [move.start(delta, delta_hbm)]
    local[...] = grads[patches : patches + local.shape[0], :]
    outs.append(move.start(local, local_hbm))
    finish(outs)


def weight_gradient_kernel(places, place_ref, *refs):
    arrays, refs = refs[: len(refs) - 10], refs[len(refs) - 10 :]
    outs_hbm, (left_n, left_c, right_m, right_a, out, sems) = refs[:4], refs[4:]
    move = Mover(sems)
    rows = left_n.shape[0] // 2
    share = out.shape[0] // 4

    def both(target, pair):
        copies = []
        for k, (index, at) in enumerate(pair):
            source = arrays[index].at[:, at : at + target.shape[1]]
            copies.append(move.start(source, target.at[k * rows : (k + 1) * rows, :]))
        return copies

    ready = [both(t, places[k]) for k, t in enumerate((left_c, right_a, left_n, right_m))]
    side = right_a.shape[1]
    core, place = place_ref[0], place_ref[1]
    where = []
    for b in range(32):
        zl, x, y = b // 16, b // 4 % 4, b % 4
        on_x = ((x + 4 - place) % 4) * 8 + y * 2 + zl
        on_y = ((y + 4 - place) % 4) * 8 + x * 2 + zl
        where.append(pl.multiple_of(jnp.where(core == 0, on_x, on_y) * 16, 16))
    outs = []

    def put(at, value):
        for b in range(32):
            out[pl.ds(where[b], 16), at : at + side] = value[b * 16 : (b + 1) * 16, :]
        columns = slice(at, at + side)
        for k in (1, 2, 3, 0):
            source = out.at[k * share : (k + 1) * share, columns]
            outs.append(move.start(source, outs_hbm[k].at[:, columns]))

    finish(ready[0] + ready[1])
    put(3 * side, mm(left_c[...], right_a[...], TN).astype(BF))
    finish(ready[2] + ready[3])
    for j in range(3):
        put(j * side, mm(left_n[...], right_m[:, j * side : (j + 1) * side], TN).astype(BF))
    finish(outs)


def add_four(parts, columns):
    total = parts[0, :, columns].astype(F32)
    for k in range(1, 4):
        total = total + parts[k, :, columns].astype(F32)
    return total.astype(BF)


def first_sum_kernel(own_hbm, a_hbm, b_hbm, c_hbm, out_hbm, parts, out, sems):
    move = Mover(sems)
    sources = (own_hbm, a_hbm, b_hbm, c_hbm)
    step = out.shape[1] // 4
    columns = [slice(j * step, (j + 1) * step) for j in range(4)]
    copies = [[move.start(r.at[:, c], parts.at[k, :, c]) for k, r in enumerate(sources)] for c in columns]
    outs = []
    for c, ready in zip(columns, copies):
        finish(ready)
        out[:, c] = add_four(parts, c)
        outs.append(move.start(out.at[:, c], out_hbm.at[:, c]))
    finish(outs)


def join_kernel(own_hbm, a_hbm, b_hbm, c_hbm, other_hbm, out_hbm, parts, out, sems):
    move = Mover(sems)
    sources = (own_hbm, a_hbm, b_hbm, c_hbm)
    width = parts.shape[2]
    step = width // 4
    columns = [slice(j * step, (j + 1) * step) for j in range(4)]
    copies = [[move.start(r.at[:, c], parts.at[k, :, c]) for k, r in enumerate(sources)] for c in columns]
    other = move.start(other_hbm, out.at[:, width:])
    outs = []
    for c, ready in zip(columns, copies):
        finish(ready)
        out[:, c] = add_four(parts, c)
        outs.append(move.start(out.at[:, c], out_hbm.at[:, c]))
    other.wait()
    outs.append(move.start(out.at[:, width:], out_hbm.at[:, width:]))
    finish(outs)


def last_sum_kernel(
    scale, parts_hbm, s_entry_hbm, s_exit_hbm, t_entry_hbm, t_exit_hbm,
    parts, s_entry, s_exit, t_entry, t_exit, sems,
):
    move = Mover(sems)
    side = s_exit.shape[1]
    columns = [slice(j * side, (j + 1) * side) for j in range(8)]
    copies = [move.start(parts_hbm.at[:, :, c], parts.at[:, :, c]) for c in columns]
    outs = []
    for j, (c, copy) in enumerate(zip(columns, copies)):
        copy.wait()
        total = (jnp.sum(parts[:, :, c].astype(F32), axis=0) * scale).astype(BF)
        entry, exit_ = ((s_entry, s_exit), (t_entry, t_exit))[j // 4]
        if j % 4 < 3:
            entry[:, (j % 4) * side : (j % 4 + 1) * side] = total
        else:
            exit_[...] = total
    for value, target in (
        (s_entry, s_entry_hbm), (s_exit, s_exit_hbm), (t_entry, t_entry_hbm), (t_exit, t_exit_hbm)
    ):
        outs.append(move.start(value, target))
    finish(outs)


HBM = pl.BlockSpec(memory_space=pltpu.HBM)
SMEM = pl.BlockSpec(memory_space=pltpu.SMEM)


def call(kernel, outs, ins, scratch, copies, flops):
    return pl.pallas_call(
        kernel,
        out_shape=tuple(jax.ShapeDtypeStruct(s, d) for s, d in outs),
        in_specs=[SMEM if a.ndim == 1 else HBM for a in ins],
        out_specs=tuple(HBM for _ in outs),
        scratch_shapes=[pltpu.VMEM(s, d) for s, d in scratch]
        + [pltpu.SemaphoreType.DMA((copies,))],
        compiler_params=pltpu.CompilerParams(vmem_limit_bytes=(64 * 1024 - 256) * 1024),
        cost_estimate=pl.CostEstimate(flops=flops, bytes_accessed=1000, transcendentals=0),
    )(*ins)


def index_of(shape, zl, x, y, zh, c):
    return (((zl * shape[1] + x) * shape[2] + y) * shape[3] + zh) * shape[4] + c


def first_pairs(shape, step):
    pairs = []
    for zl, x, y, zh, c in itertools.product(*(range(n) for n in shape)):
        to = (zl, (x + step) % shape[1], y) if c == 0 else (zl, x, (y + step) % shape[2])
        pairs.append((index_of(shape, zl, x, y, zh, c), index_of(shape, *to, zh, c)))
    return pairs


def second_groups(shape):
    zls, xs, ys, zhs = (range(n) for n in shape[:4])
    on_0 = [[index_of(shape, l, x, y, h, 0) for y in ys for l in zls for h in zhs] for x in xs]
    on_1 = [[index_of(shape, l, x, y, h, 1) for x in xs for l in zls for h in zhs] for y in ys]
    return on_0 + on_1


def per_device(
    frames_in, bottleneck, spatial_entry, spatial_exit, temporal_entry, temporal_exit,
    output_grad, joined_grad,
):
    patches, width = frames_in.shape[2], frames_in.shape[3]
    bots, side = bottleneck.shape[1], spatial_exit.shape[1]
    half = width // 2
    frames = lax.axis_size(FRAME)
    rows = patches + 16
    on = lax.axis_index("c")
    core = on.astype(jnp.int32).reshape(1)
    place = jnp.stack([on, jnp.where(on == 0, lax.axis_index("x"), lax.axis_index("y"))])
    place = place.astype(jnp.int32)
    shape = [lax.axis_size(a) for a in ALL]
    clips = lax.axis_size(("zl", "x"))
    scale = 1.0 / math.sqrt(clips * frames * patches)
    frame, bottle, joined = frames_in[0, 0], bottleneck[0], joined_grad[0]
    swap = [(0, 1), (1, 0)]

    def exchange(array):
        blocks = array.reshape(frames, patches // frames, array.shape[1])
        return lax.all_to_all(blocks, FRAME, 0, 0, tiled=True).reshape(array.shape)

    packed, mix, weights, att = call(
        spatial_forward_kernel,
        [
            ((patches, 2 * width), BF), ((rows, 3 * side), BF), ((HEADS, rows, rows), F32),
            ((rows, side), BF),
        ],
        [frame, bottle, spatial_entry, spatial_exit, output_grad[0, 0]],
        [
            ((patches, width), BF), ((bots, width), BF), ((width, 3 * side), BF),
            ((width, side), BF), ((rows, width), F32),
            ((patches, 2 * width), BF), ((rows, 3 * side), BF), ((HEADS, rows, rows), F32),
            ((rows, side), BF),
        ],
        10 + HEADS,
        1000,
    )
    moved = exchange(packed)

    send_s1, kept_sn = call(
        spatial_factors_kernel,
        [((rows, half + side), BF), ((rows, half), BF)],
        [core, frame, bottle, att],
        [
            ((patches, width), BF), ((bots, width), BF), ((rows, width), F32),
            ((rows, half + side), BF), ((rows, half), BF),
        ],
        5,
        1000,
    )
    got_s1 = lax.ppermute(send_s1, "c", swap)
    moved, got_s1 = lax.optimization_barrier((moved, got_s1))

    back, d_mix_t, att_t = call(
        functools.partial(temporal_kernel, frames),
        [((patches, width), BF), ((patches, 3 * side), BF), ((patches, side), BF)],
        [moved, temporal_entry, temporal_exit],
        [
            ((patches, 2 * width), BF), ((width, 3 * side), BF), ((width, side), BF),
            ((patches, width), BF), ((patches, 3 * side), BF), ((HEADS, patches, patches), F32),
            ((patches, side), BF), ((patches, 3 * side), BF),
        ],
        8,
        1000,
    )
    back = exchange(back)

    send_t, kept_t = call(
        temporal_factors_kernel,
        [((patches, half + side + half + 3 * side), BF), ((patches, width), BF)],
        [core, moved, att_t, d_mix_t],
        [
            ((patches, 2 * width), BF), ((patches, half + side + half + 3 * side), BF),
            ((patches, width), BF),
        ],
        5,
        1000,
    )
    got_t = lax.ppermute(send_t, "c", swap)

    def weight_gradient(count, places, arrays):
        parts = call(
            functools.partial(weight_gradient_kernel, places),
            [((half // 4, 4 * side), BF)] * 4,
            [place] + arrays,
            [
                ((2 * count, half), BF), ((2 * count, half), BF), ((2 * count, 3 * side), BF),
                ((2 * count, side), BF), ((half, 4 * side), BF),
            ],
            24,
            1000,
        )
        return parts

    def passed_on(parts):
        return [parts[0]] + [
            lax.ppermute(parts[k], ALL, first_pairs(shape, k)) for k in range(1, 4)
        ]

    cot_at, mix_at = half + side, half + side + half
    parts_t = weight_gradient(
        patches,
        (
            ((0, half), (2, cot_at)), ((1, half), (2, half)),
            ((0, 0), (2, 0)), ((1, mix_at), (2, mix_at)),
        ),
        [kept_t, send_t, got_t],
    )
    back, *parts_t = lax.optimization_barrier((back, *parts_t))
    parts_t = passed_on(parts_t)
    share = (half // 4, 4 * side)
    (sum_t,) = call(
        first_sum_kernel, [(share, BF)], parts_t, [((4, *share), BF), (share, BF)], 20, 1000
    )

    send_s2, kept_sc = call(
        functools.partial(spatial_backward_kernel, frames),
        [((rows, half + 3 * side), BF), ((rows, half), BF)],
        [core, back, joined, mix, weights, spatial_exit],
        [
            ((rows, width), BF), ((bots, width), BF), ((rows, 3 * side), BF),
            ((HEADS, rows, rows), F32), ((width, side), BF), ((rows, half + 3 * side), BF),
            ((rows, half), BF),
        ],
        6 + HEADS,
        1000,
    )
    got_s2 = lax.ppermute(send_s2, "c", swap)
    parts_s = weight_gradient(
        rows,
        (
            ((3, 0), (5, 0)), ((1, half), (2, half)),
            ((0, 0), (2, 0)), ((4, half), (5, half)),
        ),
        [kept_sn, send_s1, got_s1, kept_sc, send_s2, got_s2],
    )
    after, *parts_s = lax.optimization_barrier((send_s2, *parts_s))
    parts_s = passed_on(parts_s)
    delta, local = call(
        functools.partial(spatial_inputs_kernel, frames),
        [((patches, width), BF), ((bots, width), F32)],
        [frame, bottle, back, joined, after, spatial_entry],
        [
            ((patches, width), BF), ((bots, width), BF), ((rows, width), BF), ((bots, width), BF),
            ((rows, 3 * side), BF), ((width, 3 * side), BF), ((rows, width), F32),
            ((patches, width), BF), ((bots, width), F32),
        ],
        8,
        1000,
    )

    def with_partner(local, axis, bit):
        pairs = [(i, i ^ bit) for i in range(lax.axis_size(axis))]
        return local + lax.ppermute(local, axis, pairs)

    local = with_partner(with_partner(local, "c", 1), "zh", 1)
    local, *parts_s = lax.optimization_barrier((local, *parts_s))
    local = with_partner(with_partner(local, "y", 1), "y", 2)
    (both,) = call(
        join_kernel,
        [((half // 4, 8 * side), BF)],
        parts_s + [sum_t],
        [((4, *share), BF), ((half // 4, 8 * side), BF)],
        22,
        1000,
    )
    groups = second_groups(shape)
    count = len(groups[0])
    last = lax.all_to_all(
        both.reshape(count, -1, 8 * side), ALL, 0, 0, axis_index_groups=groups, tiled=True
    )

    own = last.shape[1]
    s_entry, s_exit, t_entry, t_exit = call(
        functools.partial(last_sum_kernel, scale),
        [((own, 3 * side), BF), ((own, side), BF)] * 2,
        [last],
        [
            (last.shape, BF),
            ((own, 3 * side), BF), ((own, side), BF), ((own, 3 * side), BF), ((own, side), BF),
        ],
        12,
        1000,
    )
    return (
        delta[None, None], local.astype(BF)[None], s_entry, s_exit, t_entry, t_exit
    )


def solution(mesh):
    finer = Mesh(mesh.devices.reshape(2, mesh.shape["dp"] // 2, 4, 2, 2), ALL)
    dp = ("zl", "x")
    row = P(ALL, None)
    clip = P(dp, None, None)
    patch = P(dp, FRAME, None, None)
    return jax.shard_map(
        per_device,
        mesh=finer,
        in_specs=(patch, clip, P(), P(), P(), P(), patch, clip),
        out_specs=(patch, clip, row, row, row, row),
        check_vma=False,
    )
```

```python
import functools
import itertools
import math

import jax
import jax.numpy as jnp
from jax import lax
from jax.experimental import pallas as pl
from jax.experimental.pallas import tpu as pltpu
from jax.sharding import Mesh
from jax.sharding import PartitionSpec as P

HEADS = 8
EPSILON = 1e-05
FRAME = ("y", "zh", "c")
ALL = ("zl", "x", "y", "zh", "c")
BF = jnp.bfloat16
F32 = jnp.float32

NN = (((1,), (0,)), ((), ()))
NT = (((1,), (1,)), ((), ()))
TN = (((0,), (0,)), ((), ()))


def mm(a, b, dims):
    return lax.dot_general(a, b, dims, preferred_element_type=F32)


def normalize(u):
    centred = u - jnp.mean(u, axis=-1, keepdims=True)
    inverse = lax.rsqrt(jnp.mean(centred * centred, axis=-1, keepdims=True) + EPSILON)
    return centred * inverse, inverse


def half_masks(size):
    lane = lax.broadcasted_iota(jnp.int32, (1, 2 * size), 1)
    low = (lane < size).astype(F32)
    return low.astype(BF), (1.0 - low).astype(BF)


def attention_forward(mix_ref, keep, masks, save, put):
    width = 2 * (mix_ref.shape[1] // 3 // HEADS)
    side = mix_ref.shape[1] // 3
    factor = 1.0 / math.sqrt(width // 2)
    for p in range(HEADS // 2):
        q2 = mix_ref[:, p * width : (p + 1) * width]
        k2 = mix_ref[:, side + p * width : side + (p + 1) * width]
        v2 = mix_ref[:, 2 * side + p * width : 2 * side + (p + 1) * width]
        total = None
        for h in range(2):
            scores = mm(k2 * masks[h], q2, NT) * factor
            scores = jnp.where(keep, scores, -jnp.inf)
            expon = jnp.exp(scores - jnp.max(scores, axis=0, keepdims=True))
            weights = expon * (1.0 / jnp.sum(expon, axis=0, keepdims=True))
            save(2 * p + h, weights)
            part = mm(weights.astype(BF), v2 * masks[h], TN)
            total = part if total is None else total + part
        put(p, width, total.astype(BF))


def attention_backward(mix_ref, load, d_att, masks, put):
    width = 2 * (mix_ref.shape[1] // 3 // HEADS)
    side = mix_ref.shape[1] // 3
    factor = 1.0 / math.sqrt(width // 2)
    for p in range(HEADS // 2):
        q2 = mix_ref[:, p * width : (p + 1) * width]
        k2 = mix_ref[:, side + p * width : side + (p + 1) * width]
        v2 = mix_ref[:, 2 * side + p * width : 2 * side + (p + 1) * width]
        d2 = d_att[:, p * width : (p + 1) * width]
        dq = dk = dv = None
        for h in range(2):
            dh = d2 * masks[h]
            weights = load(2 * p + h)
            grad = mm(v2, dh, NT)
            centre = jnp.sum(weights * grad, axis=0, keepdims=True)
            ds = (weights * (grad - centre) * factor).astype(BF)
            a = mm(ds, k2 * masks[h], TN)
            b = mm(ds, q2 * masks[h], NN)
            c = mm(weights.astype(BF), dh, NN)
            dq = a if dq is None else dq + a
            dk = b if dk is None else dk + b
            dv = c if dv is None else dv + c
        put(p * width, width, dq.astype(BF))
        put(side + p * width, width, dk.astype(BF))
        put(2 * side + p * width, width, dv.astype(BF))


def inputs_gradient(c, normed, inverse, d_normed):
    inner = (
        d_normed
        - jnp.mean(d_normed, axis=-1, keepdims=True)
        - normed * jnp.mean(d_normed * normed, axis=-1, keepdims=True)
    )
    return c.astype(F32) + inverse * inner


def picker(half):
    row = lax.broadcasted_iota(jnp.int32, (256, 128), 0)
    col = lax.broadcasted_iota(jnp.int32, (256, 128), 1)
    source = (col // 8) * 16 + half * 8 + col % 8
    return (row == source).astype(F32).astype(BF)


def pick(values, chosen, out_ref, at):
    for b in range(values.shape[1] // 256):
        part = mm(values[:, 256 * b : 256 * (b + 1)], chosen, NN)
        out_ref[:, at + 128 * b : at + 128 * (b + 1)] = part.astype(BF)


class Mover:
    def __init__(self, sems):
        self.sems, self.count = sems, 0

    def start(self, source, target):
        copy = pltpu.make_async_copy(source, target, self.sems.at[self.count])
        self.count += 1
        copy.start()
        return copy


def finish(copies):
    for copy in copies:
        copy.wait()


def fill_tokens(tokens, frames, bottle):
    patches, bots = frames.shape[0], bottle.shape[0]
    rows, width = tokens.shape
    tokens[0:patches, :] = frames[...].astype(F32)
    tokens[patches:rows, :] = jnp.zeros((rows - patches, width), F32)
    tokens[patches : patches + bots, :] = bottle[...].astype(F32)


def spatial_forward_kernel(
    frames_hbm, bottle_hbm, entry_hbm, exit_hbm, grad_hbm,
    packed_hbm, mix_hbm, weights_hbm, att_hbm,
    frames, bottle, entry, exit_, tokens, packed, mix, weights_buf, att, sems,
):
    move = Mover(sems)
    patches, bots = frames.shape[0], bottle.shape[0]
    rows, width = tokens.shape
    side = exit_.shape[1]
    first = [move.start(frames_hbm, frames), move.start(bottle_hbm, bottle)]
    columns = [slice(j * side, (j + 1) * side) for j in range(3)]
    entries = [move.start(entry_hbm.at[:, c], entry.at[:, c]) for c in columns]
    later = move.start(exit_hbm, exit_)
    grads = move.start(grad_hbm, packed.at[:, width : 2 * width])
    outs = []
    finish(first)
    fill_tokens(tokens, frames, bottle)
    low = normalize(tokens[...])[0].astype(BF)
    for c, copy in zip(columns, entries):
        copy.wait()
        mix[:, c] = mm(low, entry[:, c], NN).astype(BF)
    outs.append(move.start(mix, mix_hbm))
    masks = half_masks(side // HEADS)
    keep = lax.broadcasted_iota(jnp.int32, (rows, rows), 0) < patches + bots

    def save(h, weights):
        weights_buf[h] = weights
        outs.append(move.start(weights_buf.at[h], weights_hbm.at[h]))

    def put(p, w, value):
        att[:, p * w : (p + 1) * w] = value

    attention_forward(mix, keep, masks, save, put)
    outs.append(move.start(att, att_hbm))
    later.wait()
    out = tokens[0:patches, :] + mm(att[0:patches, :], exit_[...], NT)
    packed[:, 0:width] = out.astype(BF)
    grads.wait()
    outs.append(move.start(packed, packed_hbm))
    finish(outs)


def spatial_factors_kernel(
    core_ref, frames_hbm, bottle_hbm, att_hbm, send_hbm, kept_hbm,
    frames, bottle, tokens, send, kept, sems,
):
    move = Mover(sems)
    half = kept.shape[1]
    first = [move.start(frames_hbm, frames), move.start(bottle_hbm, bottle)]
    copied = move.start(att_hbm, send.at[:, half:])
    finish(first)
    fill_tokens(tokens, frames, bottle)
    low = normalize(tokens[...])[0].astype(BF)
    core = core_ref[0]
    pick(low, picker(1 - core), send, 0)
    copied.wait()
    outs = [move.start(send, send_hbm)]
    pick(low, picker(core), kept, 0)
    outs.append(move.start(kept, kept_hbm))
    finish(outs)


def temporal_kernel(
    frames, core_ref, moved_hbm, entry_hbm, exit_hbm, back_hbm, send_hbm, kept_hbm,
    moved, entry, exit_, back, mix, weights_buf, send, kept, sems,
):
    move = Mover(sems)
    rows, width = back.shape
    half, side = width // 2, exit_.shape[1]
    seqs = rows // frames
    first = move.start(moved_hbm, moved)
    columns = [slice(j * side, (j + 1) * side) for j in range(3)]
    entries = [move.start(entry_hbm.at[:, c], entry.at[:, c]) for c in columns]
    later = move.start(exit_hbm, exit_)
    core = core_ref[0]
    other, own = picker(1 - core), picker(core)
    first.wait()
    cot = moved[:, width : 2 * width]
    normed, inverse = normalize(moved[:, 0:width].astype(F32))
    low = normed.astype(BF)
    pick(cot, other, send, half + side)
    pick(cot, own, kept, half)
    for c, copy in zip(columns, entries):
        copy.wait()
        mix[:, c] = mm(low, entry[:, c], NN).astype(BF)
    pick(low, other, send, 0)
    pick(low, own, kept, 0)
    outs = [move.start(kept, kept_hbm)]
    masks = half_masks(side // HEADS)
    keep = (
        lax.broadcasted_iota(jnp.int32, (rows, rows), 0) % seqs
        == lax.broadcasted_iota(jnp.int32, (rows, rows), 1) % seqs
    )

    def save(h, weights):
        weights_buf[h] = weights

    def put(p, w, value):
        send[:, half + p * w : half + (p + 1) * w] = value

    attention_forward(mix, keep, masks, save, put)
    later.wait()
    d_att = mm(cot, exit_[...], NN).astype(BF)
    at_mix = width + side

    def put_grad(at, w, value):
        send[:, at_mix + at : at_mix + at + w] = value

    attention_backward(mix, lambda h: weights_buf[h], d_att, masks, put_grad)
    outs.append(move.start(send, send_hbm))
    d_normed = mm(send[:, at_mix:], entry[...], NT)
    back[...] = inputs_gradient(cot, normed, inverse, d_normed).astype(BF)
    outs.append(move.start(back, back_hbm))
    finish(outs)


def fill_cotangent(cot, joined, frames):
    patches = cot.shape[0] - 16
    rows = joined[...].astype(F32) / frames
    padded = jnp.concatenate([rows, jnp.zeros((16 - rows.shape[0], rows.shape[1]), F32)], axis=0)
    cot[patches:, :] = padded.astype(BF)


def spatial_backward_kernel(
    frames, core_ref, back_hbm, joined_hbm, mix_hbm, weights_hbm, exit_hbm, send_hbm, kept_hbm,
    cot, joined, mix, weights_buf, exit_, send, kept, sems,
):
    move = Mover(sems)
    side, half = exit_.shape[1], kept.shape[1]
    patches = back_hbm.shape[0]
    first = [move.start(joined_hbm, joined), move.start(back_hbm, cot.at[0:patches, :])]
    first.append(move.start(exit_hbm, exit_))
    second = move.start(mix_hbm, mix)
    heads = [move.start(weights_hbm.at[h], weights_buf.at[h]) for h in range(HEADS)]
    finish(first)
    fill_cotangent(cot, joined, frames)
    c = cot[...]
    d_att = mm(c, exit_[...], NN).astype(BF)
    core = core_ref[0]
    pick(c, picker(core), kept, 0)
    outs = [move.start(kept, kept_hbm)]
    pick(c, picker(1 - core), send, 0)
    masks = half_masks(side // HEADS)
    second.wait()

    def load(h):
        heads[h].wait()
        return weights_buf[h]

    def put_grad(at, w, value):
        send[:, half + at : half + at + w] = value

    attention_backward(mix, load, d_att, masks, put_grad)
    outs.append(move.start(send, send_hbm))
    finish(outs)


def spatial_inputs_kernel(
    frames_count, frames_hbm, bottle_hbm, back_hbm, joined_hbm, send_hbm, entry_hbm,
    delta_hbm, local_hbm, frames, bottle, cot, joined, d_mix, entry, tokens, delta, local, sems,
):
    move = Mover(sems)
    patches, width = delta.shape
    half = send_hbm.shape[1] - d_mix.shape[1]
    first = [move.start(frames_hbm, frames), move.start(bottle_hbm, bottle)]
    second = [
        move.start(send_hbm.at[:, half:], d_mix),
        move.start(entry_hbm, entry),
        move.start(joined_hbm, joined),
        move.start(back_hbm, cot.at[0:patches, :]),
    ]
    finish(first)
    fill_tokens(tokens, frames, bottle)
    normed, inverse = normalize(tokens[...])
    finish(second)
    fill_cotangent(cot, joined, frames_count)
    d_normed = mm(d_mix[...], entry[...], NT)
    grads = inputs_gradient(cot[...], normed, inverse, d_normed)
    delta[...] = grads[0:patches, :].astype(BF)
    outs = [move.start(delta, delta_hbm)]
    local[...] = grads[patches : patches + local.shape[0], :]
    outs.append(move.start(local, local_hbm))
    finish(outs)


def weight_gradient_kernel(places, place_ref, *refs):
    arrays, refs = refs[: len(refs) - 10], refs[len(refs) - 10 :]
    outs_hbm, (left_n, left_c, right_m, right_a, out, sems) = refs[:4], refs[4:]
    move = Mover(sems)
    rows = left_n.shape[0] // 2
    share = out.shape[0] // 4

    def both(target, pair):
        copies = []
        for k, (index, at) in enumerate(pair):
            source = arrays[index].at[:, at : at + target.shape[1]]
            copies.append(move.start(source, target.at[k * rows : (k + 1) * rows, :]))
        return copies

    ready = [both(t, places[k]) for k, t in enumerate((left_c, right_a, left_n, right_m))]
    side = right_a.shape[1]
    core, place = place_ref[0], place_ref[1]
    where = []
    for b in range(32):
        zl, x, y = b // 16, b // 4 % 4, b % 4
        on_x = ((x + 4 - place) % 4) * 8 + y * 2 + zl
        on_y = ((y + 4 - place) % 4) * 8 + x * 2 + zl
        where.append(pl.multiple_of(jnp.where(core == 0, on_x, on_y) * 16, 16))
    outs = []

    def put(at, value):
        for b in range(32):
            out[pl.ds(where[b], 16), at : at + side] = value[b * 16 : (b + 1) * 16, :]
        columns = slice(at, at + side)
        for k in (1, 2, 3, 0):
            source = out.at[k * share : (k + 1) * share, columns]
            outs.append(move.start(source, outs_hbm[k].at[:, columns]))

    finish(ready[0] + ready[1])
    put(3 * side, mm(left_c[...], right_a[...], TN).astype(BF))
    finish(ready[2] + ready[3])
    for j in range(3):
        put(j * side, mm(left_n[...], right_m[:, j * side : (j + 1) * side], TN).astype(BF))
    finish(outs)


def add_four(parts, columns):
    total = parts[0, :, columns].astype(F32)
    for k in range(1, 4):
        total = total + parts[k, :, columns].astype(F32)
    return total.astype(BF)


def first_sum_kernel(own_hbm, a_hbm, b_hbm, c_hbm, out_hbm, parts, out, sems):
    move = Mover(sems)
    sources = (own_hbm, a_hbm, b_hbm, c_hbm)
    step = out.shape[1] // 4
    columns = [slice(j * step, (j + 1) * step) for j in range(4)]
    copies = [[move.start(r.at[:, c], parts.at[k, :, c]) for k, r in enumerate(sources)] for c in columns]
    outs = []
    for c, ready in zip(columns, copies):
        finish(ready)
        out[:, c] = add_four(parts, c)
        outs.append(move.start(out.at[:, c], out_hbm.at[:, c]))
    finish(outs)


def join_kernel(
    own_hbm, a_hbm, b_hbm, c_hbm, other_hbm, local_hbm, out_hbm, parts, out, local, twice, sems
):
    move = Mover(sems)
    sources = (own_hbm, a_hbm, b_hbm, c_hbm)
    width = parts.shape[2]
    step = width // 4
    columns = [slice(j * step, (j + 1) * step) for j in range(4)]
    bottle = move.start(local_hbm, local)
    other = move.start(other_hbm, out.at[:, width : 2 * width])
    copies = [[move.start(r.at[:, c], parts.at[k, :, c]) for k, r in enumerate(sources)] for c in columns]
    bottle.wait()
    bots, half = local.shape[0], twice.shape[1]
    for k in range(16 // bots):
        twice[k * bots : (k + 1) * bots, :] = local[:, k % 2 * half : (k % 2 + 1) * half]
    rows = twice[...].astype(BF)
    for k in range(out.shape[0] // 16):
        out[16 * k : 16 * (k + 1), 2 * width :] = rows
    outs = [move.start(out.at[:, 2 * width :], out_hbm.at[:, 2 * width :])]
    other.wait()
    outs.append(move.start(out.at[:, width : 2 * width], out_hbm.at[:, width : 2 * width]))
    for c, ready in zip(columns, copies):
        finish(ready)
        out[:, c] = add_four(parts, c)
        outs.append(move.start(out.at[:, c], out_hbm.at[:, c]))
    finish(outs)


def last_sum_kernel(
    scale, place_ref, parts_hbm, bottle_hbm, s_entry_hbm, s_exit_hbm, t_entry_hbm, t_exit_hbm,
    parts, rows, bottle, s_entry, s_exit, t_entry, t_exit, sems,
):
    move = Mover(sems)
    side = s_exit.shape[1]
    first = move.start(parts_hbm.at[:, :, 8 * side :], rows)
    columns = [slice(j * side, (j + 1) * side) for j in range(8)]
    copies = [move.start(parts_hbm.at[:, :, c], parts.at[:, :, c]) for c in columns]
    outs = []
    first.wait()
    zl = place_ref[2]
    total = jnp.zeros(bottle.shape, F32)
    for k in range(rows.shape[0] // 2):
        total = total + rows[(k // 2) * 4 + zl * 2 + k % 2].astype(F32)
    bottle[...] = total.astype(BF)
    outs.append(move.start(bottle, bottle_hbm))
    for j, (c, copy) in enumerate(zip(columns, copies)):
        copy.wait()
        total = (jnp.sum(parts[:, :, c].astype(F32), axis=0) * scale).astype(BF)
        entry, exit_ = ((s_entry, s_exit), (t_entry, t_exit))[j // 4]
        if j % 4 < 3:
            entry[:, (j % 4) * side : (j % 4 + 1) * side] = total
        else:
            exit_[...] = total
    for value, target in (
        (s_entry, s_entry_hbm), (s_exit, s_exit_hbm), (t_entry, t_entry_hbm), (t_exit, t_exit_hbm)
    ):
        outs.append(move.start(value, target))
    finish(outs)


HBM = pl.BlockSpec(memory_space=pltpu.HBM)
SMEM = pl.BlockSpec(memory_space=pltpu.SMEM)


def call(kernel, outs, ins, scratch, copies, flops):
    return pl.pallas_call(
        kernel,
        out_shape=tuple(jax.ShapeDtypeStruct(s, d) for s, d in outs),
        in_specs=[SMEM if a.ndim == 1 else HBM for a in ins],
        out_specs=tuple(HBM for _ in outs),
        scratch_shapes=[pltpu.VMEM(s, d) for s, d in scratch]
        + [pltpu.SemaphoreType.DMA((copies,))],
        compiler_params=pltpu.CompilerParams(vmem_limit_bytes=(64 * 1024 - 256) * 1024),
        cost_estimate=pl.CostEstimate(flops=flops, bytes_accessed=1000, transcendentals=0),
    )(*ins)


def index_of(shape, zl, x, y, zh, c):
    return (((zl * shape[1] + x) * shape[2] + y) * shape[3] + zh) * shape[4] + c


def first_pairs(shape, step):
    pairs = []
    for zl, x, y, zh, c in itertools.product(*(range(n) for n in shape)):
        to = (zl, (x + step) % shape[1], y) if c == 0 else (zl, x, (y + step) % shape[2])
        pairs.append((index_of(shape, zl, x, y, zh, c), index_of(shape, *to, zh, c)))
    return pairs


def second_groups(shape):
    zls, xs, ys, zhs = (range(n) for n in shape[:4])
    on_0 = [[index_of(shape, l, x, y, h, 0) for y in ys for l in zls for h in zhs] for x in xs]
    on_1 = [[index_of(shape, l, x, y, h, 1) for x in xs for l in zls for h in zhs] for y in ys]
    return on_0 + on_1


def per_device(
    frames_in, bottleneck, spatial_entry, spatial_exit, temporal_entry, temporal_exit,
    output_grad, joined_grad,
):
    patches, width = frames_in.shape[2], frames_in.shape[3]
    bots, side = bottleneck.shape[1], spatial_exit.shape[1]
    half = width // 2
    frames = lax.axis_size(FRAME)
    rows = patches + 16
    on = lax.axis_index("c")
    core = on.astype(jnp.int32).reshape(1)
    first = jnp.where(on == 0, lax.axis_index("x"), lax.axis_index("y"))
    place = jnp.stack([on, first, lax.axis_index("zl")])
    place = place.astype(jnp.int32)
    shape = [lax.axis_size(a) for a in ALL]
    clips = lax.axis_size(("zl", "x"))
    scale = 1.0 / math.sqrt(clips * frames * patches)
    frame, bottle, joined = frames_in[0, 0], bottleneck[0], joined_grad[0]
    swap = [(0, 1), (1, 0)]

    def exchange(array):
        blocks = array.reshape(frames, patches // frames, array.shape[1])
        return lax.all_to_all(blocks, FRAME, 0, 0, tiled=True).reshape(array.shape)

    packed, mix, weights, att = call(
        spatial_forward_kernel,
        [
            ((patches, 2 * width), BF), ((rows, 3 * side), BF), ((HEADS, rows, rows), F32),
            ((rows, side), BF),
        ],
        [frame, bottle, spatial_entry, spatial_exit, output_grad[0, 0]],
        [
            ((patches, width), BF), ((bots, width), BF), ((width, 3 * side), BF),
            ((width, side), BF), ((rows, width), F32),
            ((patches, 2 * width), BF), ((rows, 3 * side), BF), ((HEADS, rows, rows), F32),
            ((rows, side), BF),
        ],
        10 + HEADS,
        1000,
    )
    moved = exchange(packed)

    send_s1, kept_sn = call(
        spatial_factors_kernel,
        [((rows, half + side), BF), ((rows, half), BF)],
        [core, frame, bottle, att],
        [
            ((patches, width), BF), ((bots, width), BF), ((rows, width), F32),
            ((rows, half + side), BF), ((rows, half), BF),
        ],
        5,
        1000,
    )
    got_s1 = lax.ppermute(send_s1, "c", swap)
    moved, got_s1 = lax.optimization_barrier((moved, got_s1))

    factors = half + side + half + 3 * side
    back, send_t, kept_t = call(
        functools.partial(temporal_kernel, frames),
        [((patches, width), BF), ((patches, factors), BF), ((patches, width), BF)],
        [core, moved, temporal_entry, temporal_exit],
        [
            ((patches, 2 * width), BF), ((width, 3 * side), BF), ((width, side), BF),
            ((patches, width), BF), ((patches, 3 * side), BF), ((HEADS, patches, patches), F32),
            ((patches, factors), BF), ((patches, width), BF),
        ],
        8,
        1000,
    )
    back = exchange(back)

    got_t = lax.ppermute(send_t, "c", swap)

    def weight_gradient(count, places, arrays):
        parts = call(
            functools.partial(weight_gradient_kernel, places),
            [((half // 4, 4 * side), BF)] * 4,
            [place] + arrays,
            [
                ((2 * count, half), BF), ((2 * count, half), BF), ((2 * count, 3 * side), BF),
                ((2 * count, side), BF), ((half, 4 * side), BF),
            ],
            24,
            1000,
        )
        return parts

    def passed_on(parts):
        return [parts[0]] + [
            lax.ppermute(parts[k], ALL, first_pairs(shape, k)) for k in range(1, 4)
        ]

    cot_at, mix_at = half + side, half + side + half
    parts_t = weight_gradient(
        patches,
        (
            ((0, half), (2, cot_at)), ((1, half), (2, half)),
            ((0, 0), (2, 0)), ((1, mix_at), (2, mix_at)),
        ),
        [kept_t, send_t, got_t],
    )
    parts_t = passed_on(parts_t)
    back, parts_t[0] = lax.optimization_barrier((back, parts_t[0]))
    share = (half // 4, 4 * side)
    (sum_t,) = call(
        first_sum_kernel, [(share, BF)], parts_t, [((4, *share), BF), (share, BF)], 20, 1000
    )

    send_s2, kept_sc = call(
        functools.partial(spatial_backward_kernel, frames),
        [((rows, half + 3 * side), BF), ((rows, half), BF)],
        [core, back, joined, mix, weights, spatial_exit],
        [
            ((rows, width), BF), ((bots, width), BF), ((rows, 3 * side), BF),
            ((HEADS, rows, rows), F32), ((width, side), BF), ((rows, half + 3 * side), BF),
            ((rows, half), BF),
        ],
        6 + HEADS,
        1000,
    )
    got_s2 = lax.ppermute(send_s2, "c", swap)
    parts_s = weight_gradient(
        rows,
        (
            ((3, 0), (5, 0)), ((1, half), (2, half)),
            ((0, 0), (2, 0)), ((4, half), (5, half)),
        ),
        [kept_sn, send_s1, got_s1, kept_sc, send_s2, got_s2],
    )
    after, sum_t, stays = lax.optimization_barrier((send_s2, sum_t, parts_s[0]))
    parts_s = (stays, *parts_s[1:])
    parts_s = passed_on(parts_s)
    delta, local = call(
        functools.partial(spatial_inputs_kernel, frames),
        [((patches, width), BF), ((bots, width), F32)],
        [frame, bottle, back, joined, after, spatial_entry],
        [
            ((patches, width), BF), ((bots, width), BF), ((rows, width), BF), ((bots, width), BF),
            ((rows, 3 * side), BF), ((width, 3 * side), BF), ((rows, width), F32),
            ((patches, width), BF), ((bots, width), F32),
        ],
        8,
        1000,
    )

    def with_partner(local, axis, bit):
        pairs = [(i, i ^ bit) for i in range(lax.axis_size(axis))]
        return local + lax.ppermute(local, axis, pairs)

    local = with_partner(local, "c", 1)
    wide = 8 * side + width // 2
    (both,) = call(
        join_kernel,
        [((half // 4, wide), BF)],
        parts_s + [sum_t, local],
        [
            ((4, *share), BF), ((half // 4, wide), BF), ((bots, width), F32),
            ((16, width // 2), F32),
        ],
        24,
        1000,
    )
    groups = second_groups(shape)
    count = len(groups[0])
    last = lax.all_to_all(
        both.reshape(count, -1, wide), ALL, 0, 0, axis_index_groups=groups, tiled=True
    )
    halves = (2 * bots, width // 2)
    own = last.shape[1]
    total, s_entry, s_exit, t_entry, t_exit = call(
        functools.partial(last_sum_kernel, scale),
        [(halves, BF)] + [((own, 3 * side), BF), ((own, side), BF)] * 2,
        [place, last],
        [
            ((count, own, 8 * side), BF), ((count, *halves), BF), (halves, BF),
            ((own, 3 * side), BF), ((own, side), BF), ((own, 3 * side), BF), ((own, side), BF),
        ],
        14,
        1000,
    )
    total = jnp.where(on == 0, total, lax.ppermute(total, "c", [(0, 1)]))
    local = jnp.concatenate([total[:bots], total[bots:]], axis=1)
    return (
        delta[None, None], local[None], s_entry, s_exit, t_entry, t_exit
    )


def solution(mesh):
    finer = Mesh(mesh.devices.reshape(2, mesh.shape["dp"] // 2, 4, 2, 2), ALL)
    dp = ("zl", "x")
    row = P(ALL, None)
    clip = P(dp, None, None)
    patch = P(dp, FRAME, None, None)
    return jax.shard_map(
        per_device,
        mesh=finer,
        in_specs=(patch, clip, P(), P(), P(), P(), patch, clip),
        out_specs=(patch, clip, row, row, row, row),
        check_vma=False,
    )
```

```python
import functools
import itertools
import math

import jax
import jax.numpy as jnp
from jax import lax
from jax.experimental import pallas as pl
from jax.experimental.pallas import tpu as pltpu
from jax.sharding import Mesh
from jax.sharding import PartitionSpec as P

HEADS = 8
EPSILON = 1e-05
FRAME = ("y", "zh", "c")
ALL = ("zl", "x", "y", "zh", "c")
BF = jnp.bfloat16
F32 = jnp.float32

NN = (((1,), (0,)), ((), ()))
NT = (((1,), (1,)), ((), ()))
TN = (((0,), (0,)), ((), ()))


def mm(a, b, dims):
    return lax.dot_general(a, b, dims, preferred_element_type=F32)


def normalize(u):
    centred = u - jnp.mean(u, axis=-1, keepdims=True)
    inverse = lax.rsqrt(jnp.mean(centred * centred, axis=-1, keepdims=True) + EPSILON)
    return centred * inverse, inverse


def half_masks(size):
    lane = lax.broadcasted_iota(jnp.int32, (1, 2 * size), 1)
    low = (lane < size).astype(F32)
    return low.astype(BF), (1.0 - low).astype(BF)


def attention_forward(mix_ref, keep, masks, save, put):
    width = 2 * (mix_ref.shape[1] // 3 // HEADS)
    side = mix_ref.shape[1] // 3
    factor = 1.0 / math.sqrt(width // 2)
    for p in range(HEADS // 2):
        q2 = mix_ref[:, p * width : (p + 1) * width]
        k2 = mix_ref[:, side + p * width : side + (p + 1) * width]
        v2 = mix_ref[:, 2 * side + p * width : 2 * side + (p + 1) * width]
        total = None
        for h in range(2):
            scores = mm(k2 * masks[h], q2, NT) * factor
            scores = jnp.where(keep, scores, -jnp.inf)
            expon = jnp.exp(scores - jnp.max(scores, axis=0, keepdims=True))
            weights = expon * (1.0 / jnp.sum(expon, axis=0, keepdims=True))
            save(2 * p + h, weights)
            part = mm(weights.astype(BF), v2 * masks[h], TN)
            total = part if total is None else total + part
        put(p, width, total.astype(BF))


def attention_backward(mix_ref, load, d_att, masks, put):
    width = 2 * (mix_ref.shape[1] // 3 // HEADS)
    side = mix_ref.shape[1] // 3
    factor = 1.0 / math.sqrt(width // 2)
    for p in range(HEADS // 2):
        q2 = mix_ref[:, p * width : (p + 1) * width]
        k2 = mix_ref[:, side + p * width : side + (p + 1) * width]
        v2 = mix_ref[:, 2 * side + p * width : 2 * side + (p + 1) * width]
        d2 = d_att[:, p * width : (p + 1) * width]
        dq = dk = dv = None
        for h in range(2):
            dh = d2 * masks[h]
            weights = load(2 * p + h)
            grad = mm(v2, dh, NT)
            centre = jnp.sum(weights * grad, axis=0, keepdims=True)
            ds = (weights * (grad - centre) * factor).astype(BF)
            a = mm(ds, k2 * masks[h], TN)
            b = mm(ds, q2 * masks[h], NN)
            c = mm(weights.astype(BF), dh, NN)
            dq = a if dq is None else dq + a
            dk = b if dk is None else dk + b
            dv = c if dv is None else dv + c
        put(p * width, width, dq.astype(BF))
        put(side + p * width, width, dk.astype(BF))
        put(2 * side + p * width, width, dv.astype(BF))


def inputs_gradient(c, normed, inverse, d_normed):
    inner = (
        d_normed
        - jnp.mean(d_normed, axis=-1, keepdims=True)
        - normed * jnp.mean(d_normed * normed, axis=-1, keepdims=True)
    )
    return c.astype(F32) + inverse * inner


def picker(half):
    row = lax.broadcasted_iota(jnp.int32, (256, 128), 0)
    col = lax.broadcasted_iota(jnp.int32, (256, 128), 1)
    source = (col // 8) * 16 + half * 8 + col % 8
    return (row == source).astype(F32).astype(BF)


def pick(values, chosen, out_ref, at):
    for b in range(values.shape[1] // 256):
        part = mm(values[:, 256 * b : 256 * (b + 1)], chosen, NN)
        out_ref[:, at + 128 * b : at + 128 * (b + 1)] = part.astype(BF)


class Mover:
    def __init__(self, sems):
        self.sems, self.count = sems, 0

    def start(self, source, target):
        copy = pltpu.make_async_copy(source, target, self.sems.at[self.count])
        self.count += 1
        copy.start()
        return copy


def finish(copies):
    for copy in copies:
        copy.wait()


def fill_tokens(tokens, frames, bottle):
    patches, bots = frames.shape[0], bottle.shape[0]
    rows, width = tokens.shape
    tokens[0:patches, :] = frames[...].astype(F32)
    tokens[patches:rows, :] = jnp.zeros((rows - patches, width), F32)
    tokens[patches : patches + bots, :] = bottle[...].astype(F32)


def spatial_forward_kernel(
    frames_hbm, bottle_hbm, entry_hbm, exit_hbm, grad_hbm,
    packed_hbm, mix_hbm, weights_hbm, att_hbm,
    frames, bottle, entry, exit_, tokens, packed, mix, weights_buf, att, sems,
):
    move = Mover(sems)
    patches, bots = frames.shape[0], bottle.shape[0]
    rows, width = tokens.shape
    side = exit_.shape[1]
    first = [move.start(frames_hbm, frames), move.start(bottle_hbm, bottle)]
    columns = [slice(j * side, (j + 1) * side) for j in range(3)]
    entries = [move.start(entry_hbm.at[:, c], entry.at[:, c]) for c in columns]
    later = move.start(exit_hbm, exit_)
    grads = move.start(grad_hbm, packed.at[:, width : 2 * width])
    outs = []
    finish(first)
    fill_tokens(tokens, frames, bottle)
    low = normalize(tokens[...])[0].astype(BF)
    for c, copy in zip(columns, entries):
        copy.wait()
        mix[:, c] = mm(low, entry[:, c], NN).astype(BF)
    outs.append(move.start(mix, mix_hbm))
    masks = half_masks(side // HEADS)
    keep = lax.broadcasted_iota(jnp.int32, (rows, rows), 0) < patches + bots

    def save(h, weights):
        weights_buf[h] = weights
        outs.append(move.start(weights_buf.at[h], weights_hbm.at[h]))

    def put(p, w, value):
        att[:, p * w : (p + 1) * w] = value

    attention_forward(mix, keep, masks, save, put)
    outs.append(move.start(att, att_hbm))
    later.wait()
    out = tokens[0:patches, :] + mm(att[0:patches, :], exit_[...], NT)
    packed[:, 0:width] = out.astype(BF)
    grads.wait()
    outs.append(move.start(packed, packed_hbm))
    finish(outs)


def spatial_factors_kernel(
    core_ref, frames_hbm, bottle_hbm, att_hbm, send_hbm, kept_hbm,
    frames, bottle, tokens, send, kept, sems,
):
    move = Mover(sems)
    half = kept.shape[1]
    first = [move.start(frames_hbm, frames), move.start(bottle_hbm, bottle)]
    copied = move.start(att_hbm, send.at[:, half:])
    finish(first)
    fill_tokens(tokens, frames, bottle)
    low = normalize(tokens[...])[0].astype(BF)
    core = core_ref[0]
    pick(low, picker(1 - core), send, 0)
    copied.wait()
    outs = [move.start(send, send_hbm)]
    pick(low, picker(core), kept, 0)
    outs.append(move.start(kept, kept_hbm))
    finish(outs)


def temporal_kernel(
    frames, core_ref, moved_hbm, entry_hbm, exit_hbm, back_hbm, send_hbm, kept_hbm,
    moved, entry, exit_, back, mix, weights_buf, send, kept, sems,
):
    move = Mover(sems)
    rows, width = back.shape
    half, side = width // 2, exit_.shape[1]
    seqs = rows // frames
    first = move.start(moved_hbm, moved)
    columns = [slice(j * side, (j + 1) * side) for j in range(3)]
    entries = [move.start(entry_hbm.at[:, c], entry.at[:, c]) for c in columns]
    later = move.start(exit_hbm, exit_)
    core = core_ref[0]
    other, own = picker(1 - core), picker(core)
    first.wait()
    cot = moved[:, width : 2 * width]
    normed, inverse = normalize(moved[:, 0:width].astype(F32))
    low = normed.astype(BF)
    pick(cot, other, send, half + side)
    pick(cot, own, kept, half)
    for c, copy in zip(columns, entries):
        copy.wait()
        mix[:, c] = mm(low, entry[:, c], NN).astype(BF)
    pick(low, other, send, 0)
    pick(low, own, kept, 0)
    outs = [move.start(kept, kept_hbm)]
    masks = half_masks(side // HEADS)
    keep = (
        lax.broadcasted_iota(jnp.int32, (rows, rows), 0) % seqs
        == lax.broadcasted_iota(jnp.int32, (rows, rows), 1) % seqs
    )

    def save(h, weights):
        weights_buf[h] = weights

    def put(p, w, value):
        send[:, half + p * w : half + (p + 1) * w] = value

    attention_forward(mix, keep, masks, save, put)
    later.wait()
    d_att = mm(cot, exit_[...], NN).astype(BF)
    at_mix = width + side

    def put_grad(at, w, value):
        send[:, at_mix + at : at_mix + at + w] = value

    attention_backward(mix, lambda h: weights_buf[h], d_att, masks, put_grad)
    outs.append(move.start(send, send_hbm))
    d_normed = mm(send[:, at_mix:], entry[...], NT)
    back[...] = inputs_gradient(cot, normed, inverse, d_normed).astype(BF)
    outs.append(move.start(back, back_hbm))
    finish(outs)


def fill_cotangent(cot, joined, frames):
    patches = cot.shape[0] - 16
    rows = joined[...].astype(F32) / frames
    padded = jnp.concatenate([rows, jnp.zeros((16 - rows.shape[0], rows.shape[1]), F32)], axis=0)
    cot[patches:, :] = padded.astype(BF)


def spatial_backward_kernel(
    frames, core_ref, back_hbm, joined_hbm, mix_hbm, weights_hbm, exit_hbm,
    picked_hbm, kept_hbm, d_mix_hbm,
    cot, joined, mix, weights_buf, exit_, picked, kept, d_mix, sems,
):
    move = Mover(sems)
    side = exit_.shape[1]
    patches = back_hbm.shape[0]
    first = [move.start(joined_hbm, joined), move.start(back_hbm, cot.at[0:patches, :])]
    first.append(move.start(exit_hbm, exit_))
    second = move.start(mix_hbm, mix)
    heads = [move.start(weights_hbm.at[h], weights_buf.at[h]) for h in range(HEADS)]
    finish(first)
    fill_cotangent(cot, joined, frames)
    c = cot[...]
    d_att = mm(c, exit_[...], NN).astype(BF)
    core = core_ref[0]
    pick(c, picker(core), kept, 0)
    outs = [move.start(kept, kept_hbm)]
    pick(c, picker(1 - core), picked, 0)
    outs.append(move.start(picked, picked_hbm))
    masks = half_masks(side // HEADS)
    second.wait()

    def load(h):
        heads[h].wait()
        return weights_buf[h]

    def put_grad(at, w, value):
        d_mix[:, at : at + w] = value

    attention_backward(mix, load, d_att, masks, put_grad)
    outs.append(move.start(d_mix, d_mix_hbm))
    finish(outs)


def bottle_inputs_kernel(
    frames_count, bottle_hbm, joined_hbm, d_mix_hbm, entry_hbm, local_hbm,
    bottle, joined, d_mix, entry, tokens, local, sems,
):
    move = Mover(sems)
    bots = bottle.shape[0]
    second = [
        move.start(entry_hbm, entry),
        move.start(d_mix_hbm.at[d_mix_hbm.shape[0] - 16 :, :], d_mix),
    ]
    first = [move.start(bottle_hbm, bottle), move.start(joined_hbm, joined)]
    finish(first)
    tokens[...] = jnp.zeros(tokens.shape, F32)
    tokens[0:bots, :] = bottle[...].astype(F32)
    normed, inverse = normalize(tokens[...])
    c = (joined[...].astype(F32) / frames_count).astype(BF)
    finish(second)
    d_normed = mm(d_mix[...], entry[...], NT)
    grads = inputs_gradient(c, normed[0:bots], inverse[0:bots], d_normed[0:bots])
    local[...] = grads
    move.start(local, local_hbm).wait()


def patch_inputs_kernel(
    frames_hbm, back_hbm, d_mix_hbm, entry_hbm, delta_hbm,
    frames, cot, d_mix, entry, delta, sems,
):
    move = Mover(sems)
    first = move.start(frames_hbm, frames)
    second = [
        move.start(d_mix_hbm.at[0 : d_mix.shape[0], :], d_mix),
        move.start(entry_hbm, entry),
        move.start(back_hbm, cot),
    ]
    first.wait()
    normed, inverse = normalize(frames[...].astype(F32))
    finish(second)
    d_normed = mm(d_mix[...], entry[...], NT)
    delta[...] = inputs_gradient(cot[...], normed, inverse, d_normed).astype(BF)
    move.start(delta, delta_hbm).wait()


def weight_gradient_kernel(places, place_ref, *refs):
    arrays, refs = refs[: len(refs) - 10], refs[len(refs) - 10 :]
    outs_hbm, (left_n, left_c, right_m, right_a, out, sems) = refs[:4], refs[4:]
    move = Mover(sems)
    rows = left_n.shape[0] // 2
    share = out.shape[0] // 4

    def both(target, pair):
        copies = []
        for k, (index, at) in enumerate(pair):
            source = arrays[index].at[:, at : at + target.shape[1]]
            copies.append(move.start(source, target.at[k * rows : (k + 1) * rows, :]))
        return copies

    ready = [both(t, places[k]) for k, t in enumerate((left_c, right_a, left_n, right_m))]
    side = right_a.shape[1]
    core, place = place_ref[0], place_ref[1]
    where = []
    for b in range(32):
        zl, x, y = b // 16, b // 4 % 4, b % 4
        on_x = ((x + 4 - place) % 4) * 8 + y * 2 + zl
        on_y = ((y + 4 - place) % 4) * 8 + x * 2 + zl
        where.append(pl.multiple_of(jnp.where(core == 0, on_x, on_y) * 16, 16))
    outs = []

    def put(at, value):
        for b in range(32):
            out[pl.ds(where[b], 16), at : at + side] = value[b * 16 : (b + 1) * 16, :]
        columns = slice(at, at + side)
        for k in (1, 2, 3, 0):
            source = out.at[k * share : (k + 1) * share, columns]
            outs.append(move.start(source, outs_hbm[k].at[:, columns]))

    finish(ready[0] + ready[1])
    put(3 * side, mm(left_c[...], right_a[...], TN).astype(BF))
    finish(ready[2] + ready[3])
    product = mm(left_n[...], right_m[...], TN).astype(BF)
    for j in range(3):
        put(j * side, product[:, j * side : (j + 1) * side])
    finish(outs)


def add_four(parts, columns):
    total = parts[0, :, columns].astype(F32)
    for k in range(1, 4):
        total = total + parts[k, :, columns].astype(F32)
    return total.astype(BF)


def first_sum_kernel(own_hbm, a_hbm, b_hbm, c_hbm, out_hbm, parts, out, sems):
    move = Mover(sems)
    sources = (own_hbm, a_hbm, b_hbm, c_hbm)
    step = out.shape[1] // 4
    columns = [slice(j * step, (j + 1) * step) for j in range(4)]
    copies = [[move.start(r.at[:, c], parts.at[k, :, c]) for k, r in enumerate(sources)] for c in columns]
    outs = []
    for c, ready in zip(columns, copies):
        finish(ready)
        out[:, c] = add_four(parts, c)
        outs.append(move.start(out.at[:, c], out_hbm.at[:, c]))
    finish(outs)


def join_kernel(own_hbm, a_hbm, b_hbm, c_hbm, other_hbm, out_hbm, parts, out, sems):
    move = Mover(sems)
    sources = (own_hbm, a_hbm, b_hbm, c_hbm)
    width = parts.shape[2]
    step = width // 4
    columns = [slice(j * step, (j + 1) * step) for j in range(4)]
    copies = [[move.start(r.at[:, c], parts.at[k, :, c]) for k, r in enumerate(sources)] for c in columns]
    other = move.start(other_hbm, out.at[:, width:])
    outs = []
    for c, ready in zip(columns, copies):
        finish(ready)
        out[:, c] = add_four(parts, c)
        outs.append(move.start(out.at[:, c], out_hbm.at[:, c]))
    other.wait()
    outs.append(move.start(out.at[:, width:], out_hbm.at[:, width:]))
    finish(outs)


def last_sum_kernel(
    scale, parts_hbm, s_entry_hbm, s_exit_hbm, t_entry_hbm, t_exit_hbm,
    parts, s_entry, s_exit, t_entry, t_exit, sems,
):
    move = Mover(sems)
    side = s_exit.shape[1]
    columns = [slice(j * side, (j + 1) * side) for j in range(8)]
    copies = [move.start(parts_hbm.at[:, :, c], parts.at[:, :, c]) for c in columns]
    outs = []
    for j, (c, copy) in enumerate(zip(columns, copies)):
        copy.wait()
        total = (jnp.sum(parts[:, :, c].astype(F32), axis=0) * scale).astype(BF)
        entry, exit_ = ((s_entry, s_exit), (t_entry, t_exit))[j // 4]
        if j % 4 < 3:
            entry[:, (j % 4) * side : (j % 4 + 1) * side] = total
        else:
            exit_[...] = total
    for value, target in (
        (s_entry, s_entry_hbm), (s_exit, s_exit_hbm), (t_entry, t_entry_hbm), (t_exit, t_exit_hbm)
    ):
        outs.append(move.start(value, target))
    finish(outs)


HBM = pl.BlockSpec(memory_space=pltpu.HBM)
SMEM = pl.BlockSpec(memory_space=pltpu.SMEM)


def call(kernel, outs, ins, scratch, copies, flops):
    return pl.pallas_call(
        kernel,
        out_shape=tuple(jax.ShapeDtypeStruct(s, d) for s, d in outs),
        in_specs=[SMEM if a.ndim == 1 else HBM for a in ins],
        out_specs=tuple(HBM for _ in outs),
        scratch_shapes=[pltpu.VMEM(s, d) for s, d in scratch]
        + [pltpu.SemaphoreType.DMA((copies,))],
        compiler_params=pltpu.CompilerParams(vmem_limit_bytes=(64 * 1024 - 128) * 1024),
        cost_estimate=pl.CostEstimate(flops=flops, bytes_accessed=1000, transcendentals=0),
    )(*ins)


def index_of(shape, zl, x, y, zh, c):
    return (((zl * shape[1] + x) * shape[2] + y) * shape[3] + zh) * shape[4] + c


def first_pairs(shape, step):
    pairs = []
    for zl, x, y, zh, c in itertools.product(*(range(n) for n in shape)):
        to = (zl, (x + step) % shape[1], y) if c == 0 else (zl, x, (y + step) % shape[2])
        pairs.append((index_of(shape, zl, x, y, zh, c), index_of(shape, *to, zh, c)))
    return pairs


def second_groups(shape):
    zls, xs, ys, zhs = (range(n) for n in shape[:4])
    on_0 = [[index_of(shape, l, x, y, h, 0) for y in ys for l in zls for h in zhs] for x in xs]
    on_1 = [[index_of(shape, l, x, y, h, 1) for x in xs for l in zls for h in zhs] for y in ys]
    return on_0 + on_1


def per_device(
    frames_in, bottleneck, spatial_entry, spatial_exit, temporal_entry, temporal_exit,
    output_grad, joined_grad,
):
    patches, width = frames_in.shape[2], frames_in.shape[3]
    bots, side = bottleneck.shape[1], spatial_exit.shape[1]
    half = width // 2
    frames = lax.axis_size(FRAME)
    rows = patches + 16
    on = lax.axis_index("c")
    core = on.astype(jnp.int32).reshape(1)
    first = jnp.where(on == 0, lax.axis_index("x"), lax.axis_index("y"))
    place = jnp.stack([on, first])
    place = place.astype(jnp.int32)
    shape = [lax.axis_size(a) for a in ALL]
    clips = lax.axis_size(("zl", "x"))
    scale = 1.0 / math.sqrt(clips * frames * patches)
    frame, bottle, joined = frames_in[0, 0], bottleneck[0], joined_grad[0]
    swap = [(0, 1), (1, 0)]

    def exchange(array):
        blocks = array.reshape(frames, patches // frames, array.shape[1])
        return lax.all_to_all(blocks, FRAME, 0, 0, tiled=True).reshape(array.shape)

    packed, mix, weights, att = call(
        spatial_forward_kernel,
        [
            ((patches, 2 * width), BF), ((rows, 3 * side), BF), ((HEADS, rows, rows), F32),
            ((rows, side), BF),
        ],
        [frame, bottle, spatial_entry, spatial_exit, output_grad[0, 0]],
        [
            ((patches, width), BF), ((bots, width), BF), ((width, 3 * side), BF),
            ((width, side), BF), ((rows, width), F32),
            ((patches, 2 * width), BF), ((rows, 3 * side), BF), ((HEADS, rows, rows), F32),
            ((rows, side), BF),
        ],
        10 + HEADS,
        1000,
    )
    moved = exchange(packed)

    send_s1, kept_sn = call(
        spatial_factors_kernel,
        [((rows, half + side), BF), ((rows, half), BF)],
        [core, frame, bottle, att],
        [
            ((patches, width), BF), ((bots, width), BF), ((rows, width), F32),
            ((rows, half + side), BF), ((rows, half), BF),
        ],
        5,
        1000,
    )
    got_s1 = lax.ppermute(send_s1, "c", swap)
    moved, got_s1 = lax.optimization_barrier((moved, got_s1))

    factors = half + side + half + 3 * side
    back, send_t, kept_t = call(
        functools.partial(temporal_kernel, frames),
        [((patches, width), BF), ((patches, factors), BF), ((patches, width), BF)],
        [core, moved, temporal_entry, temporal_exit],
        [
            ((patches, 2 * width), BF), ((width, 3 * side), BF), ((width, side), BF),
            ((patches, width), BF), ((patches, 3 * side), BF), ((HEADS, patches, patches), F32),
            ((patches, factors), BF), ((patches, width), BF),
        ],
        8,
        1000,
    )
    back = exchange(back)

    got_t = lax.ppermute(send_t, "c", swap)

    def weight_gradient(count, places, arrays):
        parts = call(
            functools.partial(weight_gradient_kernel, places),
            [((half // 4, 4 * side), BF)] * 4,
            [place] + arrays,
            [
                ((2 * count, half), BF), ((2 * count, half), BF), ((2 * count, 3 * side), BF),
                ((2 * count, side), BF), ((half, 4 * side), BF),
            ],
            24,
            1000,
        )
        return parts

    def passed_on(parts):
        return [parts[0]] + [
            lax.ppermute(parts[k], ALL, first_pairs(shape, k)) for k in range(1, 4)
        ]

    cot_at, mix_at = half + side, half + side + half
    parts_t = weight_gradient(
        patches,
        (
            ((0, half), (2, cot_at)), ((1, half), (2, half)),
            ((0, 0), (2, 0)), ((1, mix_at), (2, mix_at)),
        ),
        [kept_t, send_t, got_t],
    )
    parts_t = passed_on(parts_t)
    back, parts_t[0] = lax.optimization_barrier((back, parts_t[0]))
    share = (half // 4, 4 * side)
    send_sc, kept_sc, d_mix_s = call(
        functools.partial(spatial_backward_kernel, frames),
        [((rows, half), BF), ((rows, half), BF), ((rows, 3 * side), BF)],
        [core, back, joined, mix, weights, spatial_exit],
        [
            ((rows, width), BF), ((bots, width), BF), ((rows, 3 * side), BF),
            ((HEADS, rows, rows), F32), ((width, side), BF), ((rows, half), BF),
            ((rows, half), BF), ((rows, 3 * side), BF),
        ],
        7 + HEADS,
        1000,
    )
    got_sc = lax.ppermute(send_sc, "c", swap)
    got_sm = lax.ppermute(d_mix_s, "c", swap)
    parts_s = weight_gradient(
        rows,
        (
            ((3, 0), (4, 0)), ((1, half), (2, half)),
            ((0, 0), (2, 0)), ((5, 0), (6, 0)),
        ),
        [kept_sn, send_s1, got_s1, kept_sc, got_sc, d_mix_s, got_sm],
    )
    tied = lax.optimization_barrier((d_mix_s, *parts_s, *parts_t))
    after, parts_s, parts_t = tied[0], tied[1:5], list(tied[5:])
    parts_s = passed_on(parts_s)
    (local,) = call(
        functools.partial(bottle_inputs_kernel, frames),
        [((bots, width), F32)],
        [bottle, joined, after, spatial_entry],
        [
            ((bots, width), BF), ((bots, width), BF), ((16, 3 * side), BF),
            ((width, 3 * side), BF), ((16, width), F32), ((bots, width), F32),
        ],
        5,
        1000,
    )

    def with_partner(local, axis, bit):
        pairs = [(i, i ^ bit) for i in range(lax.axis_size(axis))]
        return local + lax.ppermute(local, axis, pairs)

    local = with_partner(local, "zh", 1)
    local, after, *parts_s = lax.optimization_barrier((local, after, *parts_s))
    (delta,) = call(
        patch_inputs_kernel,
        [((patches, width), BF)],
        [frame, back, after, spatial_entry],
        [
            ((patches, width), BF), ((patches, width), BF), ((patches, 3 * side), BF),
            ((width, 3 * side), BF), ((patches, width), BF),
        ],
        5,
        1000,
    )
    local = with_partner(with_partner(local, "c", 1), "y", 1)
    local, delta = lax.optimization_barrier((local, delta))
    local = with_partner(local, "y", 2)
    (sum_t,) = call(
        first_sum_kernel, [(share, BF)], parts_t, [((4, *share), BF), (share, BF)], 20, 1000
    )

    (both,) = call(
        join_kernel,
        [((half // 4, 8 * side), BF)],
        parts_s + [sum_t],
        [((4, *share), BF), ((half // 4, 8 * side), BF)],
        22,
        1000,
    )
    groups = second_groups(shape)
    count = len(groups[0])
    last = lax.all_to_all(
        both.reshape(count, -1, 8 * side), ALL, 0, 0, axis_index_groups=groups, tiled=True
    )

    own = last.shape[1]
    s_entry, s_exit, t_entry, t_exit = call(
        functools.partial(last_sum_kernel, scale),
        [((own, 3 * side), BF), ((own, side), BF)] * 2,
        [last],
        [
            (last.shape, BF),
            ((own, 3 * side), BF), ((own, side), BF), ((own, 3 * side), BF), ((own, side), BF),
        ],
        12,
        1000,
    )
    return (
        delta[None, None], local.astype(BF)[None], s_entry, s_exit, t_entry, t_exit
    )


def solution(mesh):
    finer = Mesh(mesh.devices.reshape(2, mesh.shape["dp"] // 2, 4, 2, 2), ALL)
    dp = ("zl", "x")
    row = P(ALL, None)
    clip = P(dp, None, None)
    patch = P(dp, FRAME, None, None)
    return jax.shard_map(
        per_device,
        mesh=finer,
        in_specs=(patch, clip, P(), P(), P(), P(), patch, clip),
        out_specs=(patch, clip, row, row, row, row),
        check_vma=False,
    )
```

```python
import functools
import itertools
import math

import jax
import jax.numpy as jnp
from jax import lax
from jax.experimental import pallas as pl
from jax.experimental.pallas import tpu as pltpu
from jax.sharding import Mesh
from jax.sharding import PartitionSpec as P

HEADS = 8
EPSILON = 1e-05
FRAME = ("y", "zh", "c")
ALL = ("zl", "x", "y", "zh", "c")
BF = jnp.bfloat16
F32 = jnp.float32

NN = (((1,), (0,)), ((), ()))
NT = (((1,), (1,)), ((), ()))
TN = (((0,), (0,)), ((), ()))


def mm(a, b, dims):
    return lax.dot_general(a, b, dims, preferred_element_type=F32)


def normalize(u):
    centred = u - jnp.mean(u, axis=-1, keepdims=True)
    inverse = lax.rsqrt(jnp.mean(centred * centred, axis=-1, keepdims=True) + EPSILON)
    return centred * inverse, inverse


def half_masks(size):
    lane = lax.broadcasted_iota(jnp.int32, (1, 2 * size), 1)
    low = (lane < size).astype(F32)
    return low.astype(BF), (1.0 - low).astype(BF)


def attention_forward(mix_ref, keep, masks, save, put):
    width = 2 * (mix_ref.shape[1] // 3 // HEADS)
    side = mix_ref.shape[1] // 3
    factor = 1.0 / math.sqrt(width // 2)
    for p in range(HEADS // 2):
        q2 = mix_ref[:, p * width : (p + 1) * width]
        k2 = mix_ref[:, side + p * width : side + (p + 1) * width]
        v2 = mix_ref[:, 2 * side + p * width : 2 * side + (p + 1) * width]
        total = None
        for h in range(2):
            scores = mm(k2 * masks[h], q2, NT) * factor
            scores = jnp.where(keep, scores, -jnp.inf)
            expon = jnp.exp(scores - jnp.max(scores, axis=0, keepdims=True))
            weights = expon * (1.0 / jnp.sum(expon, axis=0, keepdims=True))
            save(2 * p + h, weights)
            part = mm(weights.astype(BF), v2 * masks[h], TN)
            total = part if total is None else total + part
        put(p, width, total.astype(BF))


def attention_backward(mix_ref, load, d_att, masks, put):
    width = 2 * (mix_ref.shape[1] // 3 // HEADS)
    side = mix_ref.shape[1] // 3
    factor = 1.0 / math.sqrt(width // 2)
    for p in range(HEADS // 2):
        q2 = mix_ref[:, p * width : (p + 1) * width]
        k2 = mix_ref[:, side + p * width : side + (p + 1) * width]
        v2 = mix_ref[:, 2 * side + p * width : 2 * side + (p + 1) * width]
        d2 = d_att[:, p * width : (p + 1) * width]
        dq = dk = dv = None
        for h in range(2):
            dh = d2 * masks[h]
            weights = load(2 * p + h)
            grad = mm(v2, dh, NT)
            centre = jnp.sum(weights * grad, axis=0, keepdims=True)
            ds = (weights * (grad - centre) * factor).astype(BF)
            a = mm(ds, k2 * masks[h], TN)
            b = mm(ds, q2 * masks[h], NN)
            c = mm(weights.astype(BF), dh, NN)
            dq = a if dq is None else dq + a
            dk = b if dk is None else dk + b
            dv = c if dv is None else dv + c
        put(p * width, width, dq.astype(BF))
        put(side + p * width, width, dk.astype(BF))
        put(2 * side + p * width, width, dv.astype(BF))


def inputs_gradient(c, normed, inverse, d_normed):
    inner = (
        d_normed
        - jnp.mean(d_normed, axis=-1, keepdims=True)
        - normed * jnp.mean(d_normed * normed, axis=-1, keepdims=True)
    )
    return c.astype(F32) + inverse * inner


def picker(half):
    row = lax.broadcasted_iota(jnp.int32, (256, 128), 0)
    col = lax.broadcasted_iota(jnp.int32, (256, 128), 1)
    source = (col // 8) * 16 + half * 8 + col % 8
    return (row == source).astype(F32).astype(BF)


def pick(values, chosen, out_ref, at):
    for b in range(values.shape[1] // 256):
        part = mm(values[:, 256 * b : 256 * (b + 1)], chosen, NN)
        out_ref[:, at + 128 * b : at + 128 * (b + 1)] = part.astype(BF)


class Mover:
    def __init__(self, sems):
        self.sems, self.count = sems, 0

    def start(self, source, target):
        copy = pltpu.make_async_copy(source, target, self.sems.at[self.count])
        self.count += 1
        copy.start()
        return copy

    def spread(self, source, target, count=2):
        step = source.shape[0] // count
        rows = [slice(k * step, (k + 1) * step) for k in range(count)]
        return [self.start(source.at[r, :], target.at[r, :]) for r in rows]


def finish(copies):
    for copy in copies:
        copy.wait()


def fill_tokens(tokens, frames, bottle):
    patches, bots = frames.shape[0], bottle.shape[0]
    rows, width = tokens.shape
    tokens[0:patches, :] = frames[...].astype(F32)
    tokens[patches:rows, :] = jnp.zeros((rows - patches, width), F32)
    tokens[patches : patches + bots, :] = bottle[...].astype(F32)


def spatial_forward_kernel(
    frames_hbm, bottle_hbm, entry_hbm, exit_hbm, grad_hbm,
    packed_hbm, mix_hbm, weights_hbm, att_hbm,
    frames, bottle, entry, exit_, tokens, packed, mix, weights_buf, att, sems,
):
    move = Mover(sems)
    patches, bots = frames.shape[0], bottle.shape[0]
    rows, width = tokens.shape
    side = exit_.shape[1]
    first = [move.start(frames_hbm, frames), move.start(bottle_hbm, bottle)]
    columns = [slice(j * side, (j + 1) * side) for j in range(3)]
    entries = [move.spread(entry_hbm.at[:, c], entry.at[:, c]) for c in columns]
    later = move.spread(exit_hbm, exit_)
    grads = move.start(grad_hbm, packed.at[:, width : 2 * width])
    outs = []
    finish(first)
    fill_tokens(tokens, frames, bottle)
    low = normalize(tokens[...])[0].astype(BF)
    for c, copy in zip(columns, entries):
        finish(copy)
        mix[:, c] = mm(low, entry[:, c], NN).astype(BF)
    outs.append(move.start(mix, mix_hbm))
    masks = half_masks(side // HEADS)
    keep = lax.broadcasted_iota(jnp.int32, (rows, rows), 0) < patches + bots

    def save(h, weights):
        weights_buf[h] = weights
        outs.append(move.start(weights_buf.at[h], weights_hbm.at[h]))

    def put(p, w, value):
        att[:, p * w : (p + 1) * w] = value

    attention_forward(mix, keep, masks, save, put)
    outs.append(move.start(att, att_hbm))
    finish(later)
    out = tokens[0:patches, :] + mm(att[0:patches, :], exit_[...], NT)
    packed[:, 0:width] = out.astype(BF)
    grads.wait()
    outs.append(move.start(packed, packed_hbm))
    finish(outs)


def spatial_factors_kernel(
    core_ref, frames_hbm, bottle_hbm, att_hbm, send_hbm, kept_hbm,
    frames, bottle, tokens, send, kept, sems,
):
    move = Mover(sems)
    half = kept.shape[1]
    first = [move.start(frames_hbm, frames), move.start(bottle_hbm, bottle)]
    copied = move.start(att_hbm, send.at[:, half:])
    finish(first)
    fill_tokens(tokens, frames, bottle)
    low = normalize(tokens[...])[0].astype(BF)
    core = core_ref[0]
    pick(low, picker(1 - core), send, 0)
    copied.wait()
    outs = [move.start(send, send_hbm)]
    pick(low, picker(core), kept, 0)
    outs.append(move.start(kept, kept_hbm))
    finish(outs)


def temporal_kernel(
    frames, core_ref, moved_hbm, entry_hbm, exit_hbm, back_hbm, send_hbm, kept_hbm,
    moved, entry, exit_, back, mix, weights_buf, send, kept, sems,
):
    move = Mover(sems)
    rows, width = back.shape
    half, side = width // 2, exit_.shape[1]
    seqs = rows // frames
    first = move.start(moved_hbm, moved)
    columns = [slice(j * side, (j + 1) * side) for j in range(3)]
    entries = [move.spread(entry_hbm.at[:, c], entry.at[:, c]) for c in columns]
    later = move.spread(exit_hbm, exit_)
    core = core_ref[0]
    other, own = picker(1 - core), picker(core)
    first.wait()
    cot = moved[:, width : 2 * width]
    normed, inverse = normalize(moved[:, 0:width].astype(F32))
    low = normed.astype(BF)
    pick(cot, other, send, half + side)
    pick(cot, own, kept, half)
    for c, copy in zip(columns, entries):
        finish(copy)
        mix[:, c] = mm(low, entry[:, c], NN).astype(BF)
    pick(low, other, send, 0)
    pick(low, own, kept, 0)
    outs = [move.start(kept, kept_hbm)]
    masks = half_masks(side // HEADS)
    keep = (
        lax.broadcasted_iota(jnp.int32, (rows, rows), 0) % seqs
        == lax.broadcasted_iota(jnp.int32, (rows, rows), 1) % seqs
    )

    def save(h, weights):
        weights_buf[h] = weights

    def put(p, w, value):
        send[:, half + p * w : half + (p + 1) * w] = value

    attention_forward(mix, keep, masks, save, put)
    finish(later)
    d_att = mm(cot, exit_[...], NN).astype(BF)
    at_mix = width + side

    def put_grad(at, w, value):
        send[:, at_mix + at : at_mix + at + w] = value

    attention_backward(mix, lambda h: weights_buf[h], d_att, masks, put_grad)
    outs.append(move.start(send, send_hbm))
    d_normed = mm(send[:, at_mix:], entry[...], NT)
    back[...] = inputs_gradient(cot, normed, inverse, d_normed).astype(BF)
    outs.append(move.start(back, back_hbm))
    finish(outs)


def fill_cotangent(cot, joined, frames):
    patches = cot.shape[0] - 16
    rows = joined[...].astype(F32) / frames
    padded = jnp.concatenate([rows, jnp.zeros((16 - rows.shape[0], rows.shape[1]), F32)], axis=0)
    cot[patches:, :] = padded.astype(BF)


def spatial_backward_kernel(
    frames, core_ref, back_hbm, joined_hbm, mix_hbm, weights_hbm, exit_hbm,
    picked_hbm, kept_hbm, d_mix_hbm,
    cot, joined, mix, weights_buf, exit_, picked, kept, d_mix, sems,
):
    move = Mover(sems)
    side = exit_.shape[1]
    patches = back_hbm.shape[0]
    first = [move.start(joined_hbm, joined), move.start(back_hbm, cot.at[0:patches, :])]
    first += move.spread(exit_hbm, exit_)
    second = move.start(mix_hbm, mix)
    heads = [move.start(weights_hbm.at[h], weights_buf.at[h]) for h in range(HEADS)]
    finish(first)
    fill_cotangent(cot, joined, frames)
    c = cot[...]
    d_att = mm(c, exit_[...], NN).astype(BF)
    core = core_ref[0]
    pick(c, picker(core), kept, 0)
    outs = [move.start(kept, kept_hbm)]
    pick(c, picker(1 - core), picked, 0)
    outs.append(move.start(picked, picked_hbm))
    masks = half_masks(side // HEADS)
    second.wait()

    def load(h):
        heads[h].wait()
        return weights_buf[h]

    def put_grad(at, w, value):
        d_mix[:, at : at + w] = value

    attention_backward(mix, load, d_att, masks, put_grad)
    outs.append(move.start(d_mix, d_mix_hbm))
    finish(outs)


def bottle_inputs_kernel(
    frames_count, bottle_hbm, joined_hbm, d_mix_hbm, entry_hbm, local_hbm,
    bottle, joined, d_mix, entry, tokens, local, sems,
):
    move = Mover(sems)
    bots = bottle.shape[0]
    second = move.spread(entry_hbm, entry, 4)
    second.append(move.start(d_mix_hbm.at[d_mix_hbm.shape[0] - 16 :, :], d_mix))
    first = [move.start(bottle_hbm, bottle), move.start(joined_hbm, joined)]
    finish(first)
    tokens[...] = jnp.zeros(tokens.shape, F32)
    tokens[0:bots, :] = bottle[...].astype(F32)
    normed, inverse = normalize(tokens[...])
    c = (joined[...].astype(F32) / frames_count).astype(BF)
    finish(second)
    d_normed = mm(d_mix[...], entry[...], NT)
    grads = inputs_gradient(c, normed[0:bots], inverse[0:bots], d_normed[0:bots])
    local[...] = grads
    move.start(local, local_hbm).wait()


def patch_inputs_kernel(
    frames_hbm, back_hbm, d_mix_hbm, entry_hbm, delta_hbm,
    frames, cot, d_mix, entry, delta, sems,
):
    move = Mover(sems)
    first = move.start(frames_hbm, frames)
    second = [
        move.start(d_mix_hbm.at[0 : d_mix.shape[0], :], d_mix),
        move.start(back_hbm, cot),
        *move.spread(entry_hbm, entry, 4),
    ]
    first.wait()
    normed, inverse = normalize(frames[...].astype(F32))
    finish(second)
    d_normed = mm(d_mix[...], entry[...], NT)
    delta[...] = inputs_gradient(cot[...], normed, inverse, d_normed).astype(BF)
    move.start(delta, delta_hbm).wait()


def weight_gradient_kernel(places, place_ref, *refs):
    arrays, refs = refs[: len(refs) - 10], refs[len(refs) - 10 :]
    outs_hbm, (left_n, left_c, right_m, right_a, out, sems) = refs[:4], refs[4:]
    move = Mover(sems)
    rows = left_n.shape[0] // 2
    share = out.shape[0] // 4

    def both(target, pair):
        copies = []
        for k, (index, at) in enumerate(pair):
            source = arrays[index].at[:, at : at + target.shape[1]]
            copies.append(move.start(source, target.at[k * rows : (k + 1) * rows, :]))
        return copies

    ready = [both(t, places[k]) for k, t in enumerate((left_c, right_a, left_n, right_m))]
    side = right_a.shape[1]
    core, place = place_ref[0], place_ref[1]
    where = []
    for b in range(32):
        zl, x, y = b // 16, b // 4 % 4, b % 4
        on_x = ((x + 4 - place) % 4) * 8 + y * 2 + zl
        on_y = ((y + 4 - place) % 4) * 8 + x * 2 + zl
        where.append(pl.multiple_of(jnp.where(core == 0, on_x, on_y) * 16, 16))
    outs = []

    def put(at, value):
        for b in range(32):
            out[pl.ds(where[b], 16), at : at + side] = value[b * 16 : (b + 1) * 16, :]
        columns = slice(at, at + side)
        for k in (1, 2, 3, 0):
            source = out.at[k * share : (k + 1) * share, columns]
            outs.append(move.start(source, outs_hbm[k].at[:, columns]))

    finish(ready[0] + ready[1])
    put(3 * side, mm(left_c[...], right_a[...], TN).astype(BF))
    finish(ready[2] + ready[3])
    product = mm(left_n[...], right_m[...], TN).astype(BF)
    for j in range(3):
        put(j * side, product[:, j * side : (j + 1) * side])
    finish(outs)


def add_four(parts, columns):
    total = parts[0, :, columns].astype(F32)
    for k in range(1, 4):
        total = total + parts[k, :, columns].astype(F32)
    return total.astype(BF)


def four_sum_kernel(right, own_hbm, a_hbm, b_hbm, c_hbm, *refs):
    out_hbm, parts, out, sems = refs[-4:]
    move = Mover(sems)
    sources = (own_hbm, a_hbm, b_hbm, c_hbm)
    width = out.shape[1]
    step = width // 4
    columns = [slice(j * step, (j + 1) * step) for j in range(4)]
    copies = [[move.start(r.at[:, c], parts.at[k, :, c]) for k, r in enumerate(sources)] for c in columns]
    outs = []
    for c, ready in zip(columns, copies):
        finish(ready)
        out[:, c] = add_four(parts, c)
        at = c.start + (width if right else 0)
        outs.append(move.start(out.at[:, c], out_hbm.at[:, at : at + step]))
    finish(outs)


def last_sum_kernel(
    scale, parts_hbm, s_entry_hbm, s_exit_hbm, t_entry_hbm, t_exit_hbm,
    parts, s_entry, s_exit, t_entry, t_exit, sems,
):
    move = Mover(sems)
    side = s_exit.shape[1]
    columns = [slice(j * side, (j + 1) * side) for j in range(8)]
    copies = [move.start(parts_hbm.at[:, :, c], parts.at[:, :, c]) for c in columns]
    outs = []
    for j, (c, copy) in enumerate(zip(columns, copies)):
        copy.wait()
        total = (jnp.sum(parts[:, :, c].astype(F32), axis=0) * scale).astype(BF)
        entry, exit_ = ((s_entry, s_exit), (t_entry, t_exit))[j // 4]
        if j % 4 < 3:
            entry[:, (j % 4) * side : (j % 4 + 1) * side] = total
        else:
            exit_[...] = total
    for value, target in (
        (s_entry, s_entry_hbm), (s_exit, s_exit_hbm), (t_entry, t_entry_hbm), (t_exit, t_exit_hbm)
    ):
        outs.append(move.start(value, target))
    finish(outs)


HBM = pl.BlockSpec(memory_space=pltpu.HBM)
SMEM = pl.BlockSpec(memory_space=pltpu.SMEM)


def call(kernel, outs, ins, scratch, copies, flops, aliases=None):
    return pl.pallas_call(
        kernel,
        out_shape=tuple(jax.ShapeDtypeStruct(s, d) for s, d in outs),
        in_specs=[SMEM if a.ndim == 1 else HBM for a in ins],
        out_specs=tuple(HBM for _ in outs),
        input_output_aliases=aliases or {},
        scratch_shapes=[pltpu.VMEM(s, d) for s, d in scratch]
        + [pltpu.SemaphoreType.DMA((copies + 4,))],
        compiler_params=pltpu.CompilerParams(vmem_limit_bytes=(64 * 1024 - 128) * 1024),
        cost_estimate=pl.CostEstimate(flops=flops, bytes_accessed=1000, transcendentals=0),
    )(*ins)


def index_of(shape, zl, x, y, zh, c):
    return (((zl * shape[1] + x) * shape[2] + y) * shape[3] + zh) * shape[4] + c


def first_pairs(shape, step):
    pairs = []
    for zl, x, y, zh, c in itertools.product(*(range(n) for n in shape)):
        to = (zl, (x + step) % shape[1], y) if c == 0 else (zl, x, (y + step) % shape[2])
        pairs.append((index_of(shape, zl, x, y, zh, c), index_of(shape, *to, zh, c)))
    return pairs


def second_groups(shape):
    zls, xs, ys, zhs = (range(n) for n in shape[:4])
    on_0 = [[index_of(shape, l, x, y, h, 0) for y in ys for l in zls for h in zhs] for x in xs]
    on_1 = [[index_of(shape, l, x, y, h, 1) for x in xs for l in zls for h in zhs] for y in ys]
    return on_0 + on_1


def per_device(
    frames_in, bottleneck, spatial_entry, spatial_exit, temporal_entry, temporal_exit,
    output_grad, joined_grad,
):
    patches, width = frames_in.shape[2], frames_in.shape[3]
    bots, side = bottleneck.shape[1], spatial_exit.shape[1]
    half = width // 2
    frames = lax.axis_size(FRAME)
    rows = patches + 16
    on = lax.axis_index("c")
    core = on.astype(jnp.int32).reshape(1)
    first = jnp.where(on == 0, lax.axis_index("x"), lax.axis_index("y"))
    place = jnp.stack([on, first])
    place = place.astype(jnp.int32)
    shape = [lax.axis_size(a) for a in ALL]
    clips = lax.axis_size(("zl", "x"))
    scale = 1.0 / math.sqrt(clips * frames * patches)
    frame, bottle, joined = frames_in[0, 0], bottleneck[0], joined_grad[0]
    swap = [(0, 1), (1, 0)]

    def exchange(array):
        blocks = array.reshape(frames, patches // frames, array.shape[1])
        return lax.all_to_all(blocks, FRAME, 0, 0, tiled=True).reshape(array.shape)

    packed, mix, weights, att = call(
        spatial_forward_kernel,
        [
            ((patches, 2 * width), BF), ((rows, 3 * side), BF), ((HEADS, rows, rows), F32),
            ((rows, side), BF),
        ],
        [frame, bottle, spatial_entry, spatial_exit, output_grad[0, 0]],
        [
            ((patches, width), BF), ((bots, width), BF), ((width, 3 * side), BF),
            ((width, side), BF), ((rows, width), F32),
            ((patches, 2 * width), BF), ((rows, 3 * side), BF), ((HEADS, rows, rows), F32),
            ((rows, side), BF),
        ],
        10 + HEADS,
        1000,
    )
    moved = exchange(packed)

    send_s1, kept_sn = call(
        spatial_factors_kernel,
        [((rows, half + side), BF), ((rows, half), BF)],
        [core, frame, bottle, att],
        [
            ((patches, width), BF), ((bots, width), BF), ((rows, width), F32),
            ((rows, half + side), BF), ((rows, half), BF),
        ],
        5,
        1000,
    )
    got_s1 = lax.ppermute(send_s1, "c", swap)
    moved, got_s1 = lax.optimization_barrier((moved, got_s1))

    factors = half + side + half + 3 * side
    back, send_t, kept_t = call(
        functools.partial(temporal_kernel, frames),
        [((patches, width), BF), ((patches, factors), BF), ((patches, width), BF)],
        [core, moved, temporal_entry, temporal_exit],
        [
            ((patches, 2 * width), BF), ((width, 3 * side), BF), ((width, side), BF),
            ((patches, width), BF), ((patches, 3 * side), BF), ((HEADS, patches, patches), F32),
            ((patches, factors), BF), ((patches, width), BF),
        ],
        8,
        1000,
    )
    back = exchange(back)

    got_t = lax.ppermute(send_t, "c", swap)

    def weight_gradient(count, places, arrays):
        parts = call(
            functools.partial(weight_gradient_kernel, places),
            [((half // 4, 4 * side), BF)] * 4,
            [place] + arrays,
            [
                ((2 * count, half), BF), ((2 * count, half), BF), ((2 * count, 3 * side), BF),
                ((2 * count, side), BF), ((half, 4 * side), BF),
            ],
            24,
            1000,
        )
        return parts

    def passed_on(parts):
        return [parts[0]] + [
            lax.ppermute(parts[k], ALL, first_pairs(shape, k)) for k in (1, 3, 2)
        ]

    cot_at, mix_at = half + side, half + side + half
    parts_t = weight_gradient(
        patches,
        (
            ((0, half), (2, cot_at)), ((1, half), (2, half)),
            ((0, 0), (2, 0)), ((1, mix_at), (2, mix_at)),
        ),
        [kept_t, send_t, got_t],
    )
    parts_t = passed_on(parts_t)
    back, parts_t[0] = lax.optimization_barrier((back, parts_t[0]))
    share = (half // 4, 4 * side)
    send_sc, kept_sc, d_mix_s = call(
        functools.partial(spatial_backward_kernel, frames),
        [((rows, half), BF), ((rows, half), BF), ((rows, 3 * side), BF)],
        [core, back, joined, mix, weights, spatial_exit],
        [
            ((rows, width), BF), ((bots, width), BF), ((rows, 3 * side), BF),
            ((HEADS, rows, rows), F32), ((width, side), BF), ((rows, half), BF),
            ((rows, half), BF), ((rows, 3 * side), BF),
        ],
        7 + HEADS,
        1000,
    )
    got_sc = lax.ppermute(send_sc, "c", swap)
    got_sm = lax.ppermute(d_mix_s, "c", swap)
    parts_s = weight_gradient(
        rows,
        (
            ((3, 0), (4, 0)), ((1, half), (2, half)),
            ((0, 0), (2, 0)), ((5, 0), (6, 0)),
        ),
        [kept_sn, send_s1, got_s1, kept_sc, got_sc, d_mix_s, got_sm],
    )
    tied = lax.optimization_barrier((d_mix_s, *parts_s, *parts_t))
    after, parts_s, parts_t = tied[0], tied[1:5], list(tied[5:])
    parts_s = passed_on(parts_s)
    (local,) = call(
        functools.partial(bottle_inputs_kernel, frames),
        [((bots, width), F32)],
        [bottle, joined, after, spatial_entry],
        [
            ((bots, width), BF), ((bots, width), BF), ((16, 3 * side), BF),
            ((width, 3 * side), BF), ((16, width), F32), ((bots, width), F32),
        ],
        5,
        1000,
    )

    def with_partner(local, axis, bit):
        pairs = [(i, i ^ bit) for i in range(lax.axis_size(axis))]
        return local + lax.ppermute(local, axis, pairs)

    local = with_partner(local, "zh", 1)
    local, after, *parts_s = lax.optimization_barrier((local, after, *parts_s))
    (delta,) = call(
        patch_inputs_kernel,
        [((patches, width), BF)],
        [frame, back, after, spatial_entry],
        [
            ((patches, width), BF), ((patches, width), BF), ((patches, 3 * side), BF),
            ((width, 3 * side), BF), ((patches, width), BF),
        ],
        5,
        1000,
    )
    local = with_partner(local, "c", 1)
    ys = shape[2]
    sent = [local] + [
        lax.ppermute(local, "y", [(i, (i + k) % ys) for i in range(ys)]) for k in range(1, ys)
    ]
    total = None
    for j in range(ys):
        back_by = (lax.axis_index("y") - j) % ys
        part = sent[0]
        for k in range(1, ys):
            part = jnp.where(back_by == k, sent[k], part)
        total = part if total is None else total + part
    local = total
    wide = (half // 4, 8 * side)
    scratch = [((4, *share), BF), (share, BF)]
    (half_done,) = call(
        functools.partial(four_sum_kernel, True), [(wide, BF)], parts_t, scratch, 20, 1000
    )
    (both,) = call(
        functools.partial(four_sum_kernel, False), [(wide, BF)], [*parts_s, half_done], scratch,
        20, 1000, {4: 0},
    )
    groups = second_groups(shape)
    count = len(groups[0])
    last = lax.all_to_all(
        both.reshape(count, -1, 8 * side), ALL, 0, 0, axis_index_groups=groups, tiled=True
    )

    own = last.shape[1]
    s_entry, s_exit, t_entry, t_exit = call(
        functools.partial(last_sum_kernel, scale),
        [((own, 3 * side), BF), ((own, side), BF)] * 2,
        [last],
        [
            (last.shape, BF),
            ((own, 3 * side), BF), ((own, side), BF), ((own, 3 * side), BF), ((own, side), BF),
        ],
        12,
        1000,
    )
    return (
        delta[None, None], local.astype(BF)[None], s_entry, s_exit, t_entry, t_exit
    )


def solution(mesh):
    finer = Mesh(mesh.devices.reshape(2, mesh.shape["dp"] // 2, 4, 2, 2), ALL)
    dp = ("zl", "x")
    row = P(ALL, None)
    clip = P(dp, None, None)
    patch = P(dp, FRAME, None, None)
    return jax.shard_map(
        per_device,
        mesh=finer,
        in_specs=(patch, clip, P(), P(), P(), P(), patch, clip),
        out_specs=(patch, clip, row, row, row, row),
        check_vma=False,
    )
```

```python
import functools
import itertools
import math

import jax
import jax.numpy as jnp
from jax import lax
from jax.experimental import pallas as pl
from jax.experimental.pallas import tpu as pltpu
from jax.sharding import Mesh
from jax.sharding import PartitionSpec as P

HEADS = 8
EPSILON = 1e-05
FRAME = ("y", "zh", "c")
ALL = ("zl", "x", "y", "zh", "c")
BF = jnp.bfloat16
F32 = jnp.float32

NN = (((1,), (0,)), ((), ()))
NT = (((1,), (1,)), ((), ()))
TN = (((0,), (0,)), ((), ()))


def mm(a, b, dims):
    return lax.dot_general(a, b, dims, preferred_element_type=F32)


def normalize(u):
    centred = u - jnp.mean(u, axis=-1, keepdims=True)
    inverse = lax.rsqrt(jnp.mean(centred * centred, axis=-1, keepdims=True) + EPSILON)
    return centred * inverse, inverse


def half_masks(size):
    lane = lax.broadcasted_iota(jnp.int32, (1, 2 * size), 1)
    low = (lane < size).astype(F32)
    return low.astype(BF), (1.0 - low).astype(BF)


def head_pairs(mix_ref):
    side = mix_ref.shape[1] // 3
    width = 2 * (side // HEADS)

    def columns(part, p):
        return mix_ref[:, part * side + p * width : part * side + (p + 1) * width]

    return side, width, 1.0 / math.sqrt(width // 2), columns


def attention_forward(mix_ref, keep, masks, save, put):
    _, width, factor, columns = head_pairs(mix_ref)
    heads = [(p, h) for p in range(HEADS // 2) for h in range(2)]
    scores = [mm(columns(1, p) * masks[h], columns(0, p), NT) * factor for p, h in heads]
    scores = [jnp.where(keep, s, -jnp.inf) for s in scores]
    tops = [jnp.max(s, axis=0, keepdims=True) for s in scores]
    expons = [jnp.exp(s - t) for s, t in zip(scores, tops)]
    sums = [1.0 / jnp.sum(e, axis=0, keepdims=True) for e in expons]
    weights = [e * r for e, r in zip(expons, sums)]
    for k, w in enumerate(weights):
        save(k, w)
    parts = [mm(w.astype(BF), columns(2, p) * masks[h], TN) for w, (p, h) in zip(weights, heads)]
    for p in range(HEADS // 2):
        put(p, width, (parts[2 * p] + parts[2 * p + 1]).astype(BF))


def attention_backward(mix_ref, load, d_att, masks, put):
    side, width, factor, columns = head_pairs(mix_ref)
    heads = [(p, h) for p in range(HEADS // 2) for h in range(2)]
    d_heads = [d_att[:, p * width : (p + 1) * width] * masks[h] for p, h in heads]
    grads = [mm(columns(2, p), d, NT) for d, (p, _) in zip(d_heads, heads)]
    scores_grads = []
    for k, grad in enumerate(grads):
        weights = load(k)
        centre = jnp.sum(weights * grad, axis=0, keepdims=True)
        scores_grads.append((weights * (grad - centre) * factor).astype(BF))
    dv = [mm(load(k, True).astype(BF), d, NN) for k, d in enumerate(d_heads)]
    dk = [mm(g, columns(0, p) * masks[h], NN) for g, (p, h) in zip(scores_grads, heads)]
    dq = [mm(g, columns(1, p) * masks[h], TN) for g, (p, h) in zip(scores_grads, heads)]
    for part, each in enumerate((dq, dk, dv)):
        for p in range(HEADS // 2):
            value = each[2 * p] + each[2 * p + 1]
            put(part * side + p * width, width, value.astype(BF))


def inputs_gradient(c, normed, inverse, d_normed):
    inner = (
        d_normed
        - jnp.mean(d_normed, axis=-1, keepdims=True)
        - normed * jnp.mean(d_normed * normed, axis=-1, keepdims=True)
    )
    return c.astype(F32) + inverse * inner


def picker(half):
    row = lax.broadcasted_iota(jnp.int32, (256, 128), 0)
    col = lax.broadcasted_iota(jnp.int32, (256, 128), 1)
    source = (col // 8) * 16 + half * 8 + col % 8
    return (row == source).astype(F32).astype(BF)


def pick(values, chosen, out_ref, at):
    for b in range(values.shape[1] // 256):
        part = mm(values[:, 256 * b : 256 * (b + 1)], chosen, NN)
        out_ref[:, at + 128 * b : at + 128 * (b + 1)] = part.astype(BF)


class Mover:
    def __init__(self, sems):
        self.sems, self.count = sems, 0

    def start(self, source, target):
        copy = pltpu.make_async_copy(source, target, self.sems.at[self.count])
        self.count += 1
        copy.start()
        return copy

    def spread(self, source, target, count=2):
        step = source.shape[0] // count
        rows = [slice(k * step, (k + 1) * step) for k in range(count)]
        return [self.start(source.at[r, :], target.at[r, :]) for r in rows]


def finish(copies):
    for copy in copies:
        copy.wait()


def fill_tokens(tokens, frames, bottle):
    patches, bots = frames.shape[0], bottle.shape[0]
    rows, width = tokens.shape
    tokens[0:patches, :] = frames[...].astype(F32)
    tokens[patches:rows, :] = jnp.zeros((rows - patches, width), F32)
    tokens[patches : patches + bots, :] = bottle[...].astype(F32)


def spatial_forward_kernel(
    frames_hbm, bottle_hbm, entry_hbm, exit_hbm, grad_hbm,
    packed_hbm, mix_hbm, weights_hbm, att_hbm,
    frames, bottle, entry, exit_, tokens, packed, mix, weights_buf, att, sems,
):
    move = Mover(sems)
    patches, bots = frames.shape[0], bottle.shape[0]
    rows, width = tokens.shape
    side = exit_.shape[1]
    first = [move.start(frames_hbm, frames), move.start(bottle_hbm, bottle)]
    columns = [slice(j * side, (j + 1) * side) for j in range(3)]
    entries = [move.spread(entry_hbm.at[:, c], entry.at[:, c]) for c in columns]
    later = move.spread(exit_hbm, exit_)
    grads = move.start(grad_hbm, packed.at[:, width : 2 * width])
    outs = []
    finish(first)
    fill_tokens(tokens, frames, bottle)
    low = normalize(tokens[...])[0].astype(BF)
    for c, copy in zip(columns, entries):
        finish(copy)
        mix[:, c] = mm(low, entry[:, c], NN).astype(BF)
    outs.append(move.start(mix, mix_hbm))
    masks = half_masks(side // HEADS)
    keep = lax.broadcasted_iota(jnp.int32, (rows, rows), 0) < patches + bots

    def save(h, weights):
        weights_buf[h] = weights
        outs.append(move.start(weights_buf.at[h], weights_hbm.at[h]))

    def put(p, w, value):
        att[:, p * w : (p + 1) * w] = value

    attention_forward(mix, keep, masks, save, put)
    outs.append(move.start(att, att_hbm))
    finish(later)
    out = tokens[0:patches, :] + mm(att[0:patches, :], exit_[...], NT)
    packed[:, 0:width] = out.astype(BF)
    grads.wait()
    outs.append(move.start(packed, packed_hbm))
    finish(outs)


def spatial_factors_kernel(
    core_ref, frames_hbm, bottle_hbm, att_hbm, send_hbm, kept_hbm,
    frames, bottle, tokens, send, kept, sems,
):
    move = Mover(sems)
    half = kept.shape[1]
    first = [move.start(frames_hbm, frames), move.start(bottle_hbm, bottle)]
    copied = move.start(att_hbm, send.at[:, half:])
    finish(first)
    fill_tokens(tokens, frames, bottle)
    low = normalize(tokens[...])[0].astype(BF)
    core = core_ref[0]
    pick(low, picker(1 - core), send, 0)
    copied.wait()
    outs = [move.start(send, send_hbm)]
    pick(low, picker(core), kept, 0)
    outs.append(move.start(kept, kept_hbm))
    finish(outs)


def temporal_kernel(
    frames, core_ref, moved_hbm, entry_hbm, exit_hbm, back_hbm, send_hbm, kept_hbm,
    moved, entry, exit_, back, mix, weights_buf, send, kept, sems,
):
    move = Mover(sems)
    rows, width = back.shape
    half, side = width // 2, exit_.shape[1]
    seqs = rows // frames
    first = move.start(moved_hbm, moved)
    columns = [slice(j * side, (j + 1) * side) for j in range(3)]
    entries = [move.spread(entry_hbm.at[:, c], entry.at[:, c]) for c in columns]
    later = move.spread(exit_hbm, exit_)
    core = core_ref[0]
    other, own = picker(1 - core), picker(core)
    first.wait()
    cot = moved[:, width : 2 * width]
    normed, inverse = normalize(moved[:, 0:width].astype(F32))
    low = normed.astype(BF)
    pick(cot, other, send, half + side)
    pick(cot, own, kept, half)
    for c, copy in zip(columns, entries):
        finish(copy)
        mix[:, c] = mm(low, entry[:, c], NN).astype(BF)
    pick(low, other, send, 0)
    pick(low, own, kept, 0)
    outs = [move.start(kept, kept_hbm)]
    masks = half_masks(side // HEADS)
    keep = (
        lax.broadcasted_iota(jnp.int32, (rows, rows), 0) % seqs
        == lax.broadcasted_iota(jnp.int32, (rows, rows), 1) % seqs
    )

    def save(h, weights):
        weights_buf[h] = weights

    def put(p, w, value):
        send[:, half + p * w : half + (p + 1) * w] = value

    attention_forward(mix, keep, masks, save, put)
    finish(later)
    d_att = mm(cot, exit_[...], NN).astype(BF)
    at_mix = width + side

    def put_grad(at, w, value):
        send[:, at_mix + at : at_mix + at + w] = value

    attention_backward(mix, lambda h, again=False: weights_buf[h], d_att, masks, put_grad)
    outs.append(move.start(send, send_hbm))
    d_normed = mm(send[:, at_mix:], entry[...], NT)
    back[...] = inputs_gradient(cot, normed, inverse, d_normed).astype(BF)
    outs.append(move.start(back, back_hbm))
    finish(outs)


def fill_cotangent(cot, joined, frames):
    patches = cot.shape[0] - 16
    rows = joined[...].astype(F32) / frames
    padded = jnp.concatenate([rows, jnp.zeros((16 - rows.shape[0], rows.shape[1]), F32)], axis=0)
    cot[patches:, :] = padded.astype(BF)


def spatial_backward_kernel(
    frames, core_ref, back_hbm, joined_hbm, mix_hbm, weights_hbm, exit_hbm,
    picked_hbm, kept_hbm, d_mix_hbm,
    cot, joined, mix, weights_buf, exit_, picked, kept, d_mix, sems,
):
    move = Mover(sems)
    side = exit_.shape[1]
    patches = back_hbm.shape[0]
    first = [move.start(joined_hbm, joined), move.start(back_hbm, cot.at[0:patches, :])]
    first += move.spread(exit_hbm, exit_)
    second = move.start(mix_hbm, mix)
    heads = [move.start(weights_hbm.at[h], weights_buf.at[h]) for h in range(HEADS)]
    finish(first)
    fill_cotangent(cot, joined, frames)
    c = cot[...]
    d_att = mm(c, exit_[...], NN).astype(BF)
    core = core_ref[0]
    pick(c, picker(core), kept, 0)
    outs = [move.start(kept, kept_hbm)]
    pick(c, picker(1 - core), picked, 0)
    outs.append(move.start(picked, picked_hbm))
    masks = half_masks(side // HEADS)
    second.wait()

    def load(h, again=False):
        if not again:
            heads[h].wait()
        return weights_buf[h]

    def put_grad(at, w, value):
        d_mix[:, at : at + w] = value

    attention_backward(mix, load, d_att, masks, put_grad)
    outs.append(move.start(d_mix, d_mix_hbm))
    finish(outs)


def bottle_inputs_kernel(
    frames_count, bottle_hbm, joined_hbm, d_mix_hbm, entry_hbm, local_hbm,
    bottle, joined, d_mix, entry, tokens, local, sems,
):
    move = Mover(sems)
    bots = bottle.shape[0]
    second = move.spread(entry_hbm, entry, 4)
    second.append(move.start(d_mix_hbm.at[d_mix_hbm.shape[0] - 16 :, :], d_mix))
    first = [move.start(bottle_hbm, bottle), move.start(joined_hbm, joined)]
    finish(first)
    tokens[...] = jnp.zeros(tokens.shape, F32)
    tokens[0:bots, :] = bottle[...].astype(F32)
    normed, inverse = normalize(tokens[...])
    c = (joined[...].astype(F32) / frames_count).astype(BF)
    finish(second)
    d_normed = mm(d_mix[...], entry[...], NT)
    grads = inputs_gradient(c, normed[0:bots], inverse[0:bots], d_normed[0:bots])
    local[...] = grads
    move.start(local, local_hbm).wait()


def patch_inputs_kernel(
    frames_hbm, back_hbm, d_mix_hbm, entry_hbm, delta_hbm,
    frames, cot, d_mix, entry, delta, sems,
):
    move = Mover(sems)
    first = move.start(frames_hbm, frames)
    second = [
        move.start(d_mix_hbm.at[0 : d_mix.shape[0], :], d_mix),
        move.start(back_hbm, cot),
        *move.spread(entry_hbm, entry, 4),
    ]
    first.wait()
    normed, inverse = normalize(frames[...].astype(F32))
    finish(second)
    d_normed = mm(d_mix[...], entry[...], NT)
    delta[...] = inputs_gradient(cot[...], normed, inverse, d_normed).astype(BF)
    move.start(delta, delta_hbm).wait()


def weight_gradient_kernel(places, place_ref, *refs):
    arrays, refs = refs[: len(refs) - 10], refs[len(refs) - 10 :]
    outs_hbm, (left_n, left_c, right_m, right_a, out, sems) = refs[:4], refs[4:]
    move = Mover(sems)
    rows = left_n.shape[0] // 2
    share = out.shape[0] // 4

    def both(target, pair):
        copies = []
        for k, (index, at) in enumerate(pair):
            source = arrays[index].at[:, at : at + target.shape[1]]
            copies.append(move.start(source, target.at[k * rows : (k + 1) * rows, :]))
        return copies

    ready = [both(t, places[k]) for k, t in enumerate((left_c, right_a, left_n, right_m))]
    side = right_a.shape[1]
    core, place = place_ref[0], place_ref[1]
    where = []
    for b in range(32):
        zl, x, y = b // 16, b // 4 % 4, b % 4
        on_x = ((x + 4 - place) % 4) * 8 + y * 2 + zl
        on_y = ((y + 4 - place) % 4) * 8 + x * 2 + zl
        where.append(pl.multiple_of(jnp.where(core == 0, on_x, on_y) * 16, 16))
    outs = []

    def put(at, value):
        for b in range(32):
            out[pl.ds(where[b], 16), at : at + side] = value[b * 16 : (b + 1) * 16, :]
        columns = slice(at, at + side)
        for k in (1, 2, 3, 0):
            source = out.at[k * share : (k + 1) * share, columns]
            outs.append(move.start(source, outs_hbm[k].at[:, columns]))

    finish(ready[0] + ready[1])
    put(3 * side, mm(left_c[...], right_a[...], TN).astype(BF))
    finish(ready[2] + ready[3])
    product = mm(left_n[...], right_m[...], TN).astype(BF)
    for j in range(3):
        put(j * side, product[:, j * side : (j + 1) * side])
    finish(outs)


def add_four(parts, columns):
    total = parts[0, :, columns].astype(F32)
    for k in range(1, 4):
        total = total + parts[k, :, columns].astype(F32)
    return total.astype(BF)


def four_sum_kernel(right, own_hbm, a_hbm, b_hbm, c_hbm, *refs):
    out_hbm, parts, out, sems = refs[-4:]
    move = Mover(sems)
    sources = (own_hbm, a_hbm, b_hbm, c_hbm)
    width = out.shape[1]
    step = width // 4
    columns = [slice(j * step, (j + 1) * step) for j in range(4)]
    copies = [[move.start(r.at[:, c], parts.at[k, :, c]) for k, r in enumerate(sources)] for c in columns]
    outs = []
    for c, ready in zip(columns, copies):
        finish(ready)
        out[:, c] = add_four(parts, c)
        at = c.start + (width if right else 0)
        outs.append(move.start(out.at[:, c], out_hbm.at[:, at : at + step]))
    finish(outs)


def last_sum_kernel(
    scale, parts_hbm, s_entry_hbm, s_exit_hbm, t_entry_hbm, t_exit_hbm,
    parts, s_entry, s_exit, t_entry, t_exit, sems,
):
    move = Mover(sems)
    side = s_exit.shape[1]
    columns = [slice(j * side, (j + 1) * side) for j in range(8)]
    copies = [move.start(parts_hbm.at[:, :, c], parts.at[:, :, c]) for c in columns]
    outs = []
    for j, (c, copy) in enumerate(zip(columns, copies)):
        copy.wait()
        total = (jnp.sum(parts[:, :, c].astype(F32), axis=0) * scale).astype(BF)
        entry, exit_ = ((s_entry, s_exit), (t_entry, t_exit))[j // 4]
        if j % 4 < 3:
            entry[:, (j % 4) * side : (j % 4 + 1) * side] = total
        else:
            exit_[...] = total
    for value, target in (
        (s_entry, s_entry_hbm), (s_exit, s_exit_hbm), (t_entry, t_entry_hbm), (t_exit, t_exit_hbm)
    ):
        outs.append(move.start(value, target))
    finish(outs)


HBM = pl.BlockSpec(memory_space=pltpu.HBM)
SMEM = pl.BlockSpec(memory_space=pltpu.SMEM)


def call(kernel, outs, ins, scratch, copies, flops, aliases=None):
    return pl.pallas_call(
        kernel,
        out_shape=tuple(jax.ShapeDtypeStruct(s, d) for s, d in outs),
        in_specs=[SMEM if a.ndim == 1 else HBM for a in ins],
        out_specs=tuple(HBM for _ in outs),
        input_output_aliases=aliases or {},
        scratch_shapes=[pltpu.VMEM(s, d) for s, d in scratch]
        + [pltpu.SemaphoreType.DMA((copies + 4,))],
        compiler_params=pltpu.CompilerParams(vmem_limit_bytes=(64 * 1024 - 128) * 1024),
        cost_estimate=pl.CostEstimate(flops=flops, bytes_accessed=1000, transcendentals=0),
    )(*ins)


def index_of(shape, zl, x, y, zh, c):
    return (((zl * shape[1] + x) * shape[2] + y) * shape[3] + zh) * shape[4] + c


def first_pairs(shape, step):
    pairs = []
    for zl, x, y, zh, c in itertools.product(*(range(n) for n in shape)):
        to = (zl, (x + step) % shape[1], y) if c == 0 else (zl, x, (y + step) % shape[2])
        pairs.append((index_of(shape, zl, x, y, zh, c), index_of(shape, *to, zh, c)))
    return pairs


def second_groups(shape):
    zls, xs, ys, zhs = (range(n) for n in shape[:4])
    on_0 = [[index_of(shape, l, x, y, h, 0) for y in ys for l in zls for h in zhs] for x in xs]
    on_1 = [[index_of(shape, l, x, y, h, 1) for x in xs for l in zls for h in zhs] for y in ys]
    return on_0 + on_1


def per_device(
    frames_in, bottleneck, spatial_entry, spatial_exit, temporal_entry, temporal_exit,
    output_grad, joined_grad,
):
    patches, width = frames_in.shape[2], frames_in.shape[3]
    bots, side = bottleneck.shape[1], spatial_exit.shape[1]
    half = width // 2
    frames = lax.axis_size(FRAME)
    rows = patches + 16
    on = lax.axis_index("c")
    core = on.astype(jnp.int32).reshape(1)
    first = jnp.where(on == 0, lax.axis_index("x"), lax.axis_index("y"))
    place = jnp.stack([on, first])
    place = place.astype(jnp.int32)
    shape = [lax.axis_size(a) for a in ALL]
    clips = lax.axis_size(("zl", "x"))
    scale = 1.0 / math.sqrt(clips * frames * patches)
    frame, bottle, joined = frames_in[0, 0], bottleneck[0], joined_grad[0]
    swap = [(0, 1), (1, 0)]

    def exchange(array):
        blocks = array.reshape(frames, patches // frames, array.shape[1])
        return lax.all_to_all(blocks, FRAME, 0, 0, tiled=True).reshape(array.shape)

    packed, mix, weights, att = call(
        spatial_forward_kernel,
        [
            ((patches, 2 * width), BF), ((rows, 3 * side), BF), ((HEADS, rows, rows), F32),
            ((rows, side), BF),
        ],
        [frame, bottle, spatial_entry, spatial_exit, output_grad[0, 0]],
        [
            ((patches, width), BF), ((bots, width), BF), ((width, 3 * side), BF),
            ((width, side), BF), ((rows, width), F32),
            ((patches, 2 * width), BF), ((rows, 3 * side), BF), ((HEADS, rows, rows), F32),
            ((rows, side), BF),
        ],
        10 + HEADS,
        1000,
    )
    moved = exchange(packed)

    send_s1, kept_sn = call(
        spatial_factors_kernel,
        [((rows, half + side), BF), ((rows, half), BF)],
        [core, frame, bottle, att],
        [
            ((patches, width), BF), ((bots, width), BF), ((rows, width), F32),
            ((rows, half + side), BF), ((rows, half), BF),
        ],
        5,
        1000,
    )
    got_s1 = lax.ppermute(send_s1, "c", swap)
    moved, got_s1 = lax.optimization_barrier((moved, got_s1))

    factors = half + side + half + 3 * side
    back, send_t, kept_t = call(
        functools.partial(temporal_kernel, frames),
        [((patches, width), BF), ((patches, factors), BF), ((patches, width), BF)],
        [core, moved, temporal_entry, temporal_exit],
        [
            ((patches, 2 * width), BF), ((width, 3 * side), BF), ((width, side), BF),
            ((patches, width), BF), ((patches, 3 * side), BF), ((HEADS, patches, patches), F32),
            ((patches, factors), BF), ((patches, width), BF),
        ],
        8,
        1000,
    )
    back = exchange(back)

    got_t = lax.ppermute(send_t, "c", swap)

    def weight_gradient(count, places, arrays):
        parts = call(
            functools.partial(weight_gradient_kernel, places),
            [((half // 4, 4 * side), BF)] * 4,
            [place] + arrays,
            [
                ((2 * count, half), BF), ((2 * count, half), BF), ((2 * count, 3 * side), BF),
                ((2 * count, side), BF), ((half, 4 * side), BF),
            ],
            24,
            1000,
        )
        return parts

    def passed_on(parts):
        return [parts[0]] + [
            lax.ppermute(parts[k], ALL, first_pairs(shape, k)) for k in (1, 3, 2)
        ]

    cot_at, mix_at = half + side, half + side + half
    parts_t = weight_gradient(
        patches,
        (
            ((0, half), (2, cot_at)), ((1, half), (2, half)),
            ((0, 0), (2, 0)), ((1, mix_at), (2, mix_at)),
        ),
        [kept_t, send_t, got_t],
    )
    parts_t = passed_on(parts_t)
    back, parts_t[0] = lax.optimization_barrier((back, parts_t[0]))
    share = (half // 4, 4 * side)
    send_sc, kept_sc, d_mix_s = call(
        functools.partial(spatial_backward_kernel, frames),
        [((rows, half), BF), ((rows, half), BF), ((rows, 3 * side), BF)],
        [core, back, joined, mix, weights, spatial_exit],
        [
            ((rows, width), BF), ((bots, width), BF), ((rows, 3 * side), BF),
            ((HEADS, rows, rows), F32), ((width, side), BF), ((rows, half), BF),
            ((rows, half), BF), ((rows, 3 * side), BF),
        ],
        7 + HEADS,
        1000,
    )
    got_sc = lax.ppermute(send_sc, "c", swap)
    got_sm = lax.ppermute(d_mix_s, "c", swap)
    parts_s = weight_gradient(
        rows,
        (
            ((3, 0), (4, 0)), ((1, half), (2, half)),
            ((0, 0), (2, 0)), ((5, 0), (6, 0)),
        ),
        [kept_sn, send_s1, got_s1, kept_sc, got_sc, d_mix_s, got_sm],
    )
    tied = lax.optimization_barrier((d_mix_s, *parts_s, *parts_t))
    after, parts_s, parts_t = tied[0], tied[1:5], list(tied[5:])
    parts_s = passed_on(parts_s)
    (local,) = call(
        functools.partial(bottle_inputs_kernel, frames),
        [((bots, width), F32)],
        [bottle, joined, after, spatial_entry],
        [
            ((bots, width), BF), ((bots, width), BF), ((16, 3 * side), BF),
            ((width, 3 * side), BF), ((16, width), F32), ((bots, width), F32),
        ],
        5,
        1000,
    )

    def with_partner(local, axis, bit):
        pairs = [(i, i ^ bit) for i in range(lax.axis_size(axis))]
        return local + lax.ppermute(local, axis, pairs)

    local = with_partner(local, "zh", 1)
    local, after, *parts_s = lax.optimization_barrier((local, after, *parts_s))
    (delta,) = call(
        patch_inputs_kernel,
        [((patches, width), BF)],
        [frame, back, after, spatial_entry],
        [
            ((patches, width), BF), ((patches, width), BF), ((patches, 3 * side), BF),
            ((width, 3 * side), BF), ((patches, width), BF),
        ],
        5,
        1000,
    )
    local = with_partner(local, "c", 1)
    ys = shape[2]
    sent = [local] + [
        lax.ppermute(local, "y", [(i, (i + k) % ys) for i in range(ys)]) for k in range(1, ys)
    ]
    total = None
    for j in range(ys):
        back_by = (lax.axis_index("y") - j) % ys
        part = sent[0]
        for k in range(1, ys):
            part = jnp.where(back_by == k, sent[k], part)
        total = part if total is None else total + part
    local = total
    wide = (half // 4, 8 * side)
    scratch = [((4, *share), BF), (share, BF)]
    (half_done,) = call(
        functools.partial(four_sum_kernel, True), [(wide, BF)], parts_t, scratch, 20, 1000
    )
    (both,) = call(
        functools.partial(four_sum_kernel, False), [(wide, BF)], [*parts_s, half_done], scratch,
        20, 1000, {4: 0},
    )
    groups = second_groups(shape)
    count = len(groups[0])
    last = lax.all_to_all(
        both.reshape(count, -1, 8 * side), ALL, 0, 0, axis_index_groups=groups, tiled=True
    )

    own = last.shape[1]
    s_entry, s_exit, t_entry, t_exit = call(
        functools.partial(last_sum_kernel, scale),
        [((own, 3 * side), BF), ((own, side), BF)] * 2,
        [last],
        [
            (last.shape, BF),
            ((own, 3 * side), BF), ((own, side), BF), ((own, 3 * side), BF), ((own, side), BF),
        ],
        12,
        1000,
    )
    return (
        delta[None, None], local.astype(BF)[None], s_entry, s_exit, t_entry, t_exit
    )


def solution(mesh):
    finer = Mesh(mesh.devices.reshape(2, mesh.shape["dp"] // 2, 4, 2, 2), ALL)
    dp = ("zl", "x")
    row = P(ALL, None)
    clip = P(dp, None, None)
    patch = P(dp, FRAME, None, None)
    return jax.shard_map(
        per_device,
        mesh=finer,
        in_specs=(patch, clip, P(), P(), P(), P(), patch, clip),
        out_specs=(patch, clip, row, row, row, row),
        check_vma=False,
    )
```

```python
import functools
import itertools
import math

import jax
import jax.numpy as jnp
from jax import lax
from jax.experimental import pallas as pl
from jax.experimental.pallas import tpu as pltpu
from jax.sharding import Mesh
from jax.sharding import PartitionSpec as P

HEADS = 8
EPSILON = 1e-05
FRAME = ("y", "zh", "c")
ALL = ("zl", "x", "y", "zh", "c")
BF = jnp.bfloat16
F32 = jnp.float32

NN = (((1,), (0,)), ((), ()))
NT = (((1,), (1,)), ((), ()))
TN = (((0,), (0,)), ((), ()))


def mm(a, b, dims):
    return lax.dot_general(a, b, dims, preferred_element_type=F32)


def normalize(u):
    centred = u - jnp.mean(u, axis=-1, keepdims=True)
    inverse = lax.rsqrt(jnp.mean(centred * centred, axis=-1, keepdims=True) + EPSILON)
    return centred * inverse, inverse


def half_masks(size):
    lane = lax.broadcasted_iota(jnp.int32, (1, 2 * size), 1)
    low = (lane < size).astype(F32)
    return low.astype(BF), (1.0 - low).astype(BF)


def head_pairs(mix_ref):
    side = mix_ref.shape[1] // 3
    width = 2 * (side // HEADS)

    def columns(part, p):
        return mix_ref[:, part * side + p * width : part * side + (p + 1) * width]

    return side, width, 1.0 / math.sqrt(width // 2), columns


def attention_forward(mix_ref, keep, masks, save, put):
    _, width, factor, columns = head_pairs(mix_ref)
    heads = [(p, h) for p in range(HEADS // 2) for h in range(2)]
    scores = [mm(columns(1, p) * masks[h], columns(0, p), NT) * factor for p, h in heads]
    scores = [jnp.where(keep, s, -jnp.inf) for s in scores]
    tops = [jnp.max(s, axis=0, keepdims=True) for s in scores]
    expons = [jnp.exp(s - t) for s, t in zip(scores, tops)]
    sums = [1.0 / jnp.sum(e, axis=0, keepdims=True) for e in expons]
    weights = [e * r for e, r in zip(expons, sums)]
    for k, w in enumerate(weights):
        save(k, w)
    parts = [mm(w.astype(BF), columns(2, p) * masks[h], TN) for w, (p, h) in zip(weights, heads)]
    for p in range(HEADS // 2):
        put(p, width, (parts[2 * p] + parts[2 * p + 1]).astype(BF))


def attention_backward(mix_ref, load, d_att, masks, put):
    side, width, factor, columns = head_pairs(mix_ref)
    heads = [(p, h) for p in range(HEADS // 2) for h in range(2)]
    d_heads = [d_att[:, p * width : (p + 1) * width] * masks[h] for p, h in heads]
    grads = [mm(columns(2, p), d, NT) for d, (p, _) in zip(d_heads, heads)]
    scores_grads = []
    for k, grad in enumerate(grads):
        weights = load(k)
        centre = jnp.sum(weights * grad, axis=0, keepdims=True)
        scores_grads.append((weights * (grad - centre) * factor).astype(BF))
    dv = [mm(load(k, True).astype(BF), d, NN) for k, d in enumerate(d_heads)]
    dk = [mm(g, columns(0, p) * masks[h], NN) for g, (p, h) in zip(scores_grads, heads)]
    dq = [mm(g, columns(1, p) * masks[h], TN) for g, (p, h) in zip(scores_grads, heads)]
    for part, each in enumerate((dq, dk, dv)):
        for p in range(HEADS // 2):
            value = each[2 * p] + each[2 * p + 1]
            put(part * side + p * width, width, value.astype(BF))


def inputs_gradient(c, normed, inverse, d_normed):
    inner = (
        d_normed
        - jnp.mean(d_normed, axis=-1, keepdims=True)
        - normed * jnp.mean(d_normed * normed, axis=-1, keepdims=True)
    )
    return c.astype(F32) + inverse * inner


def picker(half):
    row = lax.broadcasted_iota(jnp.int32, (256, 128), 0)
    col = lax.broadcasted_iota(jnp.int32, (256, 128), 1)
    source = (col // 8) * 16 + half * 8 + col % 8
    return (row == source).astype(F32).astype(BF)


def pick(values, chosen, out_ref, at):
    for b in range(values.shape[1] // 256):
        part = mm(values[:, 256 * b : 256 * (b + 1)], chosen, NN)
        out_ref[:, at + 128 * b : at + 128 * (b + 1)] = part.astype(BF)


class Mover:
    def __init__(self, sems):
        self.sems, self.count = sems, 0

    def start(self, source, target):
        copy = pltpu.make_async_copy(source, target, self.sems.at[self.count])
        self.count += 1
        copy.start()
        return copy

    def spread(self, source, target, count=2):
        step = source.shape[0] // count
        rows = [slice(k * step, (k + 1) * step) for k in range(count)]
        return [self.start(source.at[r, :], target.at[r, :]) for r in rows]


def finish(copies):
    for copy in copies:
        copy.wait()


def fill_tokens(tokens, frames, bottle):
    patches, bots = frames.shape[0], bottle.shape[0]
    rows, width = tokens.shape
    tokens[0:patches, :] = frames[...].astype(F32)
    tokens[patches:rows, :] = jnp.zeros((rows - patches, width), F32)
    tokens[patches : patches + bots, :] = bottle[...].astype(F32)


def spatial_forward_kernel(
    frames_hbm, bottle_hbm, entry_hbm, exit_hbm, grad_hbm,
    packed_hbm, mix_hbm, weights_hbm, att_hbm,
    frames, bottle, entry, exit_, tokens, packed, mix, weights_buf, att, sems,
):
    move = Mover(sems)
    patches, bots = frames.shape[0], bottle.shape[0]
    rows, width = tokens.shape
    side = exit_.shape[1]
    first = [move.start(frames_hbm, frames), move.start(bottle_hbm, bottle)]
    columns = [slice(j * side, (j + 1) * side) for j in range(3)]
    entries = [move.spread(entry_hbm.at[:, c], entry.at[:, c]) for c in columns]
    outs = []
    finish(first)
    later = move.spread(exit_hbm, exit_)
    grads = move.start(grad_hbm, packed.at[:, width : 2 * width])
    fill_tokens(tokens, frames, bottle)
    low = normalize(tokens[...])[0].astype(BF)
    for c, copy in zip(columns, entries):
        finish(copy)
        mix[:, c] = mm(low, entry[:, c], NN).astype(BF)
    outs.append(move.start(mix, mix_hbm))
    masks = half_masks(side // HEADS)
    keep = lax.broadcasted_iota(jnp.int32, (rows, rows), 0) < patches + bots

    def save(h, weights):
        weights_buf[h] = weights
        outs.append(move.start(weights_buf.at[h], weights_hbm.at[h]))

    def put(p, w, value):
        att[:, p * w : (p + 1) * w] = value

    attention_forward(mix, keep, masks, save, put)
    outs.append(move.start(att, att_hbm))
    finish(later)
    out = tokens[0:patches, :] + mm(att[0:patches, :], exit_[...], NT)
    packed[:, 0:width] = out.astype(BF)
    grads.wait()
    outs.append(move.start(packed, packed_hbm))
    finish(outs)


def spatial_factors_kernel(
    core_ref, frames_hbm, bottle_hbm, att_hbm, send_hbm, kept_hbm,
    frames, bottle, tokens, send, kept, sems,
):
    move = Mover(sems)
    half = kept.shape[1]
    first = [move.start(frames_hbm, frames), move.start(bottle_hbm, bottle)]
    copied = move.start(att_hbm, send.at[:, half:])
    finish(first)
    fill_tokens(tokens, frames, bottle)
    low = normalize(tokens[...])[0].astype(BF)
    core = core_ref[0]
    pick(low, picker(1 - core), send, 0)
    copied.wait()
    outs = [move.start(send, send_hbm)]
    pick(low, picker(core), kept, 0)
    outs.append(move.start(kept, kept_hbm))
    finish(outs)


def temporal_kernel(
    frames, core_ref, moved_hbm, entry_hbm, exit_hbm, back_hbm, send_hbm, kept_hbm,
    moved, entry, exit_, back, mix, weights_buf, send, kept, sems,
):
    move = Mover(sems)
    rows, width = back.shape
    half, side = width // 2, exit_.shape[1]
    seqs = rows // frames
    first = move.start(moved_hbm, moved)
    columns = [slice(j * side, (j + 1) * side) for j in range(3)]
    entries = [move.spread(entry_hbm.at[:, c], entry.at[:, c]) for c in columns]
    core = core_ref[0]
    other, own = picker(1 - core), picker(core)
    first.wait()
    later = move.spread(exit_hbm, exit_)
    cot = moved[:, width : 2 * width]
    normed, inverse = normalize(moved[:, 0:width].astype(F32))
    low = normed.astype(BF)
    pick(cot, other, send, half + side)
    pick(cot, own, kept, half)
    for c, copy in zip(columns, entries):
        finish(copy)
        mix[:, c] = mm(low, entry[:, c], NN).astype(BF)
    pick(low, other, send, 0)
    pick(low, own, kept, 0)
    outs = [move.start(kept, kept_hbm)]
    masks = half_masks(side // HEADS)
    keep = (
        lax.broadcasted_iota(jnp.int32, (rows, rows), 0) % seqs
        == lax.broadcasted_iota(jnp.int32, (rows, rows), 1) % seqs
    )

    def save(h, weights):
        weights_buf[h] = weights

    def put(p, w, value):
        send[:, half + p * w : half + (p + 1) * w] = value

    attention_forward(mix, keep, masks, save, put)
    finish(later)
    d_att = mm(cot, exit_[...], NN).astype(BF)
    at_mix = width + side

    def put_grad(at, w, value):
        send[:, at_mix + at : at_mix + at + w] = value

    attention_backward(mix, lambda h, again=False: weights_buf[h], d_att, masks, put_grad)
    outs.append(move.start(send, send_hbm))
    d_normed = mm(send[:, at_mix:], entry[...], NT)
    back[...] = inputs_gradient(cot, normed, inverse, d_normed).astype(BF)
    outs.append(move.start(back, back_hbm))
    finish(outs)


def fill_cotangent(cot, joined, frames):
    patches = cot.shape[0] - 16
    rows = joined[...].astype(F32) / frames
    padded = jnp.concatenate([rows, jnp.zeros((16 - rows.shape[0], rows.shape[1]), F32)], axis=0)
    cot[patches:, :] = padded.astype(BF)


def spatial_backward_kernel(
    frames, core_ref, back_hbm, joined_hbm, mix_hbm, weights_hbm, exit_hbm,
    picked_hbm, kept_hbm, d_mix_hbm,
    cot, joined, mix, weights_buf, exit_, picked, kept, d_mix, sems,
):
    move = Mover(sems)
    side = exit_.shape[1]
    patches = back_hbm.shape[0]
    first = [move.start(joined_hbm, joined), move.start(back_hbm, cot.at[0:patches, :])]
    first += move.spread(exit_hbm, exit_)
    second = move.start(mix_hbm, mix)
    heads = [move.start(weights_hbm.at[h], weights_buf.at[h]) for h in range(HEADS)]
    finish(first)
    fill_cotangent(cot, joined, frames)
    c = cot[...]
    d_att = mm(c, exit_[...], NN).astype(BF)
    core = core_ref[0]
    pick(c, picker(core), kept, 0)
    outs = [move.start(kept, kept_hbm)]
    pick(c, picker(1 - core), picked, 0)
    outs.append(move.start(picked, picked_hbm))
    masks = half_masks(side // HEADS)
    second.wait()

    def load(h, again=False):
        if not again:
            heads[h].wait()
        return weights_buf[h]

    def put_grad(at, w, value):
        d_mix[:, at : at + w] = value

    attention_backward(mix, load, d_att, masks, put_grad)
    outs.append(move.start(d_mix, d_mix_hbm))
    finish(outs)


def bottle_inputs_kernel(
    frames_count, bottle_hbm, joined_hbm, d_mix_hbm, entry_hbm, local_hbm,
    bottle, joined, d_mix, entry, tokens, local, sems,
):
    move = Mover(sems)
    bots = bottle.shape[0]
    second = move.spread(entry_hbm, entry, 4)
    second.append(move.start(d_mix_hbm.at[d_mix_hbm.shape[0] - 16 :, :], d_mix))
    first = [move.start(bottle_hbm, bottle), move.start(joined_hbm, joined)]
    finish(first)
    tokens[...] = jnp.zeros(tokens.shape, F32)
    tokens[0:bots, :] = bottle[...].astype(F32)
    normed, inverse = normalize(tokens[...])
    c = (joined[...].astype(F32) / frames_count).astype(BF)
    finish(second)
    d_normed = mm(d_mix[...], entry[...], NT)
    grads = inputs_gradient(c, normed[0:bots], inverse[0:bots], d_normed[0:bots])
    local[...] = grads
    move.start(local, local_hbm).wait()


def patch_inputs_kernel(
    frames_hbm, back_hbm, d_mix_hbm, entry_hbm, delta_hbm,
    frames, cot, d_mix, entry, delta, sems,
):
    move = Mover(sems)
    first = move.start(frames_hbm, frames)
    second = [
        move.start(d_mix_hbm.at[0 : d_mix.shape[0], :], d_mix),
        move.start(back_hbm, cot),
        *move.spread(entry_hbm, entry, 4),
    ]
    first.wait()
    normed, inverse = normalize(frames[...].astype(F32))
    finish(second)
    d_normed = mm(d_mix[...], entry[...], NT)
    delta[...] = inputs_gradient(cot[...], normed, inverse, d_normed).astype(BF)
    move.start(delta, delta_hbm).wait()


def weight_gradient_kernel(places, place_ref, *refs):
    arrays, refs = refs[: len(refs) - 10], refs[len(refs) - 10 :]
    outs_hbm, (left_n, left_c, right_m, right_a, out, sems) = refs[:4], refs[4:]
    move = Mover(sems)
    rows = left_n.shape[0] // 2
    share = out.shape[0] // 4

    def both(target, pair):
        copies = []
        for k, (index, at) in enumerate(pair):
            source = arrays[index].at[:, at : at + target.shape[1]]
            copies.append(move.start(source, target.at[k * rows : (k + 1) * rows, :]))
        return copies

    ready = [both(t, places[k]) for k, t in enumerate((left_c, right_a, left_n, right_m))]
    side = right_a.shape[1]
    core, place = place_ref[0], place_ref[1]
    where = []
    for b in range(32):
        zl, x, y = b // 16, b // 4 % 4, b % 4
        on_x = ((x + 4 - place) % 4) * 8 + y * 2 + zl
        on_y = ((y + 4 - place) % 4) * 8 + x * 2 + zl
        where.append(pl.multiple_of(jnp.where(core == 0, on_x, on_y) * 16, 16))
    outs = []

    def put(at, value):
        for b in range(32):
            out[pl.ds(where[b], 16), at : at + side] = value[b * 16 : (b + 1) * 16, :]
        columns = slice(at, at + side)
        for k in (1, 2, 3, 0):
            source = out.at[k * share : (k + 1) * share, columns]
            outs.append(move.start(source, outs_hbm[k].at[:, columns]))

    finish(ready[0] + ready[1])
    put(3 * side, mm(left_c[...], right_a[...], TN).astype(BF))
    finish(ready[2] + ready[3])
    turned = left_n[...].T
    for j in range(3):
        put(j * side, mm(turned, right_m[:, j * side : (j + 1) * side], NN).astype(BF))
    finish(outs)


def add_four(parts, columns):
    total = parts[0, :, columns].astype(F32)
    for k in range(1, 4):
        total = total + parts[k, :, columns].astype(F32)
    return total.astype(BF)


def four_sum_kernel(right, own_hbm, a_hbm, b_hbm, c_hbm, *refs):
    out_hbm, parts, out, sems = refs[-4:]
    move = Mover(sems)
    sources = (own_hbm, a_hbm, b_hbm, c_hbm)
    width = out.shape[1]
    step = width // 4
    columns = [slice(j * step, (j + 1) * step) for j in range(4)]
    copies = [[move.start(r.at[:, c], parts.at[k, :, c]) for k, r in enumerate(sources)] for c in columns]
    outs = []
    for c, ready in zip(columns, copies):
        finish(ready)
        out[:, c] = add_four(parts, c)
        at = c.start + (width if right else 0)
        outs.append(move.start(out.at[:, c], out_hbm.at[:, at : at + step]))
    finish(outs)


def last_sum_kernel(
    scale, parts_hbm, s_entry_hbm, s_exit_hbm, t_entry_hbm, t_exit_hbm,
    parts, s_entry, s_exit, t_entry, t_exit, sems,
):
    move = Mover(sems)
    side = s_exit.shape[1]
    columns = [slice(j * side, (j + 1) * side) for j in range(8)]
    copies = [move.start(parts_hbm.at[:, :, c], parts.at[:, :, c]) for c in columns]
    outs = []
    for j, (c, copy) in enumerate(zip(columns, copies)):
        copy.wait()
        total = (jnp.sum(parts[:, :, c].astype(F32), axis=0) * scale).astype(BF)
        entry, exit_ = ((s_entry, s_exit), (t_entry, t_exit))[j // 4]
        if j % 4 < 3:
            entry[:, (j % 4) * side : (j % 4 + 1) * side] = total
        else:
            exit_[...] = total
    for value, target in (
        (s_entry, s_entry_hbm), (s_exit, s_exit_hbm), (t_entry, t_entry_hbm), (t_exit, t_exit_hbm)
    ):
        outs.append(move.start(value, target))
    finish(outs)


HBM = pl.BlockSpec(memory_space=pltpu.HBM)
SMEM = pl.BlockSpec(memory_space=pltpu.SMEM)


def call(kernel, outs, ins, scratch, copies, flops, aliases=None):
    return pl.pallas_call(
        kernel,
        out_shape=tuple(jax.ShapeDtypeStruct(s, d) for s, d in outs),
        in_specs=[SMEM if a.ndim == 1 else HBM for a in ins],
        out_specs=tuple(HBM for _ in outs),
        input_output_aliases=aliases or {},
        scratch_shapes=[pltpu.VMEM(s, d) for s, d in scratch]
        + [pltpu.SemaphoreType.DMA((copies + 4,))],
        compiler_params=pltpu.CompilerParams(vmem_limit_bytes=(64 * 1024 - 128) * 1024),
        cost_estimate=pl.CostEstimate(flops=flops, bytes_accessed=1000, transcendentals=0),
    )(*ins)


def index_of(shape, zl, x, y, zh, c):
    return (((zl * shape[1] + x) * shape[2] + y) * shape[3] + zh) * shape[4] + c


def first_pairs(shape, step):
    pairs = []
    for zl, x, y, zh, c in itertools.product(*(range(n) for n in shape)):
        to = (zl, (x + step) % shape[1], y) if c == 0 else (zl, x, (y + step) % shape[2])
        pairs.append((index_of(shape, zl, x, y, zh, c), index_of(shape, *to, zh, c)))
    return pairs


def second_groups(shape):
    zls, xs, ys, zhs = (range(n) for n in shape[:4])
    on_0 = [[index_of(shape, l, x, y, h, 0) for y in ys for l in zls for h in zhs] for x in xs]
    on_1 = [[index_of(shape, l, x, y, h, 1) for x in xs for l in zls for h in zhs] for y in ys]
    return on_0 + on_1


def per_device(
    frames_in, bottleneck, spatial_entry, spatial_exit, temporal_entry, temporal_exit,
    output_grad, joined_grad,
):
    patches, width = frames_in.shape[2], frames_in.shape[3]
    bots, side = bottleneck.shape[1], spatial_exit.shape[1]
    half = width // 2
    frames = lax.axis_size(FRAME)
    rows = patches + 16
    on = lax.axis_index("c")
    core = on.astype(jnp.int32).reshape(1)
    first = jnp.where(on == 0, lax.axis_index("x"), lax.axis_index("y"))
    place = jnp.stack([on, first])
    place = place.astype(jnp.int32)
    shape = [lax.axis_size(a) for a in ALL]
    clips = lax.axis_size(("zl", "x"))
    scale = 1.0 / math.sqrt(clips * frames * patches)
    frame, bottle, joined = frames_in[0, 0], bottleneck[0], joined_grad[0]
    swap = [(0, 1), (1, 0)]

    def exchange(array):
        blocks = array.reshape(frames, patches // frames, array.shape[1])
        return lax.all_to_all(blocks, FRAME, 0, 0, tiled=True).reshape(array.shape)

    packed, mix, weights, att = call(
        spatial_forward_kernel,
        [
            ((patches, 2 * width), BF), ((rows, 3 * side), BF), ((HEADS, rows, rows), F32),
            ((rows, side), BF),
        ],
        [frame, bottle, spatial_entry, spatial_exit, output_grad[0, 0]],
        [
            ((patches, width), BF), ((bots, width), BF), ((width, 3 * side), BF),
            ((width, side), BF), ((rows, width), F32),
            ((patches, 2 * width), BF), ((rows, 3 * side), BF), ((HEADS, rows, rows), F32),
            ((rows, side), BF),
        ],
        10 + HEADS,
        1000,
    )
    moved = exchange(packed)

    send_s1, kept_sn = call(
        spatial_factors_kernel,
        [((rows, half + side), BF), ((rows, half), BF)],
        [core, frame, bottle, att],
        [
            ((patches, width), BF), ((bots, width), BF), ((rows, width), F32),
            ((rows, half + side), BF), ((rows, half), BF),
        ],
        5,
        1000,
    )
    got_s1 = lax.ppermute(send_s1, "c", swap)
    moved, got_s1 = lax.optimization_barrier((moved, got_s1))

    factors = half + side + half + 3 * side
    back, send_t, kept_t = call(
        functools.partial(temporal_kernel, frames),
        [((patches, width), BF), ((patches, factors), BF), ((patches, width), BF)],
        [core, moved, temporal_entry, temporal_exit],
        [
            ((patches, 2 * width), BF), ((width, 3 * side), BF), ((width, side), BF),
            ((patches, width), BF), ((patches, 3 * side), BF), ((HEADS, patches, patches), F32),
            ((patches, factors), BF), ((patches, width), BF),
        ],
        8,
        1000,
    )
    back = exchange(back)

    got_t = lax.ppermute(send_t, "c", swap)

    def weight_gradient(count, places, arrays):
        parts = call(
            functools.partial(weight_gradient_kernel, places),
            [((half // 4, 4 * side), BF)] * 4,
            [place] + arrays,
            [
                ((2 * count, half), BF), ((2 * count, half), BF), ((2 * count, 3 * side), BF),
                ((2 * count, side), BF), ((half, 4 * side), BF),
            ],
            24,
            1000,
        )
        return parts

    def passed_on(parts):
        return [parts[0]] + [
            lax.ppermute(parts[k], ALL, first_pairs(shape, k)) for k in (1, 3, 2)
        ]

    cot_at, mix_at = half + side, half + side + half
    parts_t = weight_gradient(
        patches,
        (
            ((0, half), (2, cot_at)), ((1, half), (2, half)),
            ((0, 0), (2, 0)), ((1, mix_at), (2, mix_at)),
        ),
        [kept_t, send_t, got_t],
    )
    parts_t = passed_on(parts_t)
    back, parts_t[0] = lax.optimization_barrier((back, parts_t[0]))
    share = (half // 4, 4 * side)
    send_sc, kept_sc, d_mix_s = call(
        functools.partial(spatial_backward_kernel, frames),
        [((rows, half), BF), ((rows, half), BF), ((rows, 3 * side), BF)],
        [core, back, joined, mix, weights, spatial_exit],
        [
            ((rows, width), BF), ((bots, width), BF), ((rows, 3 * side), BF),
            ((HEADS, rows, rows), F32), ((width, side), BF), ((rows, half), BF),
            ((rows, half), BF), ((rows, 3 * side), BF),
        ],
        7 + HEADS,
        1000,
    )
    got_sc = lax.ppermute(send_sc, "c", swap)
    got_sm = lax.ppermute(d_mix_s, "c", swap)
    parts_s = weight_gradient(
        rows,
        (
            ((3, 0), (4, 0)), ((1, half), (2, half)),
            ((0, 0), (2, 0)), ((5, 0), (6, 0)),
        ),
        [kept_sn, send_s1, got_s1, kept_sc, got_sc, d_mix_s, got_sm],
    )
    tied = lax.optimization_barrier((d_mix_s, *parts_s, *parts_t))
    after, parts_s, parts_t = tied[0], tied[1:5], list(tied[5:])
    parts_s = passed_on(parts_s)
    (local,) = call(
        functools.partial(bottle_inputs_kernel, frames),
        [((bots, width), F32)],
        [bottle, joined, after, spatial_entry],
        [
            ((bots, width), BF), ((bots, width), BF), ((16, 3 * side), BF),
            ((width, 3 * side), BF), ((16, width), F32), ((bots, width), F32),
        ],
        5,
        1000,
    )

    def with_partner(local, axis, bit):
        pairs = [(i, i ^ bit) for i in range(lax.axis_size(axis))]
        return local + lax.ppermute(local, axis, pairs)

    local = with_partner(local, "zh", 1)
    local, after, *parts_s = lax.optimization_barrier((local, after, *parts_s))
    (delta,) = call(
        patch_inputs_kernel,
        [((patches, width), BF)],
        [frame, back, after, spatial_entry],
        [
            ((patches, width), BF), ((patches, width), BF), ((patches, 3 * side), BF),
            ((width, 3 * side), BF), ((patches, width), BF),
        ],
        5,
        1000,
    )
    local = with_partner(local, "c", 1)
    ys = shape[2]
    sent = [local] + [
        lax.ppermute(local, "y", [(i, (i + k) % ys) for i in range(ys)]) for k in range(1, ys)
    ]
    total = None
    for j in range(ys):
        back_by = (lax.axis_index("y") - j) % ys
        part = sent[0]
        for k in range(1, ys):
            part = jnp.where(back_by == k, sent[k], part)
        total = part if total is None else total + part
    local = total
    wide = (half // 4, 8 * side)
    scratch = [((4, *share), BF), (share, BF)]
    (half_done,) = call(
        functools.partial(four_sum_kernel, True), [(wide, BF)], parts_t, scratch, 20, 1000
    )
    (both,) = call(
        functools.partial(four_sum_kernel, False), [(wide, BF)], [*parts_s, half_done], scratch,
        20, 1000, {4: 0},
    )
    groups = second_groups(shape)
    count = len(groups[0])
    last = lax.all_to_all(
        both.reshape(count, -1, 8 * side), ALL, 0, 0, axis_index_groups=groups, tiled=True
    )

    own = last.shape[1]
    s_entry, s_exit, t_entry, t_exit = call(
        functools.partial(last_sum_kernel, scale),
        [((own, 3 * side), BF), ((own, side), BF)] * 2,
        [last],
        [
            (last.shape, BF),
            ((own, 3 * side), BF), ((own, side), BF), ((own, 3 * side), BF), ((own, side), BF),
        ],
        12,
        1000,
    )
    return (
        delta[None, None], local.astype(BF)[None], s_entry, s_exit, t_entry, t_exit
    )


def solution(mesh):
    finer = Mesh(mesh.devices.reshape(2, mesh.shape["dp"] // 2, 4, 2, 2), ALL)
    dp = ("zl", "x")
    row = P(ALL, None)
    clip = P(dp, None, None)
    patch = P(dp, FRAME, None, None)
    return jax.shard_map(
        per_device,
        mesh=finer,
        in_specs=(patch, clip, P(), P(), P(), P(), patch, clip),
        out_specs=(patch, clip, row, row, row, row),
        check_vma=False,
    )
```

```python
import functools
import itertools
import math

import jax
import jax.numpy as jnp
from jax import lax
from jax.experimental import pallas as pl
from jax.experimental.pallas import tpu as pltpu
from jax.sharding import Mesh
from jax.sharding import PartitionSpec as P

HEADS = 8
EPSILON = 1e-05
FRAME = ("y", "zh", "c")
ALL = ("zl", "x", "y", "zh", "c")
BF = jnp.bfloat16
F32 = jnp.float32

NN = (((1,), (0,)), ((), ()))
NT = (((1,), (1,)), ((), ()))
TN = (((0,), (0,)), ((), ()))


def mm(a, b, dims):
    return lax.dot_general(a, b, dims, preferred_element_type=F32)


def normalize(u):
    centred = u - jnp.mean(u, axis=-1, keepdims=True)
    inverse = lax.rsqrt(jnp.mean(centred * centred, axis=-1, keepdims=True) + EPSILON)
    return centred * inverse, inverse


def half_masks(size):
    lane = lax.broadcasted_iota(jnp.int32, (1, 2 * size), 1)
    low = (lane < size).astype(F32)
    return low.astype(BF), (1.0 - low).astype(BF)


def head_pairs(mix_ref):
    side = mix_ref.shape[1] // 3
    width = 2 * (side // HEADS)

    def columns(part, p):
        return mix_ref[:, part * side + p * width : part * side + (p + 1) * width]

    return side, width, 1.0 / math.sqrt(width // 2), columns


def attention_forward(mix_ref, keep, masks, save, put):
    _, width, factor, columns = head_pairs(mix_ref)
    heads = [(p, h) for p in range(HEADS // 2) for h in range(2)]
    scores = [mm(columns(1, p) * masks[h], columns(0, p), NT) * factor for p, h in heads]
    scores = [jnp.where(keep, s, -jnp.inf) for s in scores]
    tops = [jnp.max(s, axis=0, keepdims=True) for s in scores]
    expons = [jnp.exp(s - t) for s, t in zip(scores, tops)]
    sums = [1.0 / jnp.sum(e, axis=0, keepdims=True) for e in expons]
    weights = [e * r for e, r in zip(expons, sums)]
    for k, w in enumerate(weights):
        save(k, w)
    parts = [mm(w.astype(BF), columns(2, p) * masks[h], TN) for w, (p, h) in zip(weights, heads)]
    for p in range(HEADS // 2):
        put(p, width, (parts[2 * p] + parts[2 * p + 1]).astype(BF))


def attention_backward(mix_ref, load, d_att, masks, put):
    side, width, factor, columns = head_pairs(mix_ref)
    heads = [(p, h) for p in range(HEADS // 2) for h in range(2)]
    d_heads = [d_att[:, p * width : (p + 1) * width] * masks[h] for p, h in heads]
    grads = [mm(columns(2, p), d, NT) for d, (p, _) in zip(d_heads, heads)]
    scores_grads = []
    for k, grad in enumerate(grads):
        weights = load(k)
        centre = jnp.sum(weights * grad, axis=0, keepdims=True)
        scores_grads.append((weights * (grad - centre) * factor).astype(BF))
    dv = [mm(load(k, True).astype(BF), d, NN) for k, d in enumerate(d_heads)]
    dk = [mm(g, columns(0, p) * masks[h], NN) for g, (p, h) in zip(scores_grads, heads)]
    dq = [mm(g, columns(1, p) * masks[h], TN) for g, (p, h) in zip(scores_grads, heads)]
    for part, each in enumerate((dq, dk, dv)):
        for p in range(HEADS // 2):
            value = each[2 * p] + each[2 * p + 1]
            put(part * side + p * width, width, value.astype(BF))


def inputs_gradient(c, normed, inverse, d_normed):
    inner = (
        d_normed
        - jnp.mean(d_normed, axis=-1, keepdims=True)
        - normed * jnp.mean(d_normed * normed, axis=-1, keepdims=True)
    )
    return c.astype(F32) + inverse * inner


def picker(half):
    row = lax.broadcasted_iota(jnp.int32, (256, 128), 0)
    col = lax.broadcasted_iota(jnp.int32, (256, 128), 1)
    source = (col // 8) * 16 + half * 8 + col % 8
    return (row == source).astype(F32).astype(BF)


def pick(values, chosen, out_ref, at):
    for b in range(values.shape[1] // 256):
        part = mm(values[:, 256 * b : 256 * (b + 1)], chosen, NN)
        out_ref[:, at + 128 * b : at + 128 * (b + 1)] = part.astype(BF)


class Mover:
    def __init__(self, sems):
        self.sems, self.count = sems, 0

    def start(self, source, target):
        copy = pltpu.make_async_copy(source, target, self.sems.at[self.count])
        self.count += 1
        copy.start()
        return copy

    def spread(self, source, target, count=2):
        step = source.shape[0] // count
        rows = [slice(k * step, (k + 1) * step) for k in range(count)]
        return [self.start(source.at[r, :], target.at[r, :]) for r in rows]


def finish(copies):
    for copy in copies:
        copy.wait()


def fill_tokens(tokens, frames, bottle):
    patches, bots = frames.shape[0], bottle.shape[0]
    rows, width = tokens.shape
    tokens[0:patches, :] = frames[...].astype(F32)
    tokens[patches:rows, :] = jnp.zeros((rows - patches, width), F32)
    tokens[patches : patches + bots, :] = bottle[...].astype(F32)


def spatial_forward_kernel(
    frames_hbm, bottle_hbm, entry_hbm, exit_hbm, grad_hbm,
    packed_hbm, mix_hbm, weights_hbm, att_hbm,
    frames, bottle, entry, exit_, tokens, packed, mix, weights_buf, att, sems,
):
    move = Mover(sems)
    patches, bots = frames.shape[0], bottle.shape[0]
    rows, width = tokens.shape
    side = exit_.shape[1]
    first = [move.start(frames_hbm, frames), move.start(bottle_hbm, bottle)]
    columns = [slice(j * side, (j + 1) * side) for j in range(3)]
    entries = [move.spread(entry_hbm.at[:, c], entry.at[:, c]) for c in columns]
    outs = []
    finish(first)
    later = move.spread(exit_hbm, exit_)
    grads = move.start(grad_hbm, packed.at[:, width : 2 * width])
    fill_tokens(tokens, frames, bottle)
    low = normalize(tokens[...])[0].astype(BF)
    for c, copy in zip(columns, entries):
        finish(copy)
        mix[:, c] = mm(low, entry[:, c], NN).astype(BF)
    outs.append(move.start(mix, mix_hbm))
    masks = half_masks(side // HEADS)
    keep = lax.broadcasted_iota(jnp.int32, (rows, rows), 0) < patches + bots

    def save(h, weights):
        weights_buf[h] = weights
        outs.append(move.start(weights_buf.at[h], weights_hbm.at[h]))

    def put(p, w, value):
        att[:, p * w : (p + 1) * w] = value

    attention_forward(mix, keep, masks, save, put)
    outs.append(move.start(att, att_hbm))
    finish(later)
    out = tokens[0:patches, :] + mm(att[0:patches, :], exit_[...], NT)
    packed[:, 0:width] = out.astype(BF)
    grads.wait()
    outs.append(move.start(packed, packed_hbm))
    finish(outs)


def spatial_factors_kernel(
    core_ref, frames_hbm, bottle_hbm, att_hbm, send_hbm, kept_hbm,
    frames, bottle, tokens, send, kept, sems,
):
    move = Mover(sems)
    half = kept.shape[1]
    first = [move.start(frames_hbm, frames), move.start(bottle_hbm, bottle)]
    copied = move.start(att_hbm, send.at[:, half:])
    finish(first)
    fill_tokens(tokens, frames, bottle)
    low = normalize(tokens[...])[0].astype(BF)
    core = core_ref[0]
    pick(low, picker(1 - core), send, 0)
    copied.wait()
    outs = [move.start(send, send_hbm)]
    pick(low, picker(core), kept, 0)
    outs.append(move.start(kept, kept_hbm))
    finish(outs)


def temporal_kernel(
    frames, core_ref, moved_hbm, entry_hbm, exit_hbm, back_hbm, send_hbm, kept_hbm,
    moved, entry, exit_, back, mix, weights_buf, send, kept, sems,
):
    move = Mover(sems)
    rows, width = back.shape
    half, side = width // 2, exit_.shape[1]
    seqs = rows // frames
    first = move.start(moved_hbm, moved)
    columns = [slice(j * side, (j + 1) * side) for j in range(3)]
    entries = [move.spread(entry_hbm.at[:, c], entry.at[:, c]) for c in columns]
    core = core_ref[0]
    other, own = picker(1 - core), picker(core)
    first.wait()
    later = move.spread(exit_hbm, exit_)
    cot = moved[:, width : 2 * width]
    normed, inverse = normalize(moved[:, 0:width].astype(F32))
    low = normed.astype(BF)
    pick(cot, other, send, half + side)
    pick(cot, own, kept, half)
    for c, copy in zip(columns, entries):
        finish(copy)
        mix[:, c] = mm(low, entry[:, c], NN).astype(BF)
    pick(low, other, send, 0)
    pick(low, own, kept, 0)
    outs = [move.start(kept, kept_hbm)]
    masks = half_masks(side // HEADS)
    keep = (
        lax.broadcasted_iota(jnp.int32, (rows, rows), 0) % seqs
        == lax.broadcasted_iota(jnp.int32, (rows, rows), 1) % seqs
    )

    def save(h, weights):
        weights_buf[h] = weights

    def put(p, w, value):
        send[:, half + p * w : half + (p + 1) * w] = value

    attention_forward(mix, keep, masks, save, put)
    finish(later)
    d_att = mm(cot, exit_[...], NN).astype(BF)
    at_mix = width + side

    def put_grad(at, w, value):
        send[:, at_mix + at : at_mix + at + w] = value

    attention_backward(mix, lambda h, again=False: weights_buf[h], d_att, masks, put_grad)
    outs.append(move.start(send, send_hbm))
    d_normed = mm(send[:, at_mix:], entry[...], NT)
    back[...] = inputs_gradient(cot, normed, inverse, d_normed).astype(BF)
    outs.append(move.start(back, back_hbm))
    finish(outs)


def fill_cotangent(cot, joined, frames):
    patches = cot.shape[0] - 16
    rows = joined[...].astype(F32) / frames
    padded = jnp.concatenate([rows, jnp.zeros((16 - rows.shape[0], rows.shape[1]), F32)], axis=0)
    cot[patches:, :] = padded.astype(BF)


def spatial_backward_kernel(
    frames, core_ref, back_hbm, joined_hbm, mix_hbm, weights_hbm, exit_hbm,
    picked_hbm, kept_hbm, d_mix_hbm,
    cot, joined, mix, weights_buf, exit_, picked, kept, d_mix, sems,
):
    move = Mover(sems)
    side = exit_.shape[1]
    patches = back_hbm.shape[0]
    first = [move.start(joined_hbm, joined), move.start(back_hbm, cot.at[0:patches, :])]
    first += move.spread(exit_hbm, exit_)
    second = move.start(mix_hbm, mix)
    heads = [move.start(weights_hbm.at[h], weights_buf.at[h]) for h in range(HEADS)]
    finish(first)
    fill_cotangent(cot, joined, frames)
    c = cot[...]
    d_att = mm(c, exit_[...], NN).astype(BF)
    core = core_ref[0]
    pick(c, picker(core), kept, 0)
    outs = [move.start(kept, kept_hbm)]
    pick(c, picker(1 - core), picked, 0)
    outs.append(move.start(picked, picked_hbm))
    masks = half_masks(side // HEADS)
    second.wait()

    def load(h, again=False):
        if not again:
            heads[h].wait()
        return weights_buf[h]

    def put_grad(at, w, value):
        d_mix[:, at : at + w] = value

    attention_backward(mix, load, d_att, masks, put_grad)
    outs.append(move.start(d_mix, d_mix_hbm))
    finish(outs)


def bottle_inputs_kernel(
    frames_count, bottle_hbm, joined_hbm, d_mix_hbm, entry_hbm, local_hbm,
    bottle, joined, d_mix, entry, tokens, local, sems,
):
    move = Mover(sems)
    bots = bottle.shape[0]
    second = move.spread(entry_hbm, entry, 4)
    second.append(move.start(d_mix_hbm.at[d_mix_hbm.shape[0] - 16 :, :], d_mix))
    first = [move.start(bottle_hbm, bottle), move.start(joined_hbm, joined)]
    finish(first)
    tokens[...] = jnp.zeros(tokens.shape, F32)
    tokens[0:bots, :] = bottle[...].astype(F32)
    normed, inverse = normalize(tokens[...])
    c = (joined[...].astype(F32) / frames_count).astype(BF)
    finish(second)
    d_normed = mm(d_mix[...], entry[...], NT)
    grads = inputs_gradient(c, normed[0:bots], inverse[0:bots], d_normed[0:bots])
    local[...] = grads
    move.start(local, local_hbm).wait()


def patch_inputs_kernel(
    frames_hbm, back_hbm, d_mix_hbm, entry_hbm, delta_hbm,
    frames, cot, d_mix, entry, delta, sems,
):
    move = Mover(sems)
    first = move.start(frames_hbm, frames)
    second = [
        move.start(d_mix_hbm.at[0 : d_mix.shape[0], :], d_mix),
        move.start(back_hbm, cot),
        *move.spread(entry_hbm, entry, 4),
    ]
    first.wait()
    normed, inverse = normalize(frames[...].astype(F32))
    finish(second)
    d_normed = mm(d_mix[...], entry[...], NT)
    delta[...] = inputs_gradient(cot[...], normed, inverse, d_normed).astype(BF)
    move.start(delta, delta_hbm).wait()


def weight_gradient_kernel(places, place_ref, *refs):
    arrays, refs = refs[: len(refs) - 10], refs[len(refs) - 10 :]
    outs_hbm, (left_n, left_c, right_m, right_a, out, sems) = refs[:4], refs[4:]
    move = Mover(sems)
    rows = left_n.shape[0] // 2
    share = out.shape[0] // 4

    def both(target, pair):
        copies = []
        for k, (index, at) in enumerate(pair):
            source = arrays[index].at[:, at : at + target.shape[1]]
            copies.append(move.start(source, target.at[k * rows : (k + 1) * rows, :]))
        return copies

    ready = [both(t, places[k]) for k, t in enumerate((left_c, right_a, left_n, right_m))]
    side = right_a.shape[1]
    core, place = place_ref[0], place_ref[1]
    where = []
    for b in range(32):
        zl, x, y = b // 16, b // 4 % 4, b % 4
        on_x = ((x + 4 - place) % 4) * 8 + y * 2 + zl
        on_y = ((y + 4 - place) % 4) * 8 + x * 2 + zl
        where.append(pl.multiple_of(jnp.where(core == 0, on_x, on_y) * 16, 16))
    outs = []

    def put(at, value):
        for b in range(32):
            out[pl.ds(where[b], 16), at : at + side] = value[b * 16 : (b + 1) * 16, :]
        columns = slice(at, at + side)
        for k in (1, 2, 3, 0):
            source = out.at[k * share : (k + 1) * share, columns]
            outs.append(move.start(source, outs_hbm[k].at[:, columns]))

    finish(ready[0] + ready[1])
    put(3 * side, mm(left_c[...], right_a[...], TN).astype(BF))
    finish(ready[2] + ready[3])
    turned = left_n[...].T
    for j in range(3):
        put(j * side, mm(turned, right_m[:, j * side : (j + 1) * side], NN).astype(BF))
    finish(outs)


def four_sum_kernel(right, own_hbm, a_hbm, b_hbm, c_hbm, *refs):
    out_hbm, parts, out, sems = refs[-4:]
    move = Mover(sems)
    sources = (own_hbm, a_hbm, b_hbm, c_hbm)
    count, width = out.shape
    step = count // 4
    rows = [slice(j * step, (j + 1) * step) for j in range(4)]
    copies = [[move.start(s.at[r, :], parts.at[k, r, :]) for k, s in enumerate(sources)] for r in rows]
    at = width if right else 0
    outs = []
    for r, ready in zip(rows, copies):
        finish(ready)
        total = parts[0, r, :].astype(F32)
        for k in range(1, 4):
            total = total + parts[k, r, :].astype(F32)
        out[r, :] = total.astype(BF)
        outs.append(move.start(out.at[r, :], out_hbm.at[r, at : at + width]))
    finish(outs)


def last_sum_kernel(
    scale, parts_hbm, s_entry_hbm, s_exit_hbm, t_entry_hbm, t_exit_hbm,
    parts, s_entry, s_exit, t_entry, t_exit, sems,
):
    move = Mover(sems)
    side = s_exit.shape[1]
    columns = [slice(j * side, (j + 1) * side) for j in range(8)]
    copies = [move.start(parts_hbm.at[:, :, c], parts.at[:, :, c]) for c in columns]
    outs = []
    for j, (c, copy) in enumerate(zip(columns, copies)):
        copy.wait()
        total = (jnp.sum(parts[:, :, c].astype(F32), axis=0) * scale).astype(BF)
        entry, exit_ = ((s_entry, s_exit), (t_entry, t_exit))[j // 4]
        if j % 4 < 3:
            entry[:, (j % 4) * side : (j % 4 + 1) * side] = total
        else:
            exit_[...] = total
    for value, target in (
        (s_entry, s_entry_hbm), (s_exit, s_exit_hbm), (t_entry, t_entry_hbm), (t_exit, t_exit_hbm)
    ):
        outs.append(move.start(value, target))
    finish(outs)


HBM = pl.BlockSpec(memory_space=pltpu.HBM)
SMEM = pl.BlockSpec(memory_space=pltpu.SMEM)


def call(kernel, outs, ins, scratch, copies, flops, aliases=None):
    return pl.pallas_call(
        kernel,
        out_shape=tuple(jax.ShapeDtypeStruct(s, d) for s, d in outs),
        in_specs=[SMEM if a.ndim == 1 else HBM for a in ins],
        out_specs=tuple(HBM for _ in outs),
        input_output_aliases=aliases or {},
        scratch_shapes=[pltpu.VMEM(s, d) for s, d in scratch]
        + [pltpu.SemaphoreType.DMA((copies + 4,))],
        compiler_params=pltpu.CompilerParams(vmem_limit_bytes=(64 * 1024 - 128) * 1024),
        cost_estimate=pl.CostEstimate(flops=flops, bytes_accessed=1000, transcendentals=0),
    )(*ins)


def index_of(shape, zl, x, y, zh, c):
    return (((zl * shape[1] + x) * shape[2] + y) * shape[3] + zh) * shape[4] + c


def first_pairs(shape, step):
    pairs = []
    for zl, x, y, zh, c in itertools.product(*(range(n) for n in shape)):
        to = (zl, (x + step) % shape[1], y) if c == 0 else (zl, x, (y + step) % shape[2])
        pairs.append((index_of(shape, zl, x, y, zh, c), index_of(shape, *to, zh, c)))
    return pairs


def second_groups(shape):
    zls, xs, ys, zhs = (range(n) for n in shape[:4])
    on_0 = [[index_of(shape, l, x, y, h, 0) for y in ys for l in zls for h in zhs] for x in xs]
    on_1 = [[index_of(shape, l, x, y, h, 1) for x in xs for l in zls for h in zhs] for y in ys]
    return on_0 + on_1


def per_device(
    frames_in, bottleneck, spatial_entry, spatial_exit, temporal_entry, temporal_exit,
    output_grad, joined_grad,
):
    patches, width = frames_in.shape[2], frames_in.shape[3]
    bots, side = bottleneck.shape[1], spatial_exit.shape[1]
    half = width // 2
    frames = lax.axis_size(FRAME)
    rows = patches + 16
    on = lax.axis_index("c")
    core = on.astype(jnp.int32).reshape(1)
    first = jnp.where(on == 0, lax.axis_index("x"), lax.axis_index("y"))
    place = jnp.stack([on, first])
    place = place.astype(jnp.int32)
    shape = [lax.axis_size(a) for a in ALL]
    clips = lax.axis_size(("zl", "x"))
    scale = 1.0 / math.sqrt(clips * frames * patches)
    frame, bottle, joined = frames_in[0, 0], bottleneck[0], joined_grad[0]
    swap = [(0, 1), (1, 0)]

    def exchange(array):
        blocks = array.reshape(frames, patches // frames, array.shape[1])
        return lax.all_to_all(blocks, FRAME, 0, 0, tiled=True).reshape(array.shape)

    packed, mix, weights, att = call(
        spatial_forward_kernel,
        [
            ((patches, 2 * width), BF), ((rows, 3 * side), BF), ((HEADS, rows, rows), F32),
            ((rows, side), BF),
        ],
        [frame, bottle, spatial_entry, spatial_exit, output_grad[0, 0]],
        [
            ((patches, width), BF), ((bots, width), BF), ((width, 3 * side), BF),
            ((width, side), BF), ((rows, width), F32),
            ((patches, 2 * width), BF), ((rows, 3 * side), BF), ((HEADS, rows, rows), F32),
            ((rows, side), BF),
        ],
        10 + HEADS,
        1000,
    )
    moved = exchange(packed)

    send_s1, kept_sn = call(
        spatial_factors_kernel,
        [((rows, half + side), BF), ((rows, half), BF)],
        [core, frame, bottle, att],
        [
            ((patches, width), BF), ((bots, width), BF), ((rows, width), F32),
            ((rows, half + side), BF), ((rows, half), BF),
        ],
        5,
        1000,
    )
    got_s1 = lax.ppermute(send_s1, "c", swap)
    moved, got_s1 = lax.optimization_barrier((moved, got_s1))

    factors = half + side + half + 3 * side
    back, send_t, kept_t = call(
        functools.partial(temporal_kernel, frames),
        [((patches, width), BF), ((patches, factors), BF), ((patches, width), BF)],
        [core, moved, temporal_entry, temporal_exit],
        [
            ((patches, 2 * width), BF), ((width, 3 * side), BF), ((width, side), BF),
            ((patches, width), BF), ((patches, 3 * side), BF), ((HEADS, patches, patches), F32),
            ((patches, factors), BF), ((patches, width), BF),
        ],
        8,
        1000,
    )
    back = exchange(back)

    got_t = lax.ppermute(send_t, "c", swap)

    def weight_gradient(count, places, arrays):
        parts = call(
            functools.partial(weight_gradient_kernel, places),
            [((half // 4, 4 * side), BF)] * 4,
            [place] + arrays,
            [
                ((2 * count, half), BF), ((2 * count, half), BF), ((2 * count, 3 * side), BF),
                ((2 * count, side), BF), ((half, 4 * side), BF),
            ],
            24,
            1000,
        )
        return parts

    def passed_on(parts):
        return [parts[0]] + [
            lax.ppermute(parts[k], ALL, first_pairs(shape, k)) for k in (1, 3, 2)
        ]

    cot_at, mix_at = half + side, half + side + half
    parts_t = weight_gradient(
        patches,
        (
            ((0, half), (2, cot_at)), ((1, half), (2, half)),
            ((0, 0), (2, 0)), ((1, mix_at), (2, mix_at)),
        ),
        [kept_t, send_t, got_t],
    )
    parts_t = passed_on(parts_t)
    back, parts_t[0] = lax.optimization_barrier((back, parts_t[0]))
    share = (half // 4, 4 * side)
    send_sc, kept_sc, d_mix_s = call(
        functools.partial(spatial_backward_kernel, frames),
        [((rows, half), BF), ((rows, half), BF), ((rows, 3 * side), BF)],
        [core, back, joined, mix, weights, spatial_exit],
        [
            ((rows, width), BF), ((bots, width), BF), ((rows, 3 * side), BF),
            ((HEADS, rows, rows), F32), ((width, side), BF), ((rows, half), BF),
            ((rows, half), BF), ((rows, 3 * side), BF),
        ],
        7 + HEADS,
        1000,
    )
    got_sc = lax.ppermute(send_sc, "c", swap)
    got_sm = lax.ppermute(d_mix_s, "c", swap)
    parts_s = weight_gradient(
        rows,
        (
            ((3, 0), (4, 0)), ((1, half), (2, half)),
            ((0, 0), (2, 0)), ((5, 0), (6, 0)),
        ),
        [kept_sn, send_s1, got_s1, kept_sc, got_sc, d_mix_s, got_sm],
    )
    tied = lax.optimization_barrier((d_mix_s, *parts_s, *parts_t))
    after, parts_s, parts_t = tied[0], tied[1:5], list(tied[5:])
    parts_s = passed_on(parts_s)
    (local,) = call(
        functools.partial(bottle_inputs_kernel, frames),
        [((bots, width), F32)],
        [bottle, joined, after, spatial_entry],
        [
            ((bots, width), BF), ((bots, width), BF), ((16, 3 * side), BF),
            ((width, 3 * side), BF), ((16, width), F32), ((bots, width), F32),
        ],
        5,
        1000,
    )

    def with_partner(local, axis, bit):
        pairs = [(i, i ^ bit) for i in range(lax.axis_size(axis))]
        return local + lax.ppermute(local, axis, pairs)

    local = with_partner(local, "zh", 1)
    local, after, *parts_s = lax.optimization_barrier((local, after, *parts_s))
    (delta,) = call(
        patch_inputs_kernel,
        [((patches, width), BF)],
        [frame, back, after, spatial_entry],
        [
            ((patches, width), BF), ((patches, width), BF), ((patches, 3 * side), BF),
            ((width, 3 * side), BF), ((patches, width), BF),
        ],
        5,
        1000,
    )
    local = with_partner(local, "c", 1)
    ys = shape[2]
    sent = [local] + [
        lax.ppermute(local, "y", [(i, (i + k) % ys) for i in range(ys)]) for k in range(1, ys)
    ]
    total = None
    for j in range(ys):
        back_by = (lax.axis_index("y") - j) % ys
        part = sent[0]
        for k in range(1, ys):
            part = jnp.where(back_by == k, sent[k], part)
        total = part if total is None else total + part
    local = total
    wide = (half // 4, 8 * side)
    scratch = [((4, *share), BF), (share, BF)]
    (half_done,) = call(
        functools.partial(four_sum_kernel, True), [(wide, BF)], parts_t, scratch, 20, 1000
    )
    (both,) = call(
        functools.partial(four_sum_kernel, False), [(wide, BF)], [*parts_s, half_done], scratch,
        20, 1000, {4: 0},
    )
    groups = second_groups(shape)
    count = len(groups[0])
    last = lax.all_to_all(
        both.reshape(count, -1, 8 * side), ALL, 0, 0, axis_index_groups=groups, tiled=True
    )

    own = last.shape[1]
    s_entry, s_exit, t_entry, t_exit = call(
        functools.partial(last_sum_kernel, scale),
        [((own, 3 * side), BF), ((own, side), BF)] * 2,
        [last],
        [
            (last.shape, BF),
            ((own, 3 * side), BF), ((own, side), BF), ((own, 3 * side), BF), ((own, side), BF),
        ],
        12,
        1000,
    )
    return (
        delta[None, None], local.astype(BF)[None], s_entry, s_exit, t_entry, t_exit
    )


def solution(mesh):
    finer = Mesh(mesh.devices.reshape(2, mesh.shape["dp"] // 2, 4, 2, 2), ALL)
    dp = ("zl", "x")
    row = P(ALL, None)
    clip = P(dp, None, None)
    patch = P(dp, FRAME, None, None)
    return jax.shard_map(
        per_device,
        mesh=finer,
        in_specs=(patch, clip, P(), P(), P(), P(), patch, clip),
        out_specs=(patch, clip, row, row, row, row),
        check_vma=False,
    )
```
